32 devices in a mesh: lat: 4 (over z), wid: 2 (over core), tok: 4 (over y, x).
Axes of the slice: x: 2, y: 2, z: 4, core: 2. Of those that a mesh axis runs over, the one named last changes fastest.
Arguments:
- resid: bfloat16 [512, 4096], P('tok', 'wid'), may hold values from -6 to 6
- dictionary: bfloat16 [2048, 4096], P('lat', 'wid'), may hold values from -0.1875 to 0.1875
- enc_bias: float32 [2048], P('lat'), may hold values from -3 to 3
- dec_bias: float32 [4096], P('wid'), may hold values from -3 to 3
- active_blocks: int32 [512, 8], P('tok'), may hold values from 0 to 15, all different within a row
- level_bounds: int32 [4], replicated, may hold values from 1 to 16, as said below
Outputs:
- level_losses: float32 [4], replicated
- dict_grad: bfloat16 [4096, 2048], P(('wid', 'tok'), 'lat')
The draws below stay inside these ranges and needn't reach their ends.
Inputs may be any that keep to these rules, and one draw needn't show every extreme that they name: `active_blocks`: each row names 8 different blocks. `level_bounds`: strictly increasing; the last equals 16.
All inputs are finite; a program needn't handle non-finite values.
Results may differ from the reference program's by a relative error of at most 0.006.
Values sent between devices are 32-bit elements; how exact they have to be, the bound alone decides.
No kernel may reach another device: no remote copies, remote signals or barrier semaphores. Data moves between devices by JAX's collectives and lax.ppermute only.
A program may use at most 192 MiB of HBM per device.

```python
import jax
import jax.numpy as jnp
from jax import lax

D = 4096
KB = 8
LEVELS = 4
TOKENS = 512
LATENTS = 2048
BLOCKS = 16


def draw_level_bounds(key, part):
    shuffled = jax.random.permutation(key, BLOCKS - 1) + 1
    picked = jnp.sort(shuffled[:LEVELS - 1]).astype(jnp.int32)
    return jnp.concatenate([picked, jnp.array([BLOCKS], jnp.int32)])


def block_levels(own_key, dims, cuts, low, largest):
    gain = 1.0
    for axis_at, shards_of in cuts:
        draws = jax.random.uniform(jax.random.fold_in(jax.random.fold_in(own_key, 6), axis_at), (shards_of,), jnp.float32, low / len(cuts), largest / len(cuts))
        gain = gain * jnp.repeat(jnp.exp(draws), dims[axis_at] // shards_of).reshape((-1,) + (1,) * (len(dims) - 1 - axis_at))
    return gain


def different_ones(key, rows, amount, top, lift):
    order = jax.random.permutation(jax.random.fold_in(key, 1), amount)
    boost = order
    for power in range(3):
        boost = boost * boost // amount
    boost = boost * lift // amount
    chance = jax.random.randint(jax.random.fold_in(key, 2), (rows, amount), 0, 4096) + boost
    sure = jax.random.permutation(jax.random.fold_in(key, 3), rows)[jnp.arange(amount) % rows]
    chance = jnp.where(jnp.arange(rows)[:, None] == sure[None, :], 1 << 14, chance)
    score = chance * amount + jnp.arange(amount)
    return lax.top_k(score.astype(jnp.int32), top)[1].astype(jnp.int32)


def noise(stream_key, dims, scale, most, shards=(), kind=jnp.bfloat16):
    values = jax.random.normal(stream_key, dims, jnp.float32) * scale
    if len(shards) > 0:
        values = block_levels(stream_key, dims, shards, -0.22, 0.18) * values
    return jnp.clip(values, min=-most, max=most).astype(kind)


def setup_inputs(seed: int = 0) -> dict:
    key_of = jax.random.split(jax.random.key(seed), 7)
    resid = noise(key_of[0], (TOKENS, D), 1.0, 6.0, ((0, 4), (1, 2)))
    dictionary = noise(key_of[1], (LATENTS, D), (KB * 128) ** -0.5, 0.1875, ((0, 4), (1, 2)))
    enc_bias = noise(key_of[2], (LATENTS,), 0.5, 3.0, ((0, 4),), jnp.float32)
    dec_bias = noise(key_of[3], (D,), 0.5, 3.0, ((0, 2),), jnp.float32)
    active_blocks = different_ones(key_of[4], TOKENS, BLOCKS, KB, 8192)
    level_bounds = draw_level_bounds(jax.random.fold_in(key_of[6], 71), 0)
    return {"resid": resid, "dictionary": dictionary, "enc_bias": enc_bias, "dec_bias": dec_bias, "active_blocks": active_blocks, "level_bounds": level_bounds}


def gelu_tanh(value):
    return jax.nn.gelu(value, approximate=True)

def reference(resid, dictionary, enc_bias, dec_bias, active_blocks, level_bounds):
    token_count, width = resid.shape
    block_count = dictionary.shape[0] // 128
    resid_full = resid.astype(jnp.float32)
    dict_blocks = dictionary.reshape(block_count, 128, width)
    bias_blocks = enc_bias.reshape(block_count, 128)
    block_ids = jnp.arange(block_count, dtype=jnp.int32)

    def encode(w_block, b_block, block_id):
        pre = jnp.dot(resid, w_block.T, preferred_element_type=jnp.float32) + b_block[None, :]
        hit = jnp.any(active_blocks == block_id, axis=1).astype(jnp.float32)
        return (pre, hit)

    def forward(carry, item):
        running, levels = carry
        w_block, b_block, block_id = item
        pre, hit = encode(w_block, b_block, block_id)
        act = (gelu_tanh(pre) * hit[:, None]).astype(jnp.bfloat16)
        running = running + jnp.dot(act, w_block, preferred_element_type=jnp.float32)
        finished = level_bounds == block_id + 1
        levels = jnp.where(finished[:, None, None], running[None], levels)
        return ((running, levels), None)
    start = (jnp.zeros((token_count, width), jnp.float32), jnp.zeros((LEVELS, token_count, width), jnp.float32))
    (running, levels), _ = lax.scan(forward, start, (dict_blocks, bias_blocks, block_ids))
    errors = dec_bias[None, None, :] + levels - resid_full[None]
    level_losses = lax.optimization_barrier(jnp.sum(errors * errors, axis=(1, 2))) / (token_count * width)
    cum_err = jnp.cumsum(errors[::-1], axis=0)[::-1].astype(jnp.bfloat16)

    def backward(carry, item):
        w_block, b_block, block_id = item
        pre, hit = encode(w_block, b_block, block_id)
        act = (gelu_tanh(pre) * hit[:, None]).astype(jnp.bfloat16)
        level_of = jnp.sum((level_bounds <= block_id).astype(jnp.int32)).astype(jnp.int32)
        err_block = lax.dynamic_index_in_dim(cum_err, level_of, 0, keepdims=False)
        g_act = jnp.dot(err_block, w_block.T, preferred_element_type=jnp.float32)
        _, pull = jax.vjp(gelu_tanh, pre)
        g_pre = pull(g_act * hit[:, None])[0].astype(jnp.bfloat16)
        grad = jnp.dot(err_block.T, act, preferred_element_type=jnp.float32)
        grad = grad + jnp.dot(resid.T, g_pre, preferred_element_type=jnp.float32)
        return (carry, grad.astype(jnp.bfloat16))
    _, grads = lax.scan(backward, 0, (dict_blocks, bias_blocks, block_ids))
    dict_grad = jnp.transpose(grads, (1, 0, 2)).reshape(width, block_count * 128)
    return (level_losses, dict_grad)
```

```python
import functools

import jax
import jax.numpy as jnp
from jax import lax
from jax.experimental import pallas as pl
from jax.experimental.pallas import tpu as pltpu
from jax.sharding import PartitionSpec as P

LEVELS = 4
BLOCK = 128
GELU_C = 0.7978845608028654
GELU_A = 0.044715

VMEM = pl.BlockSpec(memory_space=pltpu.VMEM)
SMEM = pl.BlockSpec(memory_space=pltpu.SMEM)


def f32(shape):
    return jax.ShapeDtypeStruct(shape, jnp.float32)


def call(kernel, out_shape, in_specs, flops=0, scratch=()):
    outs = out_shape if isinstance(out_shape, (list, tuple)) else [out_shape]
    size = sum(o.size * o.dtype.itemsize for o in outs)
    return pl.pallas_call(
        kernel,
        out_shape=out_shape,
        in_specs=in_specs,
        out_specs=jax.tree.map(lambda _: VMEM, out_shape),
        scratch_shapes=list(scratch),
        compiler_params=pltpu.CompilerParams(vmem_limit_bytes=40 * 1024 * 1024),
        cost_estimate=pl.CostEstimate(flops=flops, bytes_accessed=2 * size, transcendentals=0),
    )


def block_mask(active_ref, first, lats):
    ids = first + lax.broadcasted_iota(jnp.int32, (1, lats), 1) // BLOCK
    hit = None
    for q in range(active_ref.shape[1]):
        same = active_ref[:, q : q + 1] == ids
        hit = same if hit is None else hit | same
    return hit


def activate_kernel(first_ref, mine, other, bias, active, pre_out, act_out):
    first = first_ref[0]
    pre = mine[...] + other[...] + bias[...]
    pre_out[...] = pre
    inner = GELU_C * (pre + GELU_A * (pre * pre * pre))
    gelu = 0.5 * pre * (1.0 + jnp.tanh(inner))
    act_out[...] = jnp.where(block_mask(active, first, pre.shape[1]), gelu, 0.0)


def g_pre_kernel(first_ref, pre_ref, mine, other, active, out):
    first = first_ref[0]
    pre = pre_ref[...]
    inner = GELU_C * (pre + GELU_A * (pre * pre * pre))
    slope = GELU_C * (1.0 + 3.0 * GELU_A * (pre * pre))
    bend = jnp.tanh(inner)
    deriv = 0.5 * (1.0 + bend) + 0.5 * pre * (1.0 - bend * bend) * slope
    hit = block_mask(active, first, pre.shape[1])
    out[...] = jnp.where(hit, deriv * (mine[...] + other[...]), 0.0)


def block_weights(first, bounds, count):
    return [
        [(first + i < bounds[m]).astype(jnp.float32) for i in range(count)]
        for m in range(LEVELS)
    ]


def block_parts(act_ref, dict_ref, count):
    parts = []
    for i in range(count):
        span = slice(i * BLOCK, (i + 1) * BLOCK)
        parts.append(
            jnp.dot(
                act_ref[:, span].astype(jnp.bfloat16),
                dict_ref[span, :],
                preferred_element_type=jnp.float32,
            )
        )
    return parts


def weighted(weights, parts):
    total = None
    for weight, part in zip(weights, parts):
        term = weight * part
        total = term if total is None else total + term
    return total


def project_kernel(first_ref, bounds_ref, act, dictionary, up_out, down_out):
    first = first_ref[0]
    bounds = [bounds_ref[m] for m in range(LEVELS)]
    count = dictionary.shape[0] // BLOCK
    below = block_weights(first, bounds, count)
    parts = block_parts(act, dictionary, count)
    up_out[...] = functools.reduce(jnp.add, parts)
    down_out[...] = weighted(
        [functools.reduce(jnp.add, [below[m][i] for m in range(LEVELS)]) for i in range(count)], parts
    )


def error_kernel(
    first_ref, bounds_ref, act, dictionary, earlier, later, resid, bias, err_out, gact_out, sq_out
):
    first = first_ref[0]
    bounds = [bounds_ref[m] for m in range(LEVELS)]
    count = dictionary.shape[0] // BLOCK
    below = block_weights(first, bounds, count)
    parts = block_parts(act, dictionary, count)
    base = bias[...] - resid[...] + earlier[...]
    for m in range(LEVELS):
        last = bounds[m] - 1 - first
        mine = jnp.logical_and(last >= 0, last < count).astype(jnp.float32)
        err = base + weighted(below[m], parts)
        sq_out[m : m + 1, :] = mine * jnp.sum(err * err, axis=0, keepdims=True)
    tail = later[...]
    for i in range(count):
        pair = [
            functools.reduce(jnp.add, [below[m][i] * below[m][i2] for m in range(LEVELS)])
            for i2 in range(count)
        ]
        own = functools.reduce(jnp.add, [below[m][i] for m in range(LEVELS)])
        err = (own * base + tail + weighted(pair, parts)).astype(jnp.bfloat16)
        err_out[i] = err
        span = slice(i * BLOCK, (i + 1) * BLOCK)
        gact_out[:, span] = lax.dot_general(
            err, dictionary[span, :], (((1,), (1,)), ((), ())), preferred_element_type=jnp.float32
        )


def decode_kernel(*refs):
    chunks = (len(refs) - 1) // 2
    errs, acts, out = refs[:chunks], refs[chunks : 2 * chunks], refs[-1]
    for i in range(errs[0].shape[0]):
        span = slice(i * BLOCK, (i + 1) * BLOCK)
        err = jnp.concatenate([e[i] for e in errs], axis=0)
        act = jnp.concatenate([a[:, span].astype(jnp.bfloat16) for a in acts], axis=0)
        out[:, span] = lax.dot_general(
            err, act, (((0,), (0,)), ((), ())), preferred_element_type=jnp.float32
        )


def encode_kernel(*refs):
    chunks = (len(refs) - 2) // 2
    resids, grads, base, out = refs[:chunks], refs[chunks : 2 * chunks], refs[-2], refs[-1]
    resid = jnp.concatenate([r[...].astype(jnp.bfloat16) for r in resids], axis=0)
    grad = jnp.concatenate([g[...].astype(jnp.bfloat16) for g in grads], axis=0)
    total = base[...] + lax.dot_general(
        resid, grad, (((0,), (0,)), ((), ())), preferred_element_type=jnp.float32
    )
    out[...] = total.astype(jnp.bfloat16)


def pick(index, choices):
    values = sorted(choices)
    result = choices[values[0]]
    for value in values[1:]:
        result = jnp.where(index == value, choices[value], result)
    return result


def body(resid, dictionary, enc_bias, dec_bias, active_blocks, level_bounds):
    rows, half = resid.shape
    lats = dictionary.shape[0]
    n_lat, n_wid, n_tok = lax.axis_size("lat"), lax.axis_size("wid"), lax.axis_size("tok")
    lat, tok = lax.axis_index("lat"), lax.axis_index("tok")
    width = half // n_tok
    count = lats // BLOCK
    first = (lat * count).astype(jnp.int32).reshape(1)
    swap = [(w, w ^ 1) for w in range(n_wid)]

    def across(array, c):
        return lax.ppermute(array, "tok", [(t, t ^ c) for t in range(n_tok)])

    partial = lax.dot_general(
        resid, dictionary, (((1,), (1,)), ((), ())), preferred_element_type=jnp.float32
    )
    other = lax.ppermute(partial, "wid", swap)
    square = (rows, lats)
    pre, act = call(activate_kernel, [f32(square), f32(square)], [SMEM, VMEM, VMEM, VMEM, VMEM])(
        first, partial, other, enc_bias.reshape(1, lats), active_blocks
    )
    acts = [act] + [across(act, c) for c in range(1, n_tok)]

    dict_here = lax.dynamic_slice(dictionary, (0, tok * width), (lats, width))
    bias_here = lax.dynamic_slice(dec_bias, (tok * width,), (width,)).reshape(1, width)
    resids = []
    for c in range(n_tok):
        piece = lax.dynamic_slice(resid, (0, (tok ^ c) * width), (rows, width)).astype(jnp.float32)
        resids.append(piece if c == 0 else across(piece, c))

    tile = (rows, width)
    flops = 2 * rows * lats * width
    ups, downs = [], []
    for c in range(n_tok):
        up, down = call(project_kernel, [f32(tile), f32(tile)], [SMEM, SMEM, VMEM, VMEM], flops)(
            first, level_bounds, acts[c], dict_here
        )
        ups.append(up)
        downs.append(down)

    from_end = n_lat - 1 - lat
    got_up, got_down = [], []
    for step in range(n_tok + n_lat - 2):
        places = [p for p in range(n_lat - 1) if 0 <= step - p < n_tok]
        send_up = pick(lat, {p: ups[step - p] for p in places})
        send_down = pick(from_end, {p: downs[step - p] for p in places})
        if step > 0:
            send_up = send_up + got_up[-1]
            send_down = send_down + got_down[-1]
        got_up.append(lax.ppermute(send_up, "lat", [(p, p + 1) for p in places]))
        got_down.append(
            lax.ppermute(send_down, "lat", [(n_lat - 1 - p, n_lat - 2 - p) for p in places])
        )

    errs, gacts, squares = [], [], []
    for c in range(n_tok):
        earlier = pick(lat, {p: got_up[c + p - 1] for p in range(1, n_lat)})
        later = pick(from_end, {p: got_down[c + p - 1] for p in range(1, n_lat)})
        err, gact, square_sums = call(
            error_kernel,
            [
                jax.ShapeDtypeStruct((count,) + tile, jnp.bfloat16),
                f32(square),
                f32((LEVELS, width)),
            ],
            [SMEM, SMEM] + [VMEM] * 6,
            2 * flops,
        )(first, level_bounds, acts[c], dict_here, earlier, later, resids[c], bias_here)
        errs.append(err)
        gacts.append(gact if c == 0 else across(gact, c))
        squares.append(square_sums)

    gact_half = functools.reduce(jnp.add, gacts)
    gact_other = lax.ppermute(gact_half, "wid", swap)
    g_pre = call(g_pre_kernel, f32(square), [SMEM] + [VMEM] * 4)(
        first, pre, gact_half, gact_other, active_blocks
    )
    g_pres = [g_pre] + [across(g_pre, c) for c in range(1, n_tok)]
    decoded = call(decode_kernel, f32((width, lats)), [VMEM] * (2 * n_tok), 2 * n_tok * flops)(
        *errs, *acts
    )
    grad = call(
        encode_kernel,
        jax.ShapeDtypeStruct((width, lats), jnp.bfloat16),
        [VMEM] * (2 * n_tok + 1),
        2 * n_tok * flops,
    )(*resids, *g_pres, decoded)

    total = jnp.sum(functools.reduce(jnp.add, squares), axis=1)
    for axis in ("wid", "tok", "lat"):
        size, gap = lax.axis_size(axis), 1
        while gap < size:
            total = total + lax.ppermute(total, axis, [(p, p ^ gap) for p in range(size)])
            gap *= 2
    level_losses = total / (rows * n_tok * half * n_wid)
    return (level_losses, grad)


def solution(mesh):
    return jax.shard_map(
        body,
        mesh=mesh,
        in_specs=(P("tok", "wid"), P("lat", "wid"), P("lat"), P("wid"), P("tok", None), P()),
        out_specs=(P(), P(("wid", "tok"), "lat")),
        check_vma=False,
    )
```

```python
import functools

import jax
import jax.numpy as jnp
from jax import lax
from jax.experimental import pallas as pl
from jax.experimental.pallas import tpu as pltpu
from jax.sharding import PartitionSpec as P

LEVELS = 4
BLOCK = 128
LOSS_ROWS = 8
GELU_C = 0.7978845608028654
GELU_A = 0.044715

FIRST, LAT, WID, TOK, BOUND = 0, 1, 2, 3, 4

VMEM = pl.BlockSpec(memory_space=pltpu.VMEM)
SMEM = pl.BlockSpec(memory_space=pltpu.SMEM)
HBM = pl.BlockSpec(memory_space=pltpu.HBM)
ANY = pl.BlockSpec(memory_space=pl.ANY)


def f32(*shape):
    return jax.ShapeDtypeStruct(shape, jnp.float32)


def bf16(*shape):
    return jax.ShapeDtypeStruct(shape, jnp.bfloat16)


def call(kernel, outs, scalars, arrays, after=(), specs=None, out_specs=None, scratch=(), flops=0):
    skip = slice(1 + len(arrays), 1 + len(arrays) + len(after))

    def run(*refs):
        kernel(*refs[: skip.start], *refs[skip.stop :])

    return pl.pallas_call(
        run,
        out_shape=outs,
        in_specs=[SMEM] + list(specs or [VMEM] * len(arrays)) + [ANY] * len(after),
        out_specs=out_specs or [VMEM] * len(outs),
        scratch_shapes=list(scratch),
        compiler_params=pltpu.CompilerParams(vmem_limit_bytes=12 * 1024 * 1024),
        cost_estimate=pl.CostEstimate(flops=flops, bytes_accessed=1 << 20, transcendentals=0),
    )(scalars, *arrays, *after)


def total_of(terms):
    return functools.reduce(jnp.add, terms)


def pre_kernel(scal, resid, dictionary, partial_out, dict_out, resid_v, dict_v, sems):
    pieces, _, width = dict_v.shape
    here = pl.ds(pl.multiple_of(scal[TOK] * width, width), width)
    copies = [pltpu.make_async_copy(resid, resid_v, sems.at[pieces])]
    for i in range(pieces):
        cols = pl.ds(i * width, width)
        copies.append(pltpu.make_async_copy(dictionary.at[:, cols], dict_v.at[i], sems.at[i]))
    copies.append(pltpu.make_async_copy(dictionary.at[:, here], dict_out, sems.at[pieces + 1]))
    for copy in copies:
        copy.start()
    copies[0].wait()
    total = None
    for i in range(pieces):
        copies[1 + i].wait()
        term = lax.dot_general(
            resid_v[:, i * width : (i + 1) * width],
            dict_v[i],
            (((1,), (1,)), ((), ())),
            preferred_element_type=jnp.float32,
        )
        total = term if total is None else total + term
    partial_out[...] = total
    copies[-1].wait()


def pieces_kernel(offsets, scal, resid, bias, bias_out, *outs):
    width = outs[0].shape[1]

    def cols(t):
        return pl.ds(pl.multiple_of(t * width, width), width)

    bias_out[...] = bias[:, cols(scal[TOK])]
    for (first, second), out in zip(offsets, outs):
        away = jnp.where(scal[WID] == 0, first, second)
        out[...] = resid[:, cols(scal[TOK] ^ away)].astype(jnp.float32)


def block_mask(active, first, lats):
    ids = first + lax.broadcasted_iota(jnp.int32, (1, lats), 1) // BLOCK
    hit = None
    for q in range(active.shape[1]):
        same = active[:, q : q + 1] == ids
        hit = same if hit is None else hit | same
    return hit


def activate_kernel(scal, mine, other, bias, active, pre_out, act_out):
    pre = mine[...] + other[...] + bias[...]
    pre_out[...] = pre
    inner = GELU_C * (pre + GELU_A * (pre * pre * pre))
    gelu = 0.5 * pre * (1.0 + jnp.tanh(inner))
    act_out[...] = jnp.where(block_mask(active[...], scal[FIRST], pre.shape[1]), gelu, 0.0)


def g_pre_kernel(scal, pre_ref, mine, other, active, loss, loss_other, out):
    pre = pre_ref[...]
    inner = GELU_C * (pre + GELU_A * (pre * pre * pre))
    slope = GELU_C * (1.0 + 3.0 * GELU_A * (pre * pre))
    bend = jnp.tanh(inner)
    deriv = 0.5 * (1.0 + bend) + 0.5 * pre * (1.0 - bend * bend) * slope
    hit = block_mask(active[...], scal[FIRST], pre.shape[1])
    rows = pre.shape[0]
    out[:rows, :] = jnp.where(hit, deriv * (mine[...] + other[...]), 0.0)
    out[rows:, :] = jnp.zeros_like(out[rows:, :])
    out[rows:, :BLOCK] = loss[...] + loss_other[...]


def last_blocks(scal, count):
    return [jnp.minimum(scal[BOUND + m] - 1 - scal[FIRST], count - 1) for m in range(LEVELS)]


def ending(lasts, i):
    return total_of([(last == i).astype(jnp.float32) for last in lasts])


def running_parts(act, dict_ref):
    sums = []
    for i in range(dict_ref.shape[0] // BLOCK):
        span = slice(i * BLOCK, (i + 1) * BLOCK)
        part = jnp.dot(
            act[:, span].astype(jnp.bfloat16), dict_ref[span, :], preferred_element_type=jnp.float32
        )
        sums.append(sums[-1] + part if sums else part)
    return sums


def project_kernel(spans, scal, act, dictionary, up_out, *down_outs):
    sums = running_parts(act[...], dictionary)
    lasts = last_blocks(scal, len(sums))
    up_out[...] = sums[-1]
    down = total_of([ending(lasts, i) * s for i, s in enumerate(sums)])
    for span, out in zip(spans, down_outs):
        out[...] = down[span, :]


def message_kernel(up, n_lat, places, has_got, scal, *refs):
    out = refs[-1]
    index = scal[LAT] if up else n_lat - 1 - scal[LAT]
    for place, piece in zip(places, refs[has_got:-1]):

        @pl.when(index == place)
        def _():
            rows = piece.shape[0]
            out[:rows, :] = piece[...] + refs[0][:rows, :] if place else piece[...]


def square_sums(scal, shifted, count):
    squares = []
    for v in shifted:
        lanes = jnp.sum(v * v, axis=0, keepdims=True)
        squares.append(total_of([lanes[:, i : i + BLOCK] for i in range(0, lanes.shape[1], BLOCK)]))
    rows = []
    for m in range(LEVELS):
        last = scal[BOUND + m] - 1 - scal[FIRST]
        rows.append(total_of([jnp.where(last == i, s, 0.0) for i, s in enumerate(squares)]))
    return jnp.concatenate(rows + [jnp.zeros((LOSS_ROWS - LEVELS, BLOCK), jnp.float32)], axis=0)


def add_chosen(index, choices, refs, span, target):
    for place, ref in zip(choices, refs):
        chosen = index == place if len(choices) < 4 else index >= 1

        @pl.when(chosen)
        def _():
            target[...] += ref[span, :]


def loss_kernel(spans, places, scal, bias, dictionary, *refs):
    refs = list(refs)
    out = refs.pop(-2)
    base = refs.pop()
    total = None
    for span in spans:
        act, resid = refs.pop(0), refs.pop(0)
        earlier = [refs.pop(0) for _ in range(len(places) if len(places) < 4 else 1)]
        rows = span.stop - span.start
        view = base.at[:rows, :]
        view[...] = bias[...] - resid[span, :]
        add_chosen(scal[LAT], places, earlier, span, view)
        sums = running_parts(act[span, :], dictionary)
        shifted = [view[...] + s for s in sums]
        term = square_sums(scal, shifted, len(sums))
        total = term if total is None else total + term
    out[...] = total_of([total] + [ref[...] for ref in refs])


def error_kernel(
    n_lat, up_places, down_places, span, squared, scal, act, dictionary, resid, bias, *refs
):
    refs = list(refs)
    earlier = [refs.pop(0) for _ in range(len(up_places) if len(up_places) < 4 else 1)]
    later = [refs.pop(0) for _ in range(len(down_places) if len(down_places) < 4 else 1)]
    base, tail = refs[-2:]
    err_out, gact_out = refs[:2]
    rows = span.stop - span.start
    base[...] = bias[...] - resid[span, :]
    add_chosen(scal[LAT], up_places, earlier, span, base)
    tail[...] = jnp.zeros_like(tail)
    add_chosen(n_lat - 1 - scal[LAT], down_places, later, slice(0, rows), tail)
    sums = running_parts(act[span, :], dictionary)
    count = len(sums)
    shifted = [base[...] + s for s in sums]
    if squared:
        refs[2][...] = square_sums(scal, shifted, count)
    lasts = last_blocks(scal, count)
    err = tail[...]
    for i in reversed(range(count)):
        err = err + ending(lasts, i) * shifted[i]
        rounded = err.astype(jnp.bfloat16)
        err_out[i] = rounded
        cols = slice(i * BLOCK, (i + 1) * BLOCK)
        gact_out[:, cols] = lax.dot_general(
            rounded,
            dictionary[cols, :],
            (((1,), (1,)), ((), ())),
            preferred_element_type=jnp.float32,
        )


def sum_kernel(cut, scal, head, tail, *rest):
    others, out = rest[:-1], rest[-1]
    out[:cut, :] = head[...] + total_of([o[:cut, :] for o in others])
    out[cut:, :] = tail[...] + total_of([o[cut:, :] for o in others])


def add_kernel(scal, one, two, out):
    out[...] = one[...] + two[...]


def decode_kernel(spans, has_base, scal, *refs):
    n = len(spans)
    errs, acts, out = refs[:n], refs[n : 2 * n], refs[-1]
    for i in range(errs[0].shape[0]):
        cols = slice(i * BLOCK, (i + 1) * BLOCK)
        err = jnp.concatenate([e[i] for e in errs], axis=0)
        act = jnp.concatenate(
            [a[s, cols].astype(jnp.bfloat16) for a, s in zip(acts, spans)], axis=0
        )
        term = lax.dot_general(err, act, (((0,), (0,)), ((), ())), preferred_element_type=jnp.float32)
        out[:, cols] = refs[2 * n][:, cols] + term if has_base else term


def encode_kernel(scale, scal, *refs):
    n = (len(refs) - 3) // 2
    resids, grads, base, out, loss_out = refs[:n], refs[n : 2 * n], refs[-3], refs[-2], refs[-1]
    rows = resids[0].shape[0]
    resid = jnp.concatenate([r[...].astype(jnp.bfloat16) for r in resids], axis=0)
    grad = jnp.concatenate([g[:rows, :].astype(jnp.bfloat16) for g in grads], axis=0)
    total = base[...] + lax.dot_general(
        resid, grad, (((0,), (0,)), ((), ())), preferred_element_type=jnp.float32
    )
    out[...] = total.astype(jnp.bfloat16)
    lanes = total_of([g[rows:, :BLOCK] for g in grads])
    for m in range(LEVELS):
        loss_out[m] = jnp.sum(lanes[m : m + 1, :]) * scale


def pick(index, choices):
    values = sorted(choices)
    result = choices[values[0]]
    for value in values[1:]:
        result = jnp.where(index == value, choices[value], result)
    return result


def body(resid, dictionary, enc_bias, dec_bias, active_blocks, level_bounds):
    rows, half = resid.shape
    lats = dictionary.shape[0]
    n_lat, n_wid, n_tok = lax.axis_size("lat"), lax.axis_size("wid"), lax.axis_size("tok")
    lat, wid, tok = lax.axis_index("lat"), lax.axis_index("wid"), lax.axis_index("tok")
    width = half // n_tok
    count = lats // BLOCK
    cut = rows // 2
    places = jnp.stack([lat * count, lat, wid, tok]).astype(jnp.int32)
    scal = jnp.concatenate([places, level_bounds])
    work = 2 * rows * lats * width

    def offset(w, q):
        return (0, 2, 1, 3)[q] if w and n_tok == 4 else q

    def across(array, q):
        pairs = [
            (w * n_tok + t, w * n_tok + (t ^ offset(w, q)))
            for w in range(n_wid)
            for t in range(n_tok)
        ]
        return lax.ppermute(array, ("wid", "tok"), pairs)

    def swap(array):
        return lax.ppermute(array, "wid", [(w, w ^ 1) for w in range(n_wid)])

    def gather(array):
        if n_tok != 4:
            return [array] + [across(array, q) for q in range(1, n_tok)]
        near = across(array, 1)
        far = across(array, 3)
        return [array, near, swap(near), far]

    partial, dict_here = call(
        pre_kernel,
        [f32(rows, lats), bf16(lats, width)],
        scal,
        (resid, dictionary),
        specs=[HBM, HBM],
        scratch=[
            pltpu.VMEM((rows, half), jnp.bfloat16),
            pltpu.VMEM((n_tok, lats, width), jnp.bfloat16),
            pltpu.SemaphoreType.DMA((n_tok + 2,)),
        ],
    )
    partial_other = swap(partial)
    bias_here, *pieces = call(
        functools.partial(pieces_kernel, [(offset(0, q), offset(1, q)) for q in range(n_tok)]),
        [f32(1, width)] + [f32(rows, width)] * n_tok,
        scal,
        (resid, dec_bias.reshape(1, half)),
        after=(partial,),
    )
    pre, act = call(
        activate_kernel,
        [f32(rows, lats)] * 2,
        scal,
        (partial, partial_other, enc_bias.reshape(1, lats), active_blocks),
        after=(bias_here,),
    )
    acts = gather(act)
    resids = [piece if q == 0 else across(piece, q) for q, piece in enumerate(pieces)]

    order = [0, 1, 3, 2] if n_tok == 4 else list(range(n_tok))
    chunks = [(0, slice(0, cut))] + [(q, slice(0, rows)) for q in order[1:]] + [(0, slice(cut, rows))]
    n_chunks = len(chunks)
    ups, downs = [], []
    for q in order:
        spans = [span for c, span in chunks if c == q]
        up, *down = call(
            functools.partial(project_kernel, spans),
            [f32(rows, width)] + [f32(s.stop - s.start, width) for s in spans],
            scal,
            (acts[q], dict_here),
            flops=work,
        )
        ups.append(up)
        downs.append(down)
    downs = [downs[0][0]] + [d[0] for d in downs[1:]] + [downs[0][1]]

    def send(pieces, got, step, up, after):
        at = [p for p in range(n_lat - 1) if 0 <= step - p < len(pieces)]
        sent = pieces[0]
        if step:
            options = [pieces[step - p] for p in at]
            sent = call(
                functools.partial(message_kernel, up, n_lat, at, 1),
                [f32(max(o.shape[0] for o in options), width)],
                scal,
                (got[-1], *options),
                after=after,
            )[0]
        if up:
            pairs = [(p, p + 1) for p in at]
        else:
            pairs = [(n_lat - 1 - p, n_lat - 2 - p) for p in at]
        got.append(lax.ppermute(sent, "lat", pairs))
        return sent

    def choose(index, got, c):
        choices = {p: got[c + p - 1] for p in range(1, n_lat)}
        if n_lat <= 4:
            return list(choices), list(choices.values())
        size = min(a.shape[0] for a in choices.values())
        one = pick(index, {p: a[:size] for p, a in choices.items()})
        return [1, 2, 3, 4], [one]

    def errors(c, after, squared):
        q, span = chunks[c]
        size = span.stop - span.start
        up_places, earlier = choose(lat, got_up, order.index(q))
        down_places, later = choose(n_lat - 1 - lat, got_down, c)
        return call(
            functools.partial(error_kernel, n_lat, up_places, down_places, span, squared),
            [bf16(count, size, width), f32(size, lats)]
            + ([f32(LOSS_ROWS, BLOCK)] if squared else []),
            scal,
            (acts[q], dict_here, resids[q], bias_here, *earlier, *later),
            after=after,
            scratch=[pltpu.VMEM((size, width), jnp.float32)] * 2,
            flops=2 * work,
        )

    got_up, got_down = [], []
    errs, gacts, squares = [], [], []
    up_steps, down_steps = len(ups) + n_lat - 2, n_chunks + n_lat - 2
    ahead = []
    for step in range(down_steps + 1):
        sent = None
        if step < up_steps:
            sent = send(ups, got_up, step, True, ahead)
            ahead = []
        if step < down_steps:
            sent = send(downs, got_down, step, False, ahead)
        c = step - (n_lat - 1)
        ahead = []
        if step == up_steps:
            open_spans = [(q, span) for q, span in (chunks[-2], chunks[-1])]
            items = []
            for q, span in open_spans:
                up_places, earlier = choose(lat, got_up, order.index(q))
                items += [acts[q], resids[q], *earlier]
            loss = call(
                functools.partial(loss_kernel, [s for _, s in open_spans], up_places),
                [f32(LOSS_ROWS, BLOCK)],
                scal,
                (bias_here, dict_here, *items, *squares),
                after=(sent,) if sent is not None else (),
                scratch=[pltpu.VMEM((rows, width), jnp.float32)],
                flops=work,
            )[0]
        if c >= 0:
            q, span = chunks[c]
            err, gact, *square = errors(
                c, (sent,) if sent is not None else (), c < n_chunks - 2
            )
            errs.append(err)
            gacts.append(gact if q == 0 else across(gact, q))
            squares += square
            ahead = [err]

    gap = 1
    while gap < n_lat:
        other = lax.ppermute(loss, "lat", [(p, p ^ gap) for p in range(n_lat)])
        loss = call(add_kernel, [f32(LOSS_ROWS, BLOCK)], scal, (loss, other))[0]
        gap *= 2

    mine = call(
        functools.partial(sum_kernel, cut),
        [f32(rows, lats)],
        scal,
        (gacts[0], gacts[-1], *gacts[1:-1]),
    )[0]
    g_pre = call(
        g_pre_kernel,
        [f32(rows + LOSS_ROWS, lats)],
        scal,
        (pre, mine, swap(mine), active_blocks, loss, swap(loss)),
    )[0]
    g_pres = gather(g_pre)

    def decode(items, base, after):
        return call(
            functools.partial(decode_kernel, [chunks[c][1] for c in items], len(base)),
            [f32(width, lats)],
            scal,
            (*[errs[c] for c in items], *[acts[chunks[c][0]] for c in items], *base),
            after=after,
            flops=n_tok * work,
        )[0]

    decoded = decode(range(n_chunks), (), ())
    grad, losses = call(
        functools.partial(encode_kernel, 1.0 / (rows * n_tok * half * n_wid)),
        [bf16(width, lats), f32(LEVELS)],
        scal,
        (*resids, *g_pres, decoded),
        out_specs=[VMEM, SMEM],
        flops=n_tok * work,
    )
    return (losses, grad)


def solution(mesh):
    return jax.shard_map(
        body,
        mesh=mesh,
        in_specs=(P("tok", "wid"), P("lat", "wid"), P("lat"), P("wid"), P("tok", None), P()),
        out_specs=(P(), P(("wid", "tok"), "lat")),
        check_vma=False,
    )
```

```python
import functools

import jax
import jax.numpy as jnp
from jax import lax
from jax.experimental import pallas as pl
from jax.experimental.pallas import tpu as pltpu
from jax.sharding import PartitionSpec as P

LEVELS = 4
BLOCK = 128
LOSS_ROWS = 8
GELU_C = 0.7978845608028654
GELU_A = 0.044715

VMEM = pl.BlockSpec(memory_space=pltpu.VMEM)
SMEM = pl.BlockSpec(memory_space=pltpu.SMEM)
HBM = pl.BlockSpec(memory_space=pltpu.HBM)
ANY = pl.BlockSpec(memory_space=pl.ANY)


def f32(*shape):
    return jax.ShapeDtypeStruct(shape, jnp.float32)


def bf16(*shape):
    return jax.ShapeDtypeStruct(shape, jnp.bfloat16)


def call(kernel, outs, arrays, after=(), specs=None, out_specs=None, scratch=(), flops=0, mib=12):
    skip = slice(len(arrays), len(arrays) + len(after))

    def run(*refs):
        kernel(*refs[: skip.start], *refs[skip.stop :])

    return pl.pallas_call(
        run,
        out_shape=outs,
        in_specs=list(specs or [VMEM] * len(arrays)) + [ANY] * len(after),
        out_specs=out_specs or [VMEM] * len(outs),
        scratch_shapes=list(scratch),
        compiler_params=pltpu.CompilerParams(vmem_limit_bytes=mib * 1024 * 1024),
        cost_estimate=pl.CostEstimate(flops=flops, bytes_accessed=1 << 20, transcendentals=0),
    )(*arrays, *after)


def total_of(terms):
    return functools.reduce(jnp.add, terms)


def place_in_chain():
    lat = lax.axis_index("lat")
    return jnp.where(lax.axis_index("wid") == 0, lat, lax.axis_size("lat") - 1 - lat)


def level_table(bounds, count, out):
    lasts = bounds[...] - 1 - lax.axis_index("lat") * count
    upward = lax.axis_index("wid") == 0

    def put(row, value):
        out[row : row + 1, :] = jnp.broadcast_to(value, (1, BLOCK))

    for i in range(count):
        hits = (jnp.minimum(lasts, count - 1) == i).astype(jnp.float32)
        ending = jnp.sum(hits, axis=1, keepdims=True)
        put(i, ending)
        put(count + i, jnp.where(upward, jnp.full_like(ending, float(i == count - 1)), ending))
    for m in range(LEVELS):
        for i in range(count):
            put((2 + m) * count + i, (lasts[:, m : m + 1] == i).astype(jnp.float32))


def pre_kernel(
    resid, dictionary, bounds, partial_out, dict_out, table_out, resid_v, dict_v, sems
):
    pieces, lats, width = dict_v.shape
    here = pl.ds(pl.multiple_of(lax.axis_index("tok") * width, width), width)
    copies = [pltpu.make_async_copy(resid, resid_v, sems.at[pieces])]
    for i in range(pieces):
        cols = pl.ds(i * width, width)
        copies.append(pltpu.make_async_copy(dictionary.at[:, cols], dict_v.at[i], sems.at[i]))
    copies.append(pltpu.make_async_copy(dictionary.at[:, here], dict_out, sems.at[pieces + 1]))
    for copy in copies:
        copy.start()
    level_table(bounds, lats // BLOCK, table_out)
    copies[0].wait()
    total = None
    for i in range(pieces):
        copies[1 + i].wait()
        term = lax.dot_general(
            resid_v[:, i * width : (i + 1) * width],
            dict_v[i],
            (((1,), (1,)), ((), ())),
            preferred_element_type=jnp.float32,
        )
        total = term if total is None else total + term
    partial_out[...] = total
    copies[-1].wait()


def widen_kernel(array, out):
    out[...] = array[...].astype(jnp.float32)


def pieces_kernel(resid, bias, bias_out, *outs):
    width = outs[0].shape[1]
    tok = lax.axis_index("tok")

    def cols(t):
        return pl.ds(pl.multiple_of(t * width, width), width)

    bias_out[...] = bias[:, cols(tok)]
    for q, out in enumerate(outs):
        out[...] = resid[:, cols(tok ^ q)].astype(jnp.float32)


def block_mask(active, lats):
    first = lax.axis_index("lat") * (lats // BLOCK)
    ids = first + lax.broadcasted_iota(jnp.int32, (1, lats), 1) // BLOCK
    hit = None
    for q in range(active.shape[1]):
        same = active[:, q : q + 1] == ids
        hit = same if hit is None else hit | same
    return hit


def activate_kernel(mine, other, bias, active, pre_out, act_out):
    pre = mine[...] + other[...] + bias[...]
    pre_out[...] = pre
    inner = GELU_C * (pre + GELU_A * (pre * pre * pre))
    gelu = 0.5 * pre * (1.0 + jnp.tanh(inner))
    act_out[...] = jnp.where(block_mask(active[...], pre.shape[1]), gelu, 0.0)


def half_of(wid, rows):
    return pl.ds(pl.multiple_of(wid * (rows // 2), rows // 2), rows // 2)


def g_pre_kernel(pre_ref, active, loss, *refs):
    terms, out = refs[:-1], refs[-1]
    mine = half_of(lax.axis_index("wid"), pre_ref.shape[0])
    pre = pre_ref[mine, :]
    inner = GELU_C * (pre + GELU_A * (pre * pre * pre))
    slope = GELU_C * (1.0 + 3.0 * GELU_A * (pre * pre))
    bend = jnp.tanh(inner)
    deriv = 0.5 * (1.0 + bend) + 0.5 * pre * (1.0 - bend * bend) * slope
    hit = block_mask(active[mine, :], pre.shape[1])
    rows = pre.shape[0]
    out[:rows, :] = jnp.where(hit, deriv * total_of([t[...] for t in terms]), 0.0)
    out[rows:, :] = jnp.zeros_like(out[rows:, :])
    out[rows:, :BLOCK] = loss[...]


def running_parts(act, dict_ref):
    sums = []
    for i in range(dict_ref.shape[0] // BLOCK):
        span = slice(i * BLOCK, (i + 1) * BLOCK)
        part = jnp.dot(
            act[:, span], dict_ref[span, :].astype(jnp.bfloat16), preferred_element_type=jnp.float32
        )
        sums.append(sums[-1] + part if sums else part)
    return sums


def project_kernel(own, other, table, *refs):
    acts, rows_out, out = refs[:-2], refs[-2], refs[-1]
    rows = acts[0][...]
    if len(acts) > 1:
        rows = jnp.where(lax.axis_index("wid") == 0, rows, acts[1][...])
    rows = rows.astype(jnp.bfloat16)
    rows_out[...] = rows
    width = own.shape[1]
    for side, dict_ref in enumerate((own, other)):
        sums = running_parts(rows, dict_ref)
        count = len(sums)
        out[:, side * width : (side + 1) * width] = total_of(
            [table[count + i : count + i + 1, :1] * s for i, s in enumerate(sums)]
        )


def message_kernel(places, got, *refs):
    out = refs[-1]
    index = place_in_chain()
    for place, piece in zip(places, refs[:-1]):

        @pl.when(index == place)
        def _():
            out[...] = piece[...] + got[...] if place else piece[...]


def choose_kernel(places, *refs):
    arrived, own_out, hand_out = refs[:-2], refs[-2], refs[-1]
    width = own_out.shape[1]
    index = place_in_chain()

    @pl.when(index == 0)
    def _():
        own_out[...] = jnp.zeros_like(own_out)
        hand_out[...] = jnp.zeros_like(hand_out)

    for place, ref in zip(places, arrived):

        @pl.when(index == place if len(arrived) > 1 else index > 0)
        def _():
            own_out[...] = ref[:, :width]
            hand_out[...] = ref[:, width:]


def square_sums(table, shifted):
    count = len(shifted)
    squares = []
    for v in shifted:
        lanes = jnp.sum(v * v, axis=0, keepdims=True)
        squares.append(total_of([lanes[:, i : i + BLOCK] for i in range(0, lanes.shape[1], BLOCK)]))
    rows = []
    for m in range(LEVELS):
        at = (2 + m) * count
        rows.append(total_of([table[at + i : at + i + 1, :] * s for i, s in enumerate(squares)]))
    return jnp.concatenate(rows + [jnp.zeros((LOSS_ROWS - LEVELS, BLOCK), jnp.float32)], axis=0)


def error_kernel(act, dictionary, resid, bias, table, mine, other, *refs):
    before, (err_out, keep_out, give_out, loss_out) = refs[:-4], refs[-4:]
    upward = lax.axis_index("wid") == 0
    earlier = jnp.where(upward, mine[...], other[...])
    later = jnp.where(upward, other[...], mine[...])
    base = bias[...] - resid[...] + earlier
    sums = running_parts(act[...], dictionary)
    shifted = [base + s for s in sums]
    loss_out[...] = total_of([square_sums(table, shifted)] + [b[...] for b in before])
    err = later
    for i in reversed(range(len(sums))):
        err = err + table[i : i + 1, :1] * shifted[i]
        rounded = err.astype(jnp.bfloat16)
        err_out[i] = rounded
        cols = slice(i * BLOCK, (i + 1) * BLOCK)
        gact = lax.dot_general(
            rounded,
            dictionary[cols, :],
            (((1,), (1,)), ((), ())),
            preferred_element_type=jnp.float32,
        )
        half = gact.shape[0] // 2
        keep_out[:, cols] = jnp.where(upward, gact[:half, :], gact[half:, :])
        give_out[:, cols] = jnp.where(upward, gact[half:, :], gact[:half, :])


def add_kernel(*refs):
    refs[-1][...] = total_of([ref[...] for ref in refs[:-1]])


def decode_kernel(*refs):
    n = (len(refs) - 1) // 2
    errs, acts, out = refs[:n], refs[n : 2 * n], refs[-1]
    for i in range(errs[0].shape[0]):
        cols = slice(i * BLOCK, (i + 1) * BLOCK)
        err = jnp.concatenate([e[i] for e in errs], axis=0)
        act = jnp.concatenate([a[:, cols] for a in acts], axis=0)
        out[:, cols] = lax.dot_general(
            err, act, (((0,), (0,)), ((), ())), preferred_element_type=jnp.float32
        )


def encode_kernel(scale, *refs):
    n = (len(refs) - 3) // 3
    resids, grads, base, out, loss_out = refs[:n], refs[n : 3 * n], refs[-3], refs[-2], refs[-1]
    rows = resids[0].shape[0]
    wid = lax.axis_index("wid")
    halves = [half_of(wid, rows), half_of(1 - wid, rows)]
    resid = jnp.concatenate([r[h, :].astype(jnp.bfloat16) for h in halves for r in resids], axis=0)
    grad = jnp.concatenate([g[: rows // 2, :].astype(jnp.bfloat16) for g in grads], axis=0)
    total = base[...] + lax.dot_general(
        resid, grad, (((0,), (0,)), ((), ())), preferred_element_type=jnp.float32
    )
    out[...] = total.astype(jnp.bfloat16)
    lanes = total_of([g[rows // 2 :, :BLOCK] for g in grads])
    for m in range(LEVELS):
        loss_out[m] = jnp.sum(lanes[m : m + 1, :]) * scale


def pick(index, choices):
    values = sorted(choices)
    result = choices[values[0]]
    for value in values[1:]:
        result = jnp.where(index == value, choices[value], result)
    return result


def body(resid, dictionary, enc_bias, dec_bias, active_blocks, level_bounds):
    rows, half = resid.shape
    lats = dictionary.shape[0]
    n_lat, n_wid, n_tok = lax.axis_size("lat"), lax.axis_size("wid"), lax.axis_size("tok")
    width = half // n_tok
    count = lats // BLOCK
    work = 2 * rows * lats * width

    def across(array, q):
        return lax.ppermute(array, "tok", [(t, t ^ q) for t in range(n_tok)])

    def swap(array):
        return lax.ppermute(array, "wid", [(w, w ^ 1) for w in range(n_wid)])

    def gather(array):
        if n_tok != 4:
            return [(array,)] + [(across(array, q),) for q in range(1, n_tok)]
        pairs = [(w * n_tok + t, w * n_tok + (t ^ (1 + w))) for w in range(n_wid) for t in range(n_tok)]
        near = lax.ppermute(array, ("wid", "tok"), pairs)
        far = across(array, 3)
        other = swap(near)
        return [(array,), (near, other), (other, near), (far,)]

    partial, dict_here, table = call(
        pre_kernel,
        [f32(rows, lats), bf16(lats, width), f32((2 + LEVELS) * count, BLOCK)],
        (resid, dictionary, level_bounds.reshape(1, LEVELS)),
        specs=[HBM, HBM, VMEM],
        scratch=[
            pltpu.VMEM((rows, half), jnp.bfloat16),
            pltpu.VMEM((n_tok, lats, width), jnp.bfloat16),
            pltpu.SemaphoreType.DMA((n_tok + 2,)),
        ],
        mib=62,
    )
    partial_other = swap(partial)
    dict_wide = call(widen_kernel, [f32(lats, width)], (dict_here,), after=(partial,))[0]
    dict_other = swap(dict_wide)
    pre, act = call(
        activate_kernel,
        [f32(rows, lats)] * 2,
        (partial, partial_other, enc_bias.reshape(1, lats), active_blocks),
        after=(dict_wide,),
    )
    gathered = gather(act)
    bias_here, *pieces = call(
        pieces_kernel,
        [f32(1, width)] + [f32(rows, width)] * n_tok,
        (resid, dec_bias.reshape(1, half)),
        after=(act,),
    )
    resids = [piece if q == 0 else across(piece, q) for q, piece in enumerate(pieces)]

    order = [0, 1, 3, 2] if n_tok == 4 else list(range(n_tok))
    acts, sums = {}, []
    for q in order:
        acts[q], passed = call(
            project_kernel,
            [bf16(rows, lats), f32(rows, 2 * width)],
            (dict_here, dict_other, table, *gathered[q]),
            flops=2 * work,
        )
        sums.append(passed)

    got, sent = [], []
    errs, gacts, loss = {}, [], ()
    for step in range(n_tok + 2 * (n_lat - 1)):
        if step < n_tok + n_lat - 2:
            at = [p for p in range(n_lat - 1) if 0 <= step - p < n_tok]
            message = sums[0]
            if step:
                done = step - n_lat
                after = [errs[order[done]]] if done >= 0 else []
                if 0 <= step - n_lat + 1 < n_tok - 1:
                    after.append(resids[order[step - n_lat + 2]])
                message = call(
                    functools.partial(message_kernel, at),
                    [f32(rows, 2 * width)],
                    (got[-1], *[sums[step - p] for p in at]),
                    after=after,
                )[0]
            pairs = []
            for p in at:
                pairs.append((2 * p, 2 * (p + 1)))
                pairs.append((2 * (n_lat - 1 - p) + 1, 2 * (n_lat - 2 - p) + 1))
            got.append(lax.ppermute(message, ("lat", "wid"), pairs))
            sent = [message]
        c = step - (n_lat - 1)
        if not 0 <= c < n_tok:
            continue
        q = order[c]
        places = list(range(1, n_lat))
        arrived = [got[c + p - 1] for p in places]
        if n_lat > 4:
            arrived = [pick(place_in_chain(), dict(zip(places, arrived)))]
        mine, hand = call(
            functools.partial(choose_kernel, places), [f32(rows, width)] * 2, arrived, after=sent
        )
        errs[q], keep, give, loss_here = call(
            error_kernel,
            [bf16(count, rows, width)] + [f32(rows // 2, lats)] * 2 + [f32(LOSS_ROWS, BLOCK)],
            (acts[q], dict_here, resids[q], bias_here, table, mine, swap(hand), *loss),
            flops=2 * work,
        )
        loss = (loss_here,)
        if q == 0:
            gacts += [keep, swap(give)]
        else:
            gacts.append(across(call(add_kernel, [f32(rows // 2, lats)], (keep, swap(give)))[0], q))
        sent = []

    loss, gap = loss[0], 1
    while gap < n_lat:
        other = lax.ppermute(loss, "lat", [(p, p ^ gap) for p in range(n_lat)])
        loss = call(add_kernel, [f32(LOSS_ROWS, BLOCK)], (loss, other))[0]
        gap *= 2

    g_pre = call(
        g_pre_kernel, [f32(rows // 2 + LOSS_ROWS, lats)], (pre, active_blocks, loss, *gacts)
    )[0]
    mine = [across(g_pre, q) if q else g_pre for q in range(n_tok)]
    others = [swap(g) for g in mine]
    decoded = call(
        decode_kernel,
        [f32(width, lats)],
        (*[errs[q] for q in order], *[acts[q] for q in order]),
        flops=n_tok * work,
    )[0]
    grad, losses = call(
        functools.partial(encode_kernel, 1.0 / (rows * n_tok * half * n_wid)),
        [bf16(width, lats), f32(LEVELS)],
        (*resids, *mine, *others, decoded),
        out_specs=[VMEM, SMEM],
        flops=n_tok * work,
    )
    return (losses, grad)


def solution(mesh):
    return jax.shard_map(
        body,
        mesh=mesh,
        in_specs=(P("tok", "wid"), P("lat", "wid"), P("lat"), P("wid"), P("tok", None), P()),
        out_specs=(P(), P(("wid", "tok"), "lat")),
        check_vma=False,
    )
```

```python
import functools

import jax
import jax.numpy as jnp
from jax import lax
from jax.experimental import pallas as pl
from jax.experimental.pallas import tpu as pltpu
from jax.sharding import PartitionSpec as P

LEVELS = 4
BLOCK = 128
LOSS_ROWS = 8
GELU_C = 0.7978845608028654
GELU_A = 0.044715

VMEM = pl.BlockSpec(memory_space=pltpu.VMEM)
SMEM = pl.BlockSpec(memory_space=pltpu.SMEM)
HBM = pl.BlockSpec(memory_space=pltpu.HBM)
ANY = pl.BlockSpec(memory_space=pl.ANY)


def f32(*shape):
    return jax.ShapeDtypeStruct(shape, jnp.float32)


def bf16(*shape):
    return jax.ShapeDtypeStruct(shape, jnp.bfloat16)


def call(kernel, outs, arrays, after=(), specs=None, out_specs=None, scratch=()):
    skip = slice(len(arrays), len(arrays) + len(after))

    def run(*refs):
        kernel(*refs[: skip.start], *refs[skip.stop :])

    return pl.pallas_call(
        run,
        out_shape=outs,
        in_specs=list(specs or [VMEM] * len(arrays)) + [ANY] * len(after),
        out_specs=out_specs or [VMEM] * len(outs),
        scratch_shapes=list(scratch),
        compiler_params=pltpu.CompilerParams(vmem_limit_bytes=12 * 1024 * 1024),
        cost_estimate=pl.CostEstimate(flops=0, bytes_accessed=1 << 10, transcendentals=0),
    )(*arrays, *after)


def in_hbm(array):
    return pltpu.with_memory_space_constraint(array, pltpu.HBM)


def total_of(terms):
    return functools.reduce(jnp.add, terms)


def place_in_chain():
    lat = lax.axis_index("lat")
    return jnp.where(lax.axis_index("wid") == 0, lat, lax.axis_size("lat") - 1 - lat)


def level_table(bounds, count, out):
    lasts = bounds[...] - 1 - lax.axis_index("lat") * count
    upward = lax.axis_index("wid") == 0

    def put(row, value):
        out[row : row + 1, :] = jnp.broadcast_to(value, (1, BLOCK))

    for i in range(count):
        hits = (jnp.minimum(lasts, count - 1) == i).astype(jnp.float32)
        ending = jnp.sum(hits, axis=1, keepdims=True)
        put(i, ending)
        put(count + i, jnp.where(upward, jnp.full_like(ending, float(i == count - 1)), ending))
    for m in range(LEVELS):
        for i in range(count):
            put((2 + m) * count + i, (lasts[:, m : m + 1] == i).astype(jnp.float32))


def pre_kernel(
    resid, dictionary, partial_out, dict_out, resid_v, dict_v, sems
):
    pieces, lats, width = dict_v.shape
    ahead = 3

    def copies(i):
        cols = pl.ds(i * width, width)
        return (
            pltpu.make_async_copy(resid.at[:, cols], resid_v.at[i], sems.at[0, i]),
            pltpu.make_async_copy(dictionary.at[:, cols], dict_v.at[i], sems.at[1, i]),
        )

    for i in range(min(ahead, pieces)):
        for copy in copies(i):
            copy.start()
    total = None
    for i in range(pieces):
        for copy in copies(i):
            copy.wait()
        if i + ahead < pieces:
            for copy in copies(i + ahead):
                copy.start()
        term = lax.dot_general(
            resid_v[i], dict_v[i], (((1,), (1,)), ((), ())), preferred_element_type=jnp.float32
        )
        total = term if total is None else total + term
    partial_out[...] = total
    parts = dict_out.shape[1] // width
    for i in range(parts):
        dict_out[:, i * width : (i + 1) * width] = dict_v[lax.axis_index("tok") * parts + i]


def widen_kernel(array, bounds, out, table_out):
    out[...] = array[...].astype(jnp.float32)
    level_table(bounds, array.shape[0] // BLOCK, table_out)


def pieces_kernel(resid, bias, bias_out, *outs):
    width = outs[0].shape[1]
    tok = lax.axis_index("tok")

    def cols(t):
        return pl.ds(pl.multiple_of(t * width, width), width)

    bias_out[...] = bias[:, cols(tok)]
    for q, out in enumerate(outs):
        out[...] = resid[:, cols(tok ^ q)].astype(jnp.float32)


def block_mask(active, lats):
    count = lats // BLOCK
    ids = lax.axis_index("lat") * count + lax.broadcasted_iota(jnp.int32, (count, 1), 0)
    hits = total_of([(active[q : q + 1, :] == ids).astype(jnp.float32) for q in range(active.shape[0])])
    spread = lax.broadcasted_iota(jnp.int32, (count, lats), 1) // BLOCK
    spread = (spread == lax.broadcasted_iota(jnp.int32, (count, lats), 0)).astype(jnp.bfloat16)
    return lax.dot_general(
        hits.astype(jnp.bfloat16),
        spread,
        (((0,), (0,)), ((), ())),
        preferred_element_type=jnp.float32,
    )


def activate_kernel(mine, other, bias, active, pre_out, act_out, mask_out):
    pre = mine[...] + other[...] + bias[...]
    pre_out[...] = pre
    inner = GELU_C * (pre + GELU_A * (pre * pre * pre))
    gelu = 0.5 * pre * (1.0 + jnp.tanh(inner))
    mask = block_mask(active[...], pre.shape[1])
    mask_out[...] = mask
    act_out[...] = jnp.where(mask > 0.0, gelu, 0.0)


def half_of(wid, rows):
    return pl.ds(pl.multiple_of(wid * (rows // 2), rows // 2), rows // 2)


def g_pre_kernel(pre_ref, mask, loss, *refs):
    terms, out = refs[:-1], refs[-1]
    mine = half_of(lax.axis_index("wid"), pre_ref.shape[0])
    pre = pre_ref[mine, :]
    inner = GELU_C * (pre + GELU_A * (pre * pre * pre))
    slope = GELU_C * (1.0 + 3.0 * GELU_A * (pre * pre))
    bend = jnp.tanh(inner)
    deriv = 0.5 * (1.0 + bend) + 0.5 * pre * (1.0 - bend * bend) * slope
    hit = mask[mine, :] > 0.0
    rows = pre.shape[0]
    out[:rows, :] = jnp.where(hit, deriv * total_of([t[...] for t in terms]), 0.0)
    out[rows:, :] = jnp.zeros_like(out[rows:, :])
    out[rows:, :BLOCK] = loss[...]


def running_parts(act, dict_ref):
    sums = []
    for i in range(dict_ref.shape[0] // BLOCK):
        span = slice(i * BLOCK, (i + 1) * BLOCK)
        part = jnp.dot(
            act[:, span], dict_ref[span, :].astype(jnp.bfloat16), preferred_element_type=jnp.float32
        )
        sums.append(sums[-1] + part if sums else part)
    return sums


def round_kernel(*refs):
    rows = refs[0][...]
    if len(refs) > 2:
        rows = jnp.where(lax.axis_index("wid") == 0, rows, refs[1][...])
    refs[-1][...] = rows.astype(jnp.bfloat16)


def project_kernel(act, dictionary, table, out):
    sums = running_parts(act[...], dictionary)
    count = len(sums)
    out[...] = total_of([table[count + i : count + i + 1, :1] * s for i, s in enumerate(sums)])


def message_kernel(places, got, *refs):
    out = refs[-1]
    index = place_in_chain()
    for place, piece in zip(places, refs[:-1]):

        @pl.when(index == place)
        def _():
            out[...] = piece[...] + got[...] if place else piece[...]


def choose_kernel(places, *refs):
    arrived, out = refs[:-1], refs[-1]
    index = place_in_chain()

    @pl.when(index == 0)
    def _():
        out[...] = jnp.zeros_like(out)

    for place, ref in zip(places, arrived):

        @pl.when(index == place if len(arrived) > 1 else index > 0)
        def _():
            out[...] = ref[...]


def square_sums(table, shifted):
    count = len(shifted)
    squares = []
    for v in shifted:
        lanes = jnp.sum(v * v, axis=0, keepdims=True)
        squares.append(total_of([lanes[:, i : i + BLOCK] for i in range(0, lanes.shape[1], BLOCK)]))
    rows = []
    for m in range(LEVELS):
        at = (2 + m) * count
        rows.append(total_of([table[at + i : at + i + 1, :] * s for i, s in enumerate(squares)]))
    return jnp.concatenate(rows + [jnp.zeros((LOSS_ROWS - LEVELS, BLOCK), jnp.float32)], axis=0)


def error_kernel(act, dictionary, resid, bias, table, mine, other, *refs):
    before, (err_out, keep_out, give_out, loss_out) = refs[:-4], refs[-4:]
    upward = lax.axis_index("wid") == 0
    earlier = jnp.where(upward, mine[...], other[...])
    later = jnp.where(upward, other[...], mine[...])
    base = bias[...] - resid[...] + earlier
    sums = running_parts(act[...], dictionary)
    shifted = [base + s for s in sums]
    loss_out[...] = total_of([square_sums(table, shifted)] + [b[...] for b in before])
    err = later
    for i in reversed(range(len(sums))):
        err = err + table[i : i + 1, :1] * shifted[i]
        rounded = err.astype(jnp.bfloat16)
        err_out[i] = rounded
        cols = slice(i * BLOCK, (i + 1) * BLOCK)
        gact = lax.dot_general(
            rounded,
            dictionary[cols, :],
            (((1,), (1,)), ((), ())),
            preferred_element_type=jnp.float32,
        )
        half = gact.shape[0] // 2
        keep_out[:, cols] = jnp.where(upward, gact[:half, :], gact[half:, :])
        give_out[:, cols] = jnp.where(upward, gact[half:, :], gact[:half, :])


def add_kernel(*refs):
    refs[-1][...] = total_of([ref[...] for ref in refs[:-1]])


def decode_kernel(*refs):
    n = (len(refs) - 1) // 2
    errs, acts, out = refs[:n], refs[n : 2 * n], refs[-1]
    for i in range(errs[0].shape[0]):
        cols = slice(i * BLOCK, (i + 1) * BLOCK)
        err = jnp.concatenate([e[i] for e in errs], axis=0)
        act = jnp.concatenate([a[:, cols] for a in acts], axis=0)
        out[:, cols] = lax.dot_general(
            err, act, (((0,), (0,)), ((), ())), preferred_element_type=jnp.float32
        )


def encode_kernel(scale, *refs):
    n = (len(refs) - 3) // 3
    resids, grads, base, out, loss_out = refs[:n], refs[n : 3 * n], refs[-3], refs[-2], refs[-1]
    rows = resids[0].shape[0]
    wid = lax.axis_index("wid")
    halves = [half_of(wid, rows), half_of(1 - wid, rows)]
    resid = jnp.concatenate([r[h, :].astype(jnp.bfloat16) for h in halves for r in resids], axis=0)
    grad = jnp.concatenate([g[: rows // 2, :].astype(jnp.bfloat16) for g in grads], axis=0)
    total = base[...] + lax.dot_general(
        resid, grad, (((0,), (0,)), ((), ())), preferred_element_type=jnp.float32
    )
    out[...] = total.astype(jnp.bfloat16)
    lanes = total_of([g[rows // 2 :, :BLOCK] for g in grads])
    for m in range(LEVELS):
        loss_out[m] = jnp.sum(lanes[m : m + 1, :]) * scale


def pick(index, choices):
    values = sorted(choices)
    result = choices[values[0]]
    for value in values[1:]:
        result = jnp.where(index == value, choices[value], result)
    return result


def body(resid, dictionary, enc_bias, dec_bias, active_blocks, level_bounds):
    rows, half = resid.shape
    lats = dictionary.shape[0]
    n_lat, n_wid, n_tok = lax.axis_size("lat"), lax.axis_size("wid"), lax.axis_size("tok")
    width = half // n_tok
    count = lats // BLOCK

    def across(array, q):
        return lax.ppermute(array, "tok", [(t, t ^ q) for t in range(n_tok)])

    def swap(array):
        return lax.ppermute(array, "wid", [(w, w ^ 1) for w in range(n_wid)])

    def gather(array):
        if n_tok != 4:
            return [(array,)] + [(across(array, q),) for q in range(1, n_tok)]
        pairs = [(w * n_tok + t, w * n_tok + (t ^ (1 + w))) for w in range(n_wid) for t in range(n_tok)]
        near = lax.ppermute(array, ("wid", "tok"), pairs)
        far = across(array, 3)
        other = swap(near)
        return [(array,), (near, other), (other, near), (far,)]

    partial, dict_here = call(
        pre_kernel,
        [f32(rows, lats), bf16(lats, width)],
        (in_hbm(resid), in_hbm(dictionary)),
        specs=[HBM, HBM],
        scratch=[
            pltpu.VMEM((2 * n_tok, rows, width // 2), jnp.bfloat16),
            pltpu.VMEM((2 * n_tok, lats, width // 2), jnp.bfloat16),
            pltpu.SemaphoreType.DMA((2, 2 * n_tok)),
        ],
    )
    partial_other = swap(partial)
    dict_wide, table = call(
        widen_kernel,
        [f32(lats, width), f32((2 + LEVELS) * count, BLOCK)],
        (dict_here, level_bounds.reshape(1, LEVELS)),
        after=(partial_other,),
    )
    dict_other = swap(dict_wide)
    pre, act, mask = call(
        activate_kernel,
        [f32(rows, lats)] * 3,
        (partial, partial_other, enc_bias.reshape(1, lats), active_blocks.T),
        after=(dict_wide,),
    )
    gathered = gather(act)
    bias_here, *pieces = call(
        pieces_kernel,
        [f32(1, width)] + [f32(rows, width)] * n_tok,
        (resid, dec_bias.reshape(1, half)),
        after=(act,),
    )
    resids = [piece if q == 0 else across(piece, q) for q, piece in enumerate(pieces)]

    order = [0, 1, 3, 2] if n_tok == 4 else list(range(n_tok))
    steps = n_tok + n_lat - 2
    places = list(range(1, n_lat))
    acts, sums, got, sent = {}, ([], []), ([], []), []
    errs, gacts, loss = {}, [], ()
    waits = {step: [] for step in range(steps)}
    for place, q in enumerate(order[1:]):
        waits[2 + min(place, 1)].append(resids[q])
    for step in range(steps + 1):
        for side, dict_ref in enumerate((dict_here, dict_other)):
            if step == steps:
                break
            if step == 0:
                q = order[0]
                if side == 0:
                    acts[q] = call(round_kernel, [bf16(rows, lats)], gathered[q])[0]
                sums[side].append(
                    call(
                        project_kernel,
                        [f32(rows, width)],
                        (acts[q], dict_ref, table),
                        after=sent,
                    )[0]
                )
            at = [p for p in range(n_lat - 1) if 0 <= step - p < n_tok]
            message = sums[side][0]
            if step:
                message = call(
                    functools.partial(message_kernel, at),
                    [f32(rows, width)],
                    (got[side][-1], *[sums[side][step - p] for p in at]),
                    after=sent + (waits[step] if side == 0 else []),
                )[0]
            pairs = []
            for p in at:
                pairs.append((2 * p, 2 * (p + 1)))
                pairs.append((2 * (n_lat - 1 - p) + 1, 2 * (n_lat - 2 - p) + 1))
            got[side].append(lax.ppermute(message, ("lat", "wid"), pairs))
            sent = [message]
        if step + 1 < n_tok:
            q = order[step + 1]
            acts[q] = call(round_kernel, [bf16(rows, lats)], gathered[q], after=sent)[0]
            for side, dict_ref in enumerate((dict_here, dict_other)):
                sums[side].append(
                    call(
                        project_kernel, [f32(rows, width)], (acts[q], dict_ref, table)
                    )[0]
                )
        c = step - (n_lat - 1)
        if c < 0:
            continue
        q = order[c]
        ahead = sent + [got[0][step]] if step < steps else []
        if c:
            ahead.append(added)
        if c > 1:
            ahead.append(gacts[-2])
        chosen = []
        for side in (1, 0):
            arrived = [got[side][c + p - 1] for p in places]
            if n_lat > 4:
                arrived = [pick(place_in_chain(), dict(zip(places, arrived)))]
            chosen.append(
                call(
                    functools.partial(choose_kernel, places),
                    [f32(rows, width)],
                    arrived,
                    after=ahead,
                )[0]
            )
        hand, mine = chosen
        errs[q], keep, give, loss_here = call(
            error_kernel,
            [bf16(count, rows, width)] + [f32(rows // 2, lats)] * 2 + [f32(LOSS_ROWS, BLOCK)],
            (acts[q], dict_here, resids[q], bias_here, table, mine, swap(hand), *loss),
        )
        loss = (loss_here,)
        waits.setdefault(step + 2, []).append(errs[q])
        added = call(add_kernel, [f32(rows // 2, lats)], (keep, swap(give)))[0]
        gacts.append(across(added, q) if q else added)

    loss, gap = loss[0], 1
    while gap < n_lat:
        other = lax.ppermute(loss, "lat", [(p, p ^ gap) for p in range(n_lat)])
        loss = call(add_kernel, [f32(LOSS_ROWS, BLOCK)], (loss, other))[0]
        gap *= 2

    g_pre = call(
        g_pre_kernel, [f32(rows // 2 + LOSS_ROWS, lats)], (pre, mask, loss, *gacts)
    )[0]
    mine = [across(g_pre, q) if q else g_pre for q in range(n_tok)]
    others = [swap(g) for g in mine]
    decoded = call(
        decode_kernel,
        [f32(width, lats)],
        (*[errs[q] for q in order], *[acts[q] for q in order]),
    )[0]
    grad, losses = call(
        functools.partial(encode_kernel, 1.0 / (rows * n_tok * half * n_wid)),
        [bf16(width, lats), f32(LEVELS)],
        (*resids, *mine, *others, decoded),
        out_specs=[VMEM, SMEM],
    )
    return (losses, grad)


def solution(mesh):
    return jax.shard_map(
        body,
        mesh=mesh,
        in_specs=(P("tok", "wid"), P("lat", "wid"), P("lat"), P("wid"), P("tok", None), P()),
        out_specs=(P(), P(("wid", "tok"), "lat")),
        check_vma=False,
    )
```

```python
import functools

import jax
import jax.numpy as jnp
from jax import lax
from jax.experimental import pallas as pl
from jax.experimental.pallas import tpu as pltpu
from jax.sharding import PartitionSpec as P

LEVELS = 4
BLOCK = 128
LOSS_ROWS = 8
GELU_C = 0.7978845608028654
GELU_A = 0.044715

VMEM = pl.BlockSpec(memory_space=pltpu.VMEM)
SMEM = pl.BlockSpec(memory_space=pltpu.SMEM)
HBM = pl.BlockSpec(memory_space=pltpu.HBM)
ANY = pl.BlockSpec(memory_space=pl.ANY)


def f32(*shape):
    return jax.ShapeDtypeStruct(shape, jnp.float32)


def bf16(*shape):
    return jax.ShapeDtypeStruct(shape, jnp.bfloat16)


def call(kernel, outs, arrays, after=(), specs=None, out_specs=None, scratch=()):
    skip = slice(len(arrays), len(arrays) + len(after))

    def run(*refs):
        kernel(*refs[: skip.start], *refs[skip.stop :])

    return pl.pallas_call(
        run,
        out_shape=outs,
        in_specs=list(specs or [VMEM] * len(arrays)) + [ANY] * len(after),
        out_specs=out_specs or [VMEM] * len(outs),
        scratch_shapes=list(scratch),
        compiler_params=pltpu.CompilerParams(vmem_limit_bytes=12 * 1024 * 1024),
        cost_estimate=pl.CostEstimate(flops=0, bytes_accessed=1 << 10, transcendentals=0),
    )(*arrays, *after)


def in_hbm(array):
    return pltpu.with_memory_space_constraint(array, pltpu.HBM)


def total_of(terms):
    return functools.reduce(jnp.add, terms)


def place_in_chain():
    lat = lax.axis_index("lat")
    return jnp.where(lax.axis_index("wid") == 0, lat, lax.axis_size("lat") - 1 - lat)


def level_table(bounds, count, out):
    lasts = bounds[...] - 1 - lax.axis_index("lat") * count
    upward = lax.axis_index("wid") == 0

    def put(row, value):
        out[row : row + 1, :] = jnp.broadcast_to(value, (1, BLOCK))

    for i in range(count):
        hits = (jnp.minimum(lasts, count - 1) == i).astype(jnp.float32)
        ending = jnp.sum(hits, axis=1, keepdims=True)
        put(i, ending)
        put(count + i, jnp.where(upward, jnp.full_like(ending, float(i == count - 1)), ending))
    for m in range(LEVELS):
        for i in range(count):
            put((2 + m) * count + i, (lasts[:, m : m + 1] == i).astype(jnp.float32))


def pre_kernel(resid, dictionary, partial_out, dict_out, resid_v, dict_v, sems):
    pieces, _, width = dict_v.shape
    copies = []
    for i in range(pieces):
        cols = pl.ds(i * width, width)
        copies.append(
            (
                pltpu.make_async_copy(resid.at[:, cols], resid_v.at[i], sems.at[0, i]),
                pltpu.make_async_copy(dictionary.at[:, cols], dict_v.at[i], sems.at[1, i]),
            )
        )
        for copy in copies[-1]:
            copy.start()
    total = None
    for i in range(pieces):
        for copy in copies[i]:
            copy.wait()
        term = lax.dot_general(
            dict_v[i], resid_v[i], (((1,), (1,)), ((), ())), preferred_element_type=jnp.float32
        )
        total = term if total is None else total + term
    partial_out[...] = total.T
    parts = dict_out.shape[1] // width
    for i in range(parts):
        dict_out[:, i * width : (i + 1) * width] = dict_v[lax.axis_index("tok") * parts + i]


def widen_kernel(array, bounds, out, table_out):
    out[...] = array[...].astype(jnp.float32)
    level_table(bounds, array.shape[0] // BLOCK, table_out)


def pieces_kernel(resid, bias, bias_out, *outs):
    width = outs[0].shape[1]
    tok = lax.axis_index("tok")

    def cols(t):
        return pl.ds(pl.multiple_of(t * width, width), width)

    bias_out[...] = bias[:, cols(tok)]
    for q, out in enumerate(outs):
        out[...] = resid[:, cols(tok ^ q)].astype(jnp.float32)


def block_mask(active, lats):
    count = lats // BLOCK
    ids = lax.axis_index("lat") * count + lax.broadcasted_iota(jnp.int32, (count, 1), 0)
    hits = total_of([(active[q : q + 1, :] == ids).astype(jnp.float32) for q in range(active.shape[0])])
    spread = lax.broadcasted_iota(jnp.int32, (count, lats), 1) // BLOCK
    spread = (spread == lax.broadcasted_iota(jnp.int32, (count, lats), 0)).astype(jnp.bfloat16)
    return lax.dot_general(
        hits.astype(jnp.bfloat16),
        spread,
        (((0,), (0,)), ((), ())),
        preferred_element_type=jnp.float32,
    )


def activate_kernel(mine, other, bias, active, pre_out, act_out, mask_out):
    pre = mine[...] + other[...] + bias[...]
    pre_out[...] = pre
    inner = GELU_C * (pre + GELU_A * (pre * pre * pre))
    gelu = 0.5 * pre * (1.0 + jnp.tanh(inner))
    mask = block_mask(active[...], pre.shape[1])
    mask_out[...] = mask
    act_out[...] = jnp.where(mask > 0.0, gelu, 0.0)


def half_of(wid, rows):
    return pl.ds(pl.multiple_of(wid * (rows // 2), rows // 2), rows // 2)


def g_pre_kernel(pre_ref, mask, loss, *refs):
    terms, out = refs[:-1], refs[-1]
    mine = half_of(lax.axis_index("wid"), pre_ref.shape[0])
    pre = pre_ref[mine, :]
    inner = GELU_C * (pre + GELU_A * (pre * pre * pre))
    slope = GELU_C * (1.0 + 3.0 * GELU_A * (pre * pre))
    bend = jnp.tanh(inner)
    deriv = 0.5 * (1.0 + bend) + 0.5 * pre * (1.0 - bend * bend) * slope
    hit = mask[mine, :] > 0.0
    rows = pre.shape[0]
    out[:rows, :] = jnp.where(hit, deriv * total_of([t[...] for t in terms]), 0.0)
    out[rows:, :] = jnp.zeros_like(out[rows:, :])
    out[rows:, :BLOCK] = loss[...]


def running_parts(act, dict_ref):
    sums = []
    for i in range(dict_ref.shape[0] // BLOCK):
        span = slice(i * BLOCK, (i + 1) * BLOCK)
        part = jnp.dot(
            act[:, span], dict_ref[span, :].astype(jnp.bfloat16), preferred_element_type=jnp.float32
        )
        sums.append(sums[-1] + part if sums else part)
    return sums


def round_kernel(act, out):
    out[...] = act[...].astype(jnp.bfloat16)


def project_kernel(act, table, *refs):
    dicts, out = refs[:-1], refs[-1]
    for side, dictionary in enumerate(dicts):
        sums = running_parts(act[...], dictionary)
        count = len(sums)
        width = dictionary.shape[1]
        out[:, side * width : (side + 1) * width] = total_of(
            [table[count + i : count + i + 1, :1] * s for i, s in enumerate(sums)]
        )


def columns(ref, col, width):
    return ref[:, col * width : (col + 1) * width]


def message_kernel(places, cols, got, *refs):
    out = refs[-1]
    width = out.shape[1]
    index = place_in_chain()
    for place, piece, col in zip(places, refs[:-1], cols[1:]):

        @pl.when(index == place)
        def _():
            own = columns(piece, col, width)
            out[...] = own + columns(got, cols[0], width) if place else own


def choose_kernel(places, cols, *refs):
    arrived, out = refs[:-1], refs[-1]
    index = place_in_chain()

    @pl.when(index == 0)
    def _():
        out[...] = jnp.zeros_like(out)

    for place, ref, col in zip(places, arrived, cols):

        @pl.when(index == place if len(arrived) > 1 else index > 0)
        def _():
            out[...] = columns(ref, col, out.shape[1])


def square_sums(table, shifted):
    count = len(shifted)
    squares = []
    for v in shifted:
        lanes = jnp.sum(v * v, axis=0, keepdims=True)
        squares.append(total_of([lanes[:, i : i + BLOCK] for i in range(0, lanes.shape[1], BLOCK)]))
    rows = []
    for m in range(LEVELS):
        at = (2 + m) * count
        rows.append(total_of([table[at + i : at + i + 1, :] * s for i, s in enumerate(squares)]))
    return jnp.concatenate(rows + [jnp.zeros((LOSS_ROWS - LEVELS, BLOCK), jnp.float32)], axis=0)


def error_kernel(act, dictionary, resid, bias, table, mine, other, *refs):
    before, (err_out, keep_out, give_out, loss_out) = refs[:-4], refs[-4:]
    upward = lax.axis_index("wid") == 0
    earlier = jnp.where(upward, mine[...], other[...])
    later = jnp.where(upward, other[...], mine[...])
    base = bias[...] - resid[...] + earlier
    sums = running_parts(act[...], dictionary)
    shifted = [base + s for s in sums]
    loss_out[...] = total_of([square_sums(table, shifted)] + [b[...] for b in before])
    err = later
    for i in reversed(range(len(sums))):
        err = err + table[i : i + 1, :1] * shifted[i]
        rounded = err.astype(jnp.bfloat16)
        err_out[i] = rounded
        cols = slice(i * BLOCK, (i + 1) * BLOCK)
        gact = lax.dot_general(
            rounded,
            dictionary[cols, :],
            (((1,), (1,)), ((), ())),
            preferred_element_type=jnp.float32,
        )
        half = gact.shape[0] // 2
        keep_out[:, cols] = jnp.where(upward, gact[:half, :], gact[half:, :])
        give_out[:, cols] = jnp.where(upward, gact[half:, :], gact[:half, :])


def add_kernel(*refs):
    refs[-1][...] = total_of([ref[...] for ref in refs[:-1]])


def decode_kernel(*refs):
    n = (len(refs) - 1) // 2
    errs, acts, out = refs[:n], refs[n : 2 * n], refs[-1]
    for i in range(errs[0].shape[0]):
        cols = slice(i * BLOCK, (i + 1) * BLOCK)
        err = jnp.concatenate([e[i] for e in errs], axis=0)
        act = jnp.concatenate([a[:, cols] for a in acts], axis=0)
        out[:, cols] = lax.dot_general(
            err, act, (((0,), (0,)), ((), ())), preferred_element_type=jnp.float32
        )


def encode_kernel(scale, *refs):
    n = (len(refs) - 3) // 3
    resids, grads, base, out, loss_out = refs[:n], refs[n : 3 * n], refs[-3], refs[-2], refs[-1]
    rows = resids[0].shape[0]
    wid = lax.axis_index("wid")
    halves = [half_of(wid, rows), half_of(1 - wid, rows)]
    resid = jnp.concatenate([r[h, :].astype(jnp.bfloat16) for h in halves for r in resids], axis=0)
    grad = jnp.concatenate([g[: rows // 2, :].astype(jnp.bfloat16) for g in grads], axis=0)
    total = base[...] + lax.dot_general(
        resid, grad, (((0,), (0,)), ((), ())), preferred_element_type=jnp.float32
    )
    out[...] = total.astype(jnp.bfloat16)
    lanes = total_of([g[rows // 2 :, :BLOCK] for g in grads])
    for m in range(LEVELS):
        loss_out[m] = jnp.sum(lanes[m : m + 1, :]) * scale


def pick(index, choices):
    values = sorted(choices)
    result = choices[values[0]]
    for value in values[1:]:
        result = jnp.where(index == value, choices[value], result)
    return result


def body(resid, dictionary, enc_bias, dec_bias, active_blocks, level_bounds):
    rows, half = resid.shape
    lats = dictionary.shape[0]
    n_lat, n_wid, n_tok = lax.axis_size("lat"), lax.axis_size("wid"), lax.axis_size("tok")
    width = half // n_tok
    count = lats // BLOCK

    def across(array, q):
        return lax.ppermute(array, "tok", [(t, t ^ q) for t in range(n_tok)])

    def swap(array):
        return lax.ppermute(array, "wid", [(w, w ^ 1) for w in range(n_wid)])

    partial, dict_here = call(
        pre_kernel,
        [f32(rows, lats), bf16(lats, width)],
        (in_hbm(resid), in_hbm(dictionary)),
        specs=[HBM, HBM],
        scratch=[
            pltpu.VMEM((2 * n_tok, rows, width // 2), jnp.bfloat16),
            pltpu.VMEM((2 * n_tok, lats, width // 2), jnp.bfloat16),
            pltpu.SemaphoreType.DMA((2, 2 * n_tok)),
        ],
    )
    partial_other = swap(partial)
    dict_wide, table = call(
        widen_kernel,
        [f32(lats, width), f32((2 + LEVELS) * count, BLOCK)],
        (dict_here, level_bounds.reshape(1, LEVELS)),
        after=(partial_other,),
    )
    dict_other = swap(dict_wide)
    pre, act, mask = call(
        activate_kernel,
        [f32(rows, lats)] * 3,
        (partial, partial_other, enc_bias.reshape(1, lats), active_blocks.T),
        after=(dict_wide,),
    )
    bias_here, *pieces = call(
        pieces_kernel,
        [f32(1, width)] + [f32(rows, width)] * n_tok,
        (resid, dec_bias.reshape(1, half)),
        after=(act,),
    )
    resids = [piece if q == 0 else across(piece, q) for q, piece in enumerate(pieces)]

    order = [0, 1, 3, 2] if n_tok == 4 else list(range(n_tok))
    steps = n_tok + n_lat - 2
    places = list(range(1, n_lat))
    acts, errs, hands, gives, gacts, loss = {}, {}, [], [], [], ()
    sums, got, sent = ([], []), ([], []), []
    waits = {step: [] for step in range(steps)}
    for place, q in enumerate(order[1:]):
        waits[min(3 + place, steps - 1)].append(resids[q])

    def project(q, dicts):
        shape = [f32(rows, width * len(dicts))]
        return call(project_kernel, shape, (acts[q], table, *dicts))[0]

    for step in range(steps + 1):
        at = [p for p in range(n_lat - 1) if 0 <= step - p < n_tok]
        pairs = []
        for p in at:
            pairs.append((2 * p, 2 * (p + 1)))
            pairs.append((2 * (n_lat - 1 - p) + 1, 2 * (n_lat - 2 - p) + 1))
        if step == 0:
            acts[order[0]] = call(round_kernel, [bf16(rows, lats)], (act,))[0]
            message = project(order[0], (dict_here, dict_other))
            arrived = lax.ppermute(message, ("lat", "wid"), pairs)
            for side in range(2):
                sums[side].append((message, side))
                got[side].append((arrived, side))
            sent = [arrived]
        elif step < steps:
            for side in range(2):
                items = [got[side][-1], *[sums[side][step - p] for p in at]]
                message = call(
                    functools.partial(message_kernel, at, [col for _, col in items]),
                    [f32(rows, width)],
                    [array for array, _ in items],
                    after=sent + (waits[step] if side == 0 else []) if step > 1 else (),
                )[0]
                got[side].append((lax.ppermute(message, ("lat", "wid"), pairs), 0))
                sent = [message]
        if step + 1 < n_tok:
            q = order[step + 1]
            gathered = across(act, q)
            acts[q] = call(round_kernel, [bf16(rows, lats)], (gathered,), after=sent)[0]
            for side, dict_ref in enumerate((dict_here, dict_other)):
                sums[side].append((project(q, (dict_ref,)), 0))
        ready = []
        c = step - (n_lat - 1)
        if c >= 0:
            chosen = []
            for side in (1, 0):
                items = [got[side][c + p - 1] for p in places]
                if n_lat > 4:
                    items = [a[:, col * width : (col + 1) * width] for a, col in items]
                    items = [(pick(place_in_chain(), dict(zip(places, items))), 0)]
                chosen.append(
                    call(
                        functools.partial(choose_kernel, places, [col for _, col in items]),
                        [f32(rows, width)],
                        [array for array, _ in items],
                        after=sent if step < steps else ready_before,
                    )[0]
                )
            hands.append((swap(chosen[0]), chosen[1]))
            ready += chosen
        stages = [c - 1] if step < steps - 1 else [c - 1, c] if step < steps else [c]
        for c in stages:
            if c < 0:
                continue
            q = order[c]
            errs[q], keep, give, loss_here = call(
                error_kernel,
                [bf16(count, rows, width)] + [f32(rows // 2, lats)] * 2 + [f32(LOSS_ROWS, BLOCK)],
                (acts[q], dict_here, resids[q], bias_here, table, hands[c][1], hands[c][0], *loss),
                after=sent if step < steps else (),
            )
            loss = (loss_here,)
            gives.append((keep, swap(give)))
            ready.append(errs[q])
        stages = [c - 2] if step < steps - 1 else [c - 2, c - 1, c] if step < steps else [c]
        for c in stages:
            if c < 0:
                continue
            q = order[c]
            added = call(
                add_kernel, [f32(rows // 2, lats)], gives[c], after=sent if step < steps else ()
            )[0]
            gacts.append(across(added, q) if q else added)
            ready.append(added)
        if step + 1 < steps:
            waits[step + 1] += ready
        ready_before = ready

    loss, gap = loss[0], 1
    while gap < n_lat:
        other = lax.ppermute(loss, "lat", [(p, p ^ gap) for p in range(n_lat)])
        loss = call(add_kernel, [f32(LOSS_ROWS, BLOCK)], (loss, other))[0]
        gap *= 2

    g_pre = call(
        g_pre_kernel, [f32(rows // 2 + LOSS_ROWS, lats)], (pre, mask, loss, *gacts)
    )[0]
    mine = [across(g_pre, q) if q else g_pre for q in range(n_tok)]
    others = [swap(g) for g in mine]
    decoded = call(
        decode_kernel,
        [f32(width, lats)],
        (*[errs[q] for q in order], *[acts[q] for q in order]),
    )[0]
    grad, losses = call(
        functools.partial(encode_kernel, 1.0 / (rows * n_tok * half * n_wid)),
        [bf16(width, lats), f32(LEVELS)],
        (*resids, *mine, *others, decoded),
        out_specs=[VMEM, SMEM],
    )
    return (losses, grad)


def solution(mesh):
    return jax.shard_map(
        body,
        mesh=mesh,
        in_specs=(P("tok", "wid"), P("lat", "wid"), P("lat"), P("wid"), P("tok", None), P()),
        out_specs=(P(), P(("wid", "tok"), "lat")),
        check_vma=False,
    )
```

```python
import functools

import jax
import jax.numpy as jnp
from jax import lax
from jax.experimental import pallas as pl
from jax.experimental.pallas import tpu as pltpu
from jax.sharding import PartitionSpec as P

LEVELS = 4
BLOCK = 128
LOSS_ROWS = 8
LOSS_PART = 4
GELU_C = 0.7978845608028654
GELU_A = 0.044715

VMEM = pl.BlockSpec(memory_space=pltpu.VMEM)
SMEM = pl.BlockSpec(memory_space=pltpu.SMEM)
HBM = pl.BlockSpec(memory_space=pltpu.HBM)
ANY = pl.BlockSpec(memory_space=pl.ANY)


def f32(*shape):
    return jax.ShapeDtypeStruct(shape, jnp.float32)


def bf16(*shape):
    return jax.ShapeDtypeStruct(shape, jnp.bfloat16)


def call(kernel, outs, arrays, after=(), specs=None, out_specs=None, scratch=()):
    skip = slice(len(arrays), len(arrays) + len(after))

    def run(*refs):
        kernel(*refs[: skip.start], *refs[skip.stop :])

    return pl.pallas_call(
        run,
        out_shape=outs,
        in_specs=list(specs or [VMEM] * len(arrays)) + [ANY] * len(after),
        out_specs=out_specs or [VMEM] * len(outs),
        scratch_shapes=list(scratch),
        compiler_params=pltpu.CompilerParams(vmem_limit_bytes=12 * 1024 * 1024),
        cost_estimate=pl.CostEstimate(flops=0, bytes_accessed=1 << 10, transcendentals=0),
    )(*arrays, *after)


def in_hbm(array):
    return pltpu.with_memory_space_constraint(array, pltpu.HBM)


def total_of(terms):
    return functools.reduce(jnp.add, terms)


def place_in_chain():
    lat = lax.axis_index("lat")
    return jnp.where(lax.axis_index("wid") == 0, lat, lax.axis_size("lat") - 1 - lat)


def level_table(bounds, count, out):
    lasts = bounds[...] - 1 - lax.axis_index("lat") * count
    upward = lax.axis_index("wid") == 0

    def put(row, value):
        out[row : row + 1, :] = jnp.broadcast_to(value, (1, BLOCK))

    for i in range(count):
        hits = (jnp.minimum(lasts, count - 1) == i).astype(jnp.float32)
        ending = jnp.sum(hits, axis=1, keepdims=True)
        put(i, ending)
        put(count + i, jnp.where(upward, jnp.full_like(ending, float(i == count - 1)), ending))
    for m in range(LEVELS):
        for i in range(count):
            put((2 + m) * count + i, (lasts[:, m : m + 1] == i).astype(jnp.float32))


def pre_kernel(resid, dictionary, partial_out, dict_out, resid_v, dict_v, sems):
    pieces, _, width = dict_v.shape
    copies = []
    for i in range(pieces):
        cols = pl.ds(i * width, width)
        copies.append(
            (
                pltpu.make_async_copy(resid.at[:, cols], resid_v.at[i], sems.at[0, i]),
                pltpu.make_async_copy(dictionary.at[:, cols], dict_v.at[i], sems.at[1, i]),
            )
        )
        for copy in copies[-1]:
            copy.start()
    total = None
    for i in range(pieces):
        for copy in copies[i]:
            copy.wait()
        term = lax.dot_general(
            dict_v[i], resid_v[i], (((1,), (1,)), ((), ())), preferred_element_type=jnp.float32
        )
        total = term if total is None else total + term
    partial_out[...] = total.T
    parts = dict_out.shape[1] // width
    for i in range(parts):
        dict_out[:, i * width : (i + 1) * width] = dict_v[lax.axis_index("tok") * parts + i]


def widen_kernel(array, bounds, out, table_out):
    out[...] = array[...].astype(jnp.float32)
    level_table(bounds, array.shape[0] // BLOCK, table_out)


def pieces_kernel(resid, bias, bias_out, *outs):
    width = outs[0].shape[1]
    tok = lax.axis_index("tok")

    def cols(t):
        return pl.ds(pl.multiple_of(t * width, width), width)

    bias_out[...] = bias[:, cols(tok)]
    for q, out in enumerate(outs):
        out[...] = resid[:, cols(tok ^ q)].astype(jnp.float32)


def block_mask(active, lats):
    count = lats // BLOCK
    ids = lax.axis_index("lat") * count + lax.broadcasted_iota(jnp.int32, (count, 1), 0)
    hits = total_of([(active[q : q + 1, :] == ids).astype(jnp.float32) for q in range(active.shape[0])])
    spread = lax.broadcasted_iota(jnp.int32, (count, lats), 1) // BLOCK
    spread = (spread == lax.broadcasted_iota(jnp.int32, (count, lats), 0)).astype(jnp.bfloat16)
    return lax.dot_general(
        hits.astype(jnp.bfloat16),
        spread,
        (((0,), (0,)), ((), ())),
        preferred_element_type=jnp.float32,
    )


def activate_kernel(mine, other, bias, active, pre_out, act_out, mask_out):
    pre = mine[...] + other[...] + bias[...]
    pre_out[...] = pre
    inner = GELU_C * (pre + GELU_A * (pre * pre * pre))
    gelu = 0.5 * pre * (1.0 + jnp.tanh(inner))
    mask = block_mask(active[...], pre.shape[1])
    mask_out[...] = mask
    act_out[...] = jnp.where(mask > 0.0, gelu, 0.0)


def half_of(wid, rows):
    return pl.ds(pl.multiple_of(wid * (rows // 2), rows // 2), rows // 2)


def g_pre_kernel(pre_ref, mask, loss, *refs):
    terms, out = refs[:-1], refs[-1]
    mine = half_of(lax.axis_index("wid"), pre_ref.shape[0])
    pre = pre_ref[mine, :]
    inner = GELU_C * (pre + GELU_A * (pre * pre * pre))
    slope = GELU_C * (1.0 + 3.0 * GELU_A * (pre * pre))
    bend = jnp.tanh(inner)
    deriv = 0.5 * (1.0 + bend) + 0.5 * pre * (1.0 - bend * bend) * slope
    hit = mask[mine, :] > 0.0
    rows = pre.shape[0]
    out[:rows, :] = jnp.where(hit, deriv * total_of([t[...] for t in terms]), 0.0)
    out[rows:, :] = jnp.zeros_like(out[rows:, :])
    out[rows:, :BLOCK] = loss[:LOSS_ROWS, :BLOCK]


def running_parts(act, dict_ref):
    sums = []
    for i in range(dict_ref.shape[0] // BLOCK):
        span = slice(i * BLOCK, (i + 1) * BLOCK)
        part = jnp.dot(
            act[:, span], dict_ref[span, :].astype(jnp.bfloat16), preferred_element_type=jnp.float32
        )
        sums.append(sums[-1] + part if sums else part)
    return sums


def round_kernel(act, out):
    out[...] = act[...].astype(jnp.bfloat16)


def project_kernel(act, table, *refs):
    dicts, out = refs[:-1], refs[-1]
    for side, dictionary in enumerate(dicts):
        sums = running_parts(act[...], dictionary)
        count = len(sums)
        width = dictionary.shape[1]
        out[:, side * width : (side + 1) * width] = total_of(
            [table[count + i : count + i + 1, :1] * s for i, s in enumerate(sums)]
        )


def columns(ref, col, width):
    return ref[:, col * width : (col + 1) * width]


def message_kernel(places, cols, got, *refs):
    out = refs[-1]
    width = out.shape[1]
    index = place_in_chain()
    for place, piece, col in zip(places, refs[:-1], cols[1:]):

        @pl.when(index == place)
        def _():
            own = columns(piece, col, width)
            out[...] = own + columns(got, cols[0], width) if place else own


def choose_kernel(places, cols, *refs):
    arrived, out = refs[:-1], refs[-1]
    index = place_in_chain()

    @pl.when(index == 0)
    def _():
        out[...] = jnp.zeros_like(out)

    for place, ref, col in zip(places, arrived, cols):

        @pl.when(index == place if len(arrived) > 1 else index > 0)
        def _():
            out[...] = columns(ref, col, out.shape[1])


def square_sums(table, shifted):
    count = len(shifted)
    squares = []
    for v in shifted:
        lanes = jnp.sum(v * v, axis=0, keepdims=True)
        squares.append(total_of([lanes[:, i : i + BLOCK] for i in range(0, lanes.shape[1], BLOCK)]))
    rows = []
    for m in range(LEVELS):
        at = (2 + m) * count
        rows.append(total_of([table[at + i : at + i + 1, :] * s for i, s in enumerate(squares)]))
    return jnp.concatenate(rows + [jnp.zeros((LOSS_ROWS - LEVELS, BLOCK), jnp.float32)], axis=0)


def error_kernel(act, dictionary, resid, bias, table, mine, other, *refs):
    before, (err_out, keep_out, give_out, loss_out) = refs[:-4], refs[-4:]
    upward = lax.axis_index("wid") == 0
    earlier = jnp.where(upward, mine[...], other[...])
    later = jnp.where(upward, other[...], mine[...])
    base = bias[...] - resid[...] + earlier
    sums = running_parts(act[...], dictionary)
    shifted = [base + s for s in sums]
    loss_out[...] = total_of([square_sums(table, shifted)] + [b[...] for b in before])
    err = later
    for i in reversed(range(len(sums))):
        err = err + table[i : i + 1, :1] * shifted[i]
        rounded = err.astype(jnp.bfloat16)
        err_out[i] = rounded
        cols = slice(i * BLOCK, (i + 1) * BLOCK)
        gact = lax.dot_general(
            rounded,
            dictionary[cols, :],
            (((1,), (1,)), ((), ())),
            preferred_element_type=jnp.float32,
        )
        half = gact.shape[0] // 2
        keep_out[:, cols] = jnp.where(upward, gact[:half, :], gact[half:, :])
        give_out[:, cols] = jnp.where(upward, gact[half:, :], gact[:half, :])


def spread_kernel(loss, out):
    out[...] = jnp.zeros_like(out)
    out[:LOSS_ROWS, :BLOCK] = loss[...]


def add_kernel(*refs):
    refs[-1][...] = total_of([ref[...] for ref in refs[:-1]])


def decode_kernel(*refs):
    n = (len(refs) - 1) // 2
    errs, acts, out = refs[:n], refs[n : 2 * n], refs[-1]
    for i in range(errs[0].shape[0]):
        cols = slice(i * BLOCK, (i + 1) * BLOCK)
        err = jnp.concatenate([e[i] for e in errs], axis=0)
        act = jnp.concatenate([a[:, cols] for a in acts], axis=0)
        out[:, cols] = lax.dot_general(
            err, act, (((0,), (0,)), ((), ())), preferred_element_type=jnp.float32
        )


def encode_kernel(scale, *refs):
    n = (len(refs) - 3) // 3
    resids, grads, base, out, loss_out = refs[:n], refs[n : 3 * n], refs[-3], refs[-2], refs[-1]
    rows = resids[0].shape[0]
    wid = lax.axis_index("wid")
    halves = [half_of(wid, rows), half_of(1 - wid, rows)]
    resid = jnp.concatenate([r[h, :].astype(jnp.bfloat16) for h in halves for r in resids], axis=0)
    grad = jnp.concatenate([g[: rows // 2, :].astype(jnp.bfloat16) for g in grads], axis=0)
    total = base[...] + lax.dot_general(
        resid, grad, (((0,), (0,)), ((), ())), preferred_element_type=jnp.float32
    )
    out[...] = total.astype(jnp.bfloat16)
    lanes = total_of([g[rows // 2 :, :BLOCK] for g in grads])
    for m in range(LEVELS):
        loss_out[m] = jnp.sum(lanes[m : m + 1, :]) * scale


def pick(index, choices):
    values = sorted(choices)
    result = choices[values[0]]
    for value in values[1:]:
        result = jnp.where(index == value, choices[value], result)
    return result


def body(resid, dictionary, enc_bias, dec_bias, active_blocks, level_bounds):
    rows, half = resid.shape
    lats = dictionary.shape[0]
    n_lat, n_wid, n_tok = lax.axis_size("lat"), lax.axis_size("wid"), lax.axis_size("tok")
    width = half // n_tok
    count = lats // BLOCK

    def across(array, q):
        return lax.ppermute(array, "tok", [(t, t ^ q) for t in range(n_tok)])

    def swap(array):
        return lax.ppermute(array, "wid", [(w, w ^ 1) for w in range(n_wid)])

    partial, dict_here = call(
        pre_kernel,
        [f32(rows, lats), bf16(lats, width)],
        (in_hbm(resid), in_hbm(dictionary)),
        specs=[HBM, HBM],
        scratch=[
            pltpu.VMEM((2 * n_tok, rows, width // 2), jnp.bfloat16),
            pltpu.VMEM((2 * n_tok, lats, width // 2), jnp.bfloat16),
            pltpu.SemaphoreType.DMA((2, 2 * n_tok)),
        ],
    )
    partial_other = swap(partial)
    dict_wide, table = call(
        widen_kernel,
        [f32(lats, width), f32((2 + LEVELS) * count, BLOCK)],
        (dict_here, level_bounds.reshape(1, LEVELS)),
        after=(partial_other,),
    )
    dict_other = swap(dict_wide)
    pre, act, mask = call(
        activate_kernel,
        [f32(rows, lats)] * 3,
        (partial, partial_other, enc_bias.reshape(1, lats), active_blocks.T),
        after=(dict_wide,),
    )
    gathered = [act] + [across(act, q) for q in range(1, n_tok)]
    bias_here, *pieces = call(
        pieces_kernel,
        [f32(1, width)] + [f32(rows, width)] * n_tok,
        (resid, dec_bias.reshape(1, half)),
        after=(act,),
    )
    resids = [piece if q == 0 else across(piece, q) for q, piece in enumerate(pieces)]

    order = [0, 1, 3, 2] if n_tok == 4 else list(range(n_tok))
    steps = n_tok + n_lat - 2
    places = list(range(1, n_lat))
    acts, errs, hands, gives, gacts, loss = {}, {}, [], [], [], ()
    sums, got, sent = ([], []), ([], []), []
    waits = {step: [] for step in range(steps)}
    for place, q in enumerate(order[1:]):
        waits[min(3 + place, steps - 1)].append(resids[q])

    def project(q, dicts):
        shape = [f32(rows, width * len(dicts))]
        return call(project_kernel, shape, (acts[q], table, *dicts))[0]

    for step in range(steps + 1):
        at = [p for p in range(n_lat - 1) if 0 <= step - p < n_tok]
        pairs = []
        for p in at:
            pairs.append((2 * p, 2 * (p + 1)))
            pairs.append((2 * (n_lat - 1 - p) + 1, 2 * (n_lat - 2 - p) + 1))
        if step == 0:
            acts[order[0]] = call(round_kernel, [bf16(rows, lats)], (act,))[0]
            for side, dict_ref in enumerate((dict_here, dict_other)):
                message = project(order[0], (dict_ref,))
                sums[side].append((message, 0))
                got[side].append((lax.ppermute(message, ("lat", "wid"), pairs), 0))
                sent = [message]
        elif step < steps:
            for side in range(2):
                items = [got[side][-1], *[sums[side][step - p] for p in at]]
                message = call(
                    functools.partial(message_kernel, at, [col for _, col in items]),
                    [f32(rows, width)],
                    [array for array, _ in items],
                    after=sent + (waits[step] if side == 0 else []) if step > 1 else (),
                )[0]
                got[side].append((lax.ppermute(message, ("lat", "wid"), pairs), 0))
                sent = [message]
        if step + 1 < n_tok:
            q = order[step + 1]
            acts[q] = call(round_kernel, [bf16(rows, lats)], (gathered[q],), after=sent)[0]
            for side, dict_ref in enumerate((dict_here, dict_other)):
                sums[side].append((project(q, (dict_ref,)), 0))
        ready = []
        c = step - (n_lat - 1)
        if c >= 0:
            chosen = []
            for side in (1, 0) if step < steps else (0, 1):
                items = [got[side][c + p - 1] for p in places]
                if n_lat > 4:
                    items = [a[:, col * width : (col + 1) * width] for a, col in items]
                    items = [(pick(place_in_chain(), dict(zip(places, items))), 0)]
                chosen.append(
                    call(
                        functools.partial(choose_kernel, places, [col for _, col in items]),
                        [f32(rows, width)],
                        [array for array, _ in items],
                        after=sent if step < steps else ready_before + chosen,
                    )[0]
                )
            hand, mine = chosen if step < steps else chosen[::-1]
            hands.append((swap(hand), mine))
            ready += chosen
        stages = [c - 1] if step < steps else [c - 1, c]
        for c in stages:
            if c < 0:
                continue
            q = order[c]
            errs[q], keep, give, loss_here = call(
                error_kernel,
                [bf16(count, rows, width)] + [f32(rows // 2, lats)] * 2 + [f32(LOSS_ROWS, BLOCK)],
                (acts[q], dict_here, resids[q], bias_here, table, hands[c][1], hands[c][0], *loss),
                after=sent if step < steps else (),
            )
            loss = (loss_here,)
            gives.append((keep, swap(give)))
            ready.append(errs[q])
        stages = range(n_tok) if step == steps else []
        for c in stages:
            if c < 0:
                continue
            q = order[c]
            added = call(
                add_kernel, [f32(rows // 2, lats)], gives[c], after=sent if step < steps else ()
            )[0]
            gacts.append(across(added, q) if q else added)
            ready.append(added)
        if step + 1 < steps:
            waits[step + 1] += ready
        ready_before = ready

    loss, gap = call(spread_kernel, [f32(rows // LOSS_PART, lats)], loss)[0], 1
    while gap < n_lat:
        other = lax.ppermute(loss, "lat", [(p, p ^ gap) for p in range(n_lat)])
        loss = call(add_kernel, [f32(*loss.shape)], (loss, other))[0]
        gap *= 2

    g_pre = call(
        g_pre_kernel, [f32(rows // 2 + LOSS_ROWS, lats)], (pre, mask, loss, *gacts)
    )[0]
    mine = [across(g_pre, q) if q else g_pre for q in range(n_tok)]
    others = [swap(g) for g in mine]
    decoded = call(
        decode_kernel,
        [f32(width, lats)],
        (*[errs[q] for q in order], *[acts[q] for q in order]),
    )[0]
    grad, losses = call(
        functools.partial(encode_kernel, 1.0 / (rows * n_tok * half * n_wid)),
        [bf16(width, lats), f32(LEVELS)],
        (*resids, *mine, *others, decoded),
        out_specs=[VMEM, SMEM],
    )
    return (losses, grad)


def solution(mesh):
    return jax.shard_map(
        body,
        mesh=mesh,
        in_specs=(P("tok", "wid"), P("lat", "wid"), P("lat"), P("wid"), P("tok", None), P()),
        out_specs=(P(), P(("wid", "tok"), "lat")),
        check_vma=False,
    )
```

```python
import functools

import jax
import jax.numpy as jnp
from jax import lax
from jax.experimental import pallas as pl
from jax.experimental.pallas import tpu as pltpu
from jax.sharding import PartitionSpec as P

LEVELS = 4
BLOCK = 128
LOSS_ROWS = 8
LOSS_PART = 4
GELU_C = 0.7978845608028654
GELU_A = 0.044715

VMEM = pl.BlockSpec(memory_space=pltpu.VMEM)
SMEM = pl.BlockSpec(memory_space=pltpu.SMEM)
HBM = pl.BlockSpec(memory_space=pltpu.HBM)
ANY = pl.BlockSpec(memory_space=pl.ANY)


def f32(*shape):
    return jax.ShapeDtypeStruct(shape, jnp.float32)


def bf16(*shape):
    return jax.ShapeDtypeStruct(shape, jnp.bfloat16)


def call(kernel, outs, arrays, after=(), specs=None, out_specs=None, scratch=()):
    skip = slice(len(arrays), len(arrays) + len(after))

    def run(*refs):
        kernel(*refs[: skip.start], *refs[skip.stop :])

    return pl.pallas_call(
        run,
        out_shape=outs,
        in_specs=list(specs or [VMEM] * len(arrays)) + [ANY] * len(after),
        out_specs=out_specs or [VMEM] * len(outs),
        scratch_shapes=list(scratch),
        compiler_params=pltpu.CompilerParams(vmem_limit_bytes=12 * 1024 * 1024),
        cost_estimate=pl.CostEstimate(flops=0, bytes_accessed=1 << 10, transcendentals=0),
    )(*arrays, *after)


def in_hbm(array):
    return pltpu.with_memory_space_constraint(array, pltpu.HBM)


def total_of(terms):
    return functools.reduce(jnp.add, terms)


def place_in_chain():
    lat = lax.axis_index("lat")
    return jnp.where(lax.axis_index("wid") == 0, lat, lax.axis_size("lat") - 1 - lat)


def level_table(bounds, count, out):
    lasts = bounds[...] - 1 - lax.axis_index("lat") * count
    upward = lax.axis_index("wid") == 0

    def put(row, value):
        out[row : row + 1, :] = jnp.broadcast_to(value, (1, BLOCK))

    for i in range(count):
        hits = (jnp.minimum(lasts, count - 1) == i).astype(jnp.float32)
        ending = jnp.sum(hits, axis=1, keepdims=True)
        put(i, ending)
        put(count + i, jnp.where(upward, jnp.full_like(ending, float(i == count - 1)), ending))
    for m in range(LEVELS):
        for i in range(count):
            put((2 + m) * count + i, (lasts[:, m : m + 1] == i).astype(jnp.float32))


def pre_kernel(resid, dictionary, partial_out, dict_out, resid_v, dict_v, sems):
    pieces, _, width = dict_v.shape
    copies = []
    for i in range(pieces):
        cols = pl.ds(i * width, width)
        copies.append(
            (
                pltpu.make_async_copy(resid.at[:, cols], resid_v.at[i], sems.at[0, i]),
                pltpu.make_async_copy(dictionary.at[:, cols], dict_v.at[i], sems.at[1, i]),
            )
        )
        for copy in copies[-1]:
            copy.start()
    total = None
    for i in range(pieces):
        for copy in copies[i]:
            copy.wait()
        term = lax.dot_general(
            dict_v[i], resid_v[i], (((1,), (1,)), ((), ())), preferred_element_type=jnp.float32
        )
        total = term if total is None else total + term
    partial_out[...] = total.T
    parts = dict_out.shape[1] // width
    for i in range(parts):
        dict_out[:, i * width : (i + 1) * width] = dict_v[lax.axis_index("tok") * parts + i]


def widen_kernel(array, bounds, out, table_out):
    out[...] = array[...].astype(jnp.float32)
    level_table(bounds, array.shape[0] // BLOCK, table_out)


def pieces_kernel(resid, bias, bias_out, *outs):
    width = outs[0].shape[1]
    tok = lax.axis_index("tok")

    def cols(t):
        return pl.ds(pl.multiple_of(t * width, width), width)

    bias_out[...] = bias[:, cols(tok)]
    for q, out in enumerate(outs):
        out[...] = resid[:, cols(tok ^ q)].astype(jnp.float32)


def block_mask(active, lats):
    count = lats // BLOCK
    ids = lax.axis_index("lat") * count + lax.broadcasted_iota(jnp.int32, (count, 1), 0)
    hits = total_of([(active[q : q + 1, :] == ids).astype(jnp.float32) for q in range(active.shape[0])])
    spread = lax.broadcasted_iota(jnp.int32, (count, lats), 1) // BLOCK
    spread = (spread == lax.broadcasted_iota(jnp.int32, (count, lats), 0)).astype(jnp.bfloat16)
    return lax.dot_general(
        hits.astype(jnp.bfloat16),
        spread,
        (((0,), (0,)), ((), ())),
        preferred_element_type=jnp.float32,
    )


def activate_kernel(mine, other, bias, active, pre_out, act_out, mask_out):
    pre = mine[...] + other[...] + bias[...]
    pre_out[...] = pre
    inner = GELU_C * (pre + GELU_A * (pre * pre * pre))
    gelu = 0.5 * pre * (1.0 + jnp.tanh(inner))
    mask = block_mask(active[...], pre.shape[1])
    mask_out[...] = mask
    act_out[...] = jnp.where(mask > 0.0, gelu, 0.0)


def half_of(wid, rows):
    return pl.ds(pl.multiple_of(wid * (rows // 2), rows // 2), rows // 2)


def g_pre_kernel(pre_ref, mask, loss, *refs):
    terms, out = refs[:-1], refs[-1]
    mine = half_of(lax.axis_index("wid"), pre_ref.shape[0])
    pre = pre_ref[mine, :]
    inner = GELU_C * (pre + GELU_A * (pre * pre * pre))
    slope = GELU_C * (1.0 + 3.0 * GELU_A * (pre * pre))
    bend = jnp.tanh(inner)
    deriv = 0.5 * (1.0 + bend) + 0.5 * pre * (1.0 - bend * bend) * slope
    hit = mask[mine, :] > 0.0
    rows = pre.shape[0]
    out[:rows, :] = jnp.where(hit, deriv * total_of([t[...] for t in terms]), 0.0)
    out[rows:, :] = jnp.zeros_like(out[rows:, :])
    out[rows:, :BLOCK] = loss[:LOSS_ROWS, :BLOCK]


def running_parts(act, dict_ref):
    sums = []
    for i in range(dict_ref.shape[0] // BLOCK):
        span = slice(i * BLOCK, (i + 1) * BLOCK)
        part = jnp.dot(
            act[:, span], dict_ref[span, :].astype(jnp.bfloat16), preferred_element_type=jnp.float32
        )
        sums.append(sums[-1] + part if sums else part)
    return sums


def round_kernel(act, out):
    out[...] = act[...].astype(jnp.bfloat16)


def project_kernel(act, table, *refs):
    dicts, out = refs[:-1], refs[-1]
    for side, dictionary in enumerate(dicts):
        sums = running_parts(act[...], dictionary)
        count = len(sums)
        width = dictionary.shape[1]
        out[:, side * width : (side + 1) * width] = total_of(
            [table[count + i : count + i + 1, :1] * s for i, s in enumerate(sums)]
        )


def columns(ref, col, width):
    return ref[:, col * width : (col + 1) * width]


def message_kernel(places, cols, got, *refs):
    out = refs[-1]
    width = out.shape[1]
    index = place_in_chain()
    for place, piece, col in zip(places, refs[:-1], cols[1:]):

        @pl.when(index == place)
        def _():
            own = columns(piece, col, width)
            out[...] = own + columns(got, cols[0], width) if place else own


def choose_kernel(places, cols, *refs):
    arrived, out = refs[:-1], refs[-1]
    index = place_in_chain()

    @pl.when(index == 0)
    def _():
        out[...] = jnp.zeros_like(out)

    for place, ref, col in zip(places, arrived, cols):

        @pl.when(index == place if len(arrived) > 1 else index > 0)
        def _():
            out[...] = columns(ref, col, out.shape[1])


def square_sums(table, shifted):
    count = len(shifted)
    squares = []
    for v in shifted:
        lanes = jnp.sum(v * v, axis=0, keepdims=True)
        squares.append(total_of([lanes[:, i : i + BLOCK] for i in range(0, lanes.shape[1], BLOCK)]))
    rows = []
    for m in range(LEVELS):
        at = (2 + m) * count
        rows.append(total_of([table[at + i : at + i + 1, :] * s for i, s in enumerate(squares)]))
    return jnp.concatenate(rows + [jnp.zeros((LOSS_ROWS - LEVELS, BLOCK), jnp.float32)], axis=0)


def error_kernel(act, dictionary, resid, bias, table, mine, other, *refs):
    before, (err_out, keep_out, give_out, loss_out) = refs[:-4], refs[-4:]
    upward = lax.axis_index("wid") == 0
    earlier = jnp.where(upward, mine[...], other[...])
    later = jnp.where(upward, other[...], mine[...])
    base = bias[...] - resid[...] + earlier
    sums = running_parts(act[...], dictionary)
    shifted = [base + s for s in sums]
    loss_out[...] = total_of([square_sums(table, shifted)] + [b[...] for b in before])
    err = later
    for i in reversed(range(len(sums))):
        err = err + table[i : i + 1, :1] * shifted[i]
        rounded = err.astype(jnp.bfloat16)
        err_out[i] = rounded
        cols = slice(i * BLOCK, (i + 1) * BLOCK)
        gact = lax.dot_general(
            rounded,
            dictionary[cols, :],
            (((1,), (1,)), ((), ())),
            preferred_element_type=jnp.float32,
        )
        half = gact.shape[0] // 2
        keep_out[:, cols] = jnp.where(upward, gact[:half, :], gact[half:, :])
        give_out[:, cols] = jnp.where(upward, gact[half:, :], gact[:half, :])


def spread_kernel(loss, out):
    out[...] = jnp.zeros_like(out)
    out[:LOSS_ROWS, :BLOCK] = loss[...]


def add_kernel(*refs):
    refs[-1][...] = total_of([ref[...] for ref in refs[:-1]])


def decode_kernel(*refs):
    n = (len(refs) - 1) // 2
    errs, acts, out = refs[:n], refs[n : 2 * n], refs[-1]
    for i in range(errs[0].shape[0]):
        cols = slice(i * BLOCK, (i + 1) * BLOCK)
        err = jnp.concatenate([e[i] for e in errs], axis=0)
        act = jnp.concatenate([a[:, cols] for a in acts], axis=0)
        out[:, cols] = lax.dot_general(
            err, act, (((0,), (0,)), ((), ())), preferred_element_type=jnp.float32
        )


def encode_kernel(scale, *refs):
    n = (len(refs) - 3) // 3
    resids, grads, base, out, loss_out = refs[:n], refs[n : 3 * n], refs[-3], refs[-2], refs[-1]
    rows = resids[0].shape[0]
    wid = lax.axis_index("wid")
    halves = [half_of(wid, rows), half_of(1 - wid, rows)]
    resid = jnp.concatenate([r[h, :].astype(jnp.bfloat16) for h in halves for r in resids], axis=0)
    grad = jnp.concatenate([g[: rows // 2, :].astype(jnp.bfloat16) for g in grads], axis=0)
    total = base[...] + lax.dot_general(
        resid, grad, (((0,), (0,)), ((), ())), preferred_element_type=jnp.float32
    )
    out[...] = total.astype(jnp.bfloat16)
    lanes = total_of([g[rows // 2 :, :BLOCK] for g in grads])
    for m in range(LEVELS):
        loss_out[m] = jnp.sum(lanes[m : m + 1, :]) * scale


def pick(index, choices):
    values = sorted(choices)
    result = choices[values[0]]
    for value in values[1:]:
        result = jnp.where(index == value, choices[value], result)
    return result


def body(resid, dictionary, enc_bias, dec_bias, active_blocks, level_bounds):
    rows, half = resid.shape
    lats = dictionary.shape[0]
    n_lat, n_wid, n_tok = lax.axis_size("lat"), lax.axis_size("wid"), lax.axis_size("tok")
    width = half // n_tok
    count = lats // BLOCK

    def across(array, q):
        return lax.ppermute(array, "tok", [(t, t ^ q) for t in range(n_tok)])

    def swap(array):
        return lax.ppermute(array, "wid", [(w, w ^ 1) for w in range(n_wid)])

    partial, dict_here = call(
        pre_kernel,
        [f32(rows, lats), bf16(lats, width)],
        (in_hbm(resid), in_hbm(dictionary)),
        specs=[HBM, HBM],
        scratch=[
            pltpu.VMEM((2 * n_tok, rows, width // 2), jnp.bfloat16),
            pltpu.VMEM((2 * n_tok, lats, width // 2), jnp.bfloat16),
            pltpu.SemaphoreType.DMA((2, 2 * n_tok)),
        ],
    )
    partial_other = swap(partial)
    dict_wide, table = call(
        widen_kernel,
        [f32(lats, width), f32((2 + LEVELS) * count, BLOCK)],
        (dict_here, level_bounds.reshape(1, LEVELS)),
        after=(partial_other,),
    )
    dict_other = swap(dict_wide)
    pre, act, mask = call(
        activate_kernel,
        [f32(rows, lats)] * 3,
        (partial, partial_other, enc_bias.reshape(1, lats), active_blocks.T),
        after=(dict_wide,),
    )
    gathered = [act] + [across(act, q) for q in range(1, n_tok)]
    bias_here, *pieces = call(
        pieces_kernel,
        [f32(1, width)] + [f32(rows, width)] * n_tok,
        (resid, dec_bias.reshape(1, half)),
        after=(act,),
    )
    resids = [piece if q == 0 else across(piece, q) for q, piece in enumerate(pieces)]

    order = [0, 1, 3, 2] if n_tok == 4 else list(range(n_tok))
    steps = n_tok + n_lat - 2
    places = list(range(1, n_lat))
    acts, errs, hands, gives, gacts, loss = {}, {}, [], [], [], ()
    sums, got, sent = ([], []), ([], []), []
    waits = {step: [] for step in range(steps)}
    for place, q in enumerate(order[1:]):
        waits[min(3 + place, steps - 1)].append(resids[q])

    def project(q, dicts):
        shape = [f32(rows, width * len(dicts))]
        return call(project_kernel, shape, (acts[q], table, *dicts))[0]

    for step in range(steps + 1):
        at = [p for p in range(n_lat - 1) if 0 <= step - p < n_tok]
        pairs = []
        for p in at:
            pairs.append((2 * p, 2 * (p + 1)))
            pairs.append((2 * (n_lat - 1 - p) + 1, 2 * (n_lat - 2 - p) + 1))
        if step == 0:
            acts[order[0]] = call(round_kernel, [bf16(rows, lats)], (act,))[0]
            for side, dict_ref in enumerate((dict_here, dict_other)):
                message = project(order[0], (dict_ref,))
                sums[side].append((message, 0))
                got[side].append((lax.ppermute(message, ("lat", "wid"), pairs), 0))
                sent = [message]
        elif step < steps:
            for side in range(2):
                items = [got[side][-1], *[sums[side][step - p] for p in at]]
                message = call(
                    functools.partial(message_kernel, at, [col for _, col in items]),
                    [f32(rows, width)],
                    [array for array, _ in items],
                    after=sent + (waits[step] if side == 0 else []) if step > 1 else (),
                )[0]
                got[side].append((lax.ppermute(message, ("lat", "wid"), pairs), 0))
                sent = [message]
        if step + 1 < n_tok:
            q = order[step + 1]
            acts[q] = call(round_kernel, [bf16(rows, lats)], (gathered[q],), after=sent)[0]
            for side, dict_ref in enumerate((dict_here, dict_other)):
                sums[side].append((project(q, (dict_ref,)), 0))
        ready = []
        c = step - (n_lat - 1)
        if c >= 0:
            chosen = []
            for side in (1, 0) if step < steps else (0, 1):
                items = [got[side][c + p - 1] for p in places]
                if n_lat > 4:
                    items = [a[:, col * width : (col + 1) * width] for a, col in items]
                    items = [(pick(place_in_chain(), dict(zip(places, items))), 0)]
                chosen.append(
                    call(
                        functools.partial(choose_kernel, places, [col for _, col in items]),
                        [f32(rows, width)],
                        [array for array, _ in items],
                        after=sent if step < steps else ready_before + chosen,
                    )[0]
                )
            hand, mine = chosen if step < steps else chosen[::-1]
            hands.append((swap(hand), mine))
            ready += chosen
        stages = [c - 1] if step < steps else [c - 1, c]
        for c in stages:
            if c < 0:
                continue
            q = order[c]
            errs[q], keep, give, loss_here = call(
                error_kernel,
                [bf16(count, rows, width)] + [f32(rows // 2, lats)] * 2 + [f32(LOSS_ROWS, BLOCK)],
                (acts[q], dict_here, resids[q], bias_here, table, hands[c][1], hands[c][0], *loss),
                after=sent if step < steps else (),
            )
            loss = (loss_here,)
            gives.append((keep, swap(give)))
            ready.append(errs[q])
        stages = [1] if step == steps - 1 else [0, *range(2, n_tok)] if step == steps else []
        for c in stages:
            if c < 0:
                continue
            q = order[c]
            added = call(
                add_kernel, [f32(rows // 2, lats)], gives[c], after=sent if step < steps else ()
            )[0]
            gacts.append(across(added, q) if q else added)
            ready.append(added)
        if step + 1 < steps:
            waits[step + 1] += ready
        ready_before = ready

    loss, gap = call(spread_kernel, [f32(rows // LOSS_PART, lats)], loss)[0], 1
    while gap < n_lat:
        other = lax.ppermute(loss, "lat", [(p, p ^ gap) for p in range(n_lat)])
        loss = call(add_kernel, [f32(*loss.shape)], (loss, other))[0]
        gap *= 2

    decoded = call(
        decode_kernel,
        [f32(width, lats)],
        (*[errs[q] for q in order], *[acts[q] for q in order]),
    )[0]
    g_pre = call(
        g_pre_kernel,
        [f32(rows // 2 + LOSS_ROWS, lats)],
        (pre, mask, loss, *gacts),
        after=(decoded,),
    )[0]
    mine = [across(g_pre, q) if q else g_pre for q in range(n_tok)]
    others = [swap(g) for g in mine]
    grad, losses = call(
        functools.partial(encode_kernel, 1.0 / (rows * n_tok * half * n_wid)),
        [bf16(width, lats), f32(LEVELS)],
        (*resids, *mine, *others, decoded),
        out_specs=[VMEM, SMEM],
    )
    return (losses, grad)


def solution(mesh):
    return jax.shard_map(
        body,
        mesh=mesh,
        in_specs=(P("tok", "wid"), P("lat", "wid"), P("lat"), P("wid"), P("tok", None), P()),
        out_specs=(P(), P(("wid", "tok"), "lat")),
        check_vma=False,
    )
```

```python
import functools

import jax
import jax.numpy as jnp
from jax import lax
from jax.experimental import pallas as pl
from jax.experimental.pallas import tpu as pltpu
from jax.sharding import PartitionSpec as P

LEVELS = 4
BLOCK = 128
LOSS_ROWS = 8
LOSS_PART = 4
GIVE_PARTS = 1
GELU_C = 0.7978845608028654
GELU_A = 0.044715

VMEM = pl.BlockSpec(memory_space=pltpu.VMEM)
SMEM = pl.BlockSpec(memory_space=pltpu.SMEM)
HBM = pl.BlockSpec(memory_space=pltpu.HBM)
ANY = pl.BlockSpec(memory_space=pl.ANY)


def f32(*shape):
    return jax.ShapeDtypeStruct(shape, jnp.float32)


def bf16(*shape):
    return jax.ShapeDtypeStruct(shape, jnp.bfloat16)


def call(kernel, outs, arrays, after=(), specs=None, out_specs=None, scratch=()):
    skip = slice(len(arrays), len(arrays) + len(after))

    def run(*refs):
        kernel(*refs[: skip.start], *refs[skip.stop :])

    return pl.pallas_call(
        run,
        out_shape=outs,
        in_specs=list(specs or [VMEM] * len(arrays)) + [ANY] * len(after),
        out_specs=out_specs or [VMEM] * len(outs),
        scratch_shapes=list(scratch),
        compiler_params=pltpu.CompilerParams(vmem_limit_bytes=12 * 1024 * 1024),
        cost_estimate=pl.CostEstimate(flops=0, bytes_accessed=1 << 10, transcendentals=0),
    )(*arrays, *after)


def in_hbm(array):
    return pltpu.with_memory_space_constraint(array, pltpu.HBM)


def total_of(terms):
    return functools.reduce(jnp.add, terms)


def place_in_chain():
    lat = lax.axis_index("lat")
    return jnp.where(lax.axis_index("wid") == 0, lat, lax.axis_size("lat") - 1 - lat)


def level_table(bounds, count, out):
    lasts = bounds[...] - 1 - lax.axis_index("lat") * count
    upward = lax.axis_index("wid") == 0

    def put(row, value):
        out[row : row + 1, :] = jnp.broadcast_to(value, (1, BLOCK))

    for i in range(count):
        hits = (jnp.minimum(lasts, count - 1) == i).astype(jnp.float32)
        ending = jnp.sum(hits, axis=1, keepdims=True)
        put(i, ending)
        put(count + i, jnp.where(upward, jnp.full_like(ending, float(i == count - 1)), ending))
    for m in range(LEVELS):
        for i in range(count):
            put((2 + m) * count + i, (lasts[:, m : m + 1] == i).astype(jnp.float32))


def pre_kernel(resid, dictionary, partial_out, dict_out, resid_v, dict_v, sems):
    pieces, _, width = dict_v.shape
    copies = []
    for i in range(pieces):
        cols = pl.ds(i * width, width)
        copies.append(
            (
                pltpu.make_async_copy(resid.at[:, cols], resid_v.at[i], sems.at[0, i]),
                pltpu.make_async_copy(dictionary.at[:, cols], dict_v.at[i], sems.at[1, i]),
            )
        )
        for copy in copies[-1]:
            copy.start()
    total = None
    for i in range(pieces):
        for copy in copies[i]:
            copy.wait()
        term = lax.dot_general(
            dict_v[i], resid_v[i], (((1,), (1,)), ((), ())), preferred_element_type=jnp.float32
        )
        total = term if total is None else total + term
    partial_out[...] = total.T
    parts = dict_out.shape[1] // width
    for i in range(parts):
        dict_out[:, i * width : (i + 1) * width] = dict_v[lax.axis_index("tok") * parts + i]


def widen_kernel(array, bounds, out, table_out):
    out[...] = array[...].astype(jnp.float32)
    level_table(bounds, array.shape[0] // BLOCK, table_out)


def pieces_kernel(resid, bias, bias_out, *outs):
    width = outs[0].shape[1]
    tok = lax.axis_index("tok")

    def cols(t):
        return pl.ds(pl.multiple_of(t * width, width), width)

    bias_out[...] = bias[:, cols(tok)]
    for q, out in enumerate(outs):
        out[...] = resid[:, cols(tok ^ q)].astype(jnp.float32)


def block_mask(active, lats):
    count = lats // BLOCK
    ids = lax.axis_index("lat") * count + lax.broadcasted_iota(jnp.int32, (count, 1), 0)
    hits = total_of([(active[q : q + 1, :] == ids).astype(jnp.float32) for q in range(active.shape[0])])
    spread = lax.broadcasted_iota(jnp.int32, (count, lats), 1) // BLOCK
    spread = (spread == lax.broadcasted_iota(jnp.int32, (count, lats), 0)).astype(jnp.bfloat16)
    return lax.dot_general(
        hits.astype(jnp.bfloat16),
        spread,
        (((0,), (0,)), ((), ())),
        preferred_element_type=jnp.float32,
    )


def activate_kernel(mine, other, bias, active, pre_out, act_out, mask_out):
    pre = mine[...] + other[...] + bias[...]
    pre_out[...] = pre
    inner = GELU_C * (pre + GELU_A * (pre * pre * pre))
    gelu = 0.5 * pre * (1.0 + jnp.tanh(inner))
    mask = block_mask(active[...], pre.shape[1])
    mask_out[...] = mask
    act_out[...] = jnp.where(mask > 0.0, gelu, 0.0)


def half_of(wid, rows):
    return pl.ds(pl.multiple_of(wid * (rows // 2), rows // 2), rows // 2)


def g_pre_kernel(pre_ref, mask, loss, *refs):
    terms, out = refs[:-1], refs[-1]
    mine = half_of(lax.axis_index("wid"), pre_ref.shape[0])
    pre = pre_ref[mine, :]
    inner = GELU_C * (pre + GELU_A * (pre * pre * pre))
    slope = GELU_C * (1.0 + 3.0 * GELU_A * (pre * pre))
    bend = jnp.tanh(inner)
    deriv = 0.5 * (1.0 + bend) + 0.5 * pre * (1.0 - bend * bend) * slope
    hit = mask[mine, :] > 0.0
    rows = pre.shape[0]
    out[:rows, :] = jnp.where(hit, deriv * total_of([t[...] for t in terms]), 0.0)
    out[rows:, :] = jnp.zeros_like(out[rows:, :])
    out[rows:, :BLOCK] = loss[:LOSS_ROWS, :BLOCK]


def running_parts(act, dict_ref):
    sums = []
    for i in range(dict_ref.shape[0] // BLOCK):
        span = slice(i * BLOCK, (i + 1) * BLOCK)
        part = jnp.dot(
            act[:, span], dict_ref[span, :].astype(jnp.bfloat16), preferred_element_type=jnp.float32
        )
        sums.append(sums[-1] + part if sums else part)
    return sums


def round_kernel(act, out):
    out[...] = act[...].astype(jnp.bfloat16)


def project_kernel(act, table, *refs):
    dicts, out = refs[:-1], refs[-1]
    for side, dictionary in enumerate(dicts):
        sums = running_parts(act[...], dictionary)
        count = len(sums)
        width = dictionary.shape[1]
        out[:, side * width : (side + 1) * width] = total_of(
            [table[count + i : count + i + 1, :1] * s for i, s in enumerate(sums)]
        )


def columns(ref, col, width):
    return ref[:, col * width : (col + 1) * width]


def message_kernel(places, cols, got, *refs):
    out = refs[-1]
    width = out.shape[1]
    index = place_in_chain()
    for place, piece, col in zip(places, refs[:-1], cols[1:]):

        @pl.when(index == place)
        def _():
            own = columns(piece, col, width)
            out[...] = own + columns(got, cols[0], width) if place else own


def choose_kernel(places, cols, *refs):
    arrived, out = refs[:-1], refs[-1]
    index = place_in_chain()

    @pl.when(index == 0)
    def _():
        out[...] = jnp.zeros_like(out)

    for place, ref, col in zip(places, arrived, cols):

        @pl.when(index == place if len(arrived) > 1 else index > 0)
        def _():
            out[...] = columns(ref, col, out.shape[1])


def square_sums(table, shifted):
    count = len(shifted)
    squares = []
    for v in shifted:
        lanes = jnp.sum(v * v, axis=0, keepdims=True)
        squares.append(total_of([lanes[:, i : i + BLOCK] for i in range(0, lanes.shape[1], BLOCK)]))
    rows = []
    for m in range(LEVELS):
        at = (2 + m) * count
        rows.append(total_of([table[at + i : at + i + 1, :] * s for i, s in enumerate(squares)]))
    return jnp.concatenate(rows + [jnp.zeros((LOSS_ROWS - LEVELS, BLOCK), jnp.float32)], axis=0)


def error_kernel(loss_count, act, dictionary, resid, bias, table, mine, other, *refs):
    before, refs = refs[:loss_count], refs[loss_count:]
    err_out, keep_out, *give_outs, loss_out = refs
    upward = lax.axis_index("wid") == 0
    earlier = jnp.where(upward, mine[...], other[...])
    later = jnp.where(upward, other[...], mine[...])
    base = bias[...] - resid[...] + earlier
    sums = running_parts(act[...], dictionary)
    shifted = [base + s for s in sums]
    loss_out[...] = total_of([square_sums(table, shifted)] + [b[...] for b in before])
    err = later
    for i in reversed(range(len(sums))):
        err = err + table[i : i + 1, :1] * shifted[i]
        rounded = err.astype(jnp.bfloat16)
        err_out[i] = rounded
        cols = slice(i * BLOCK, (i + 1) * BLOCK)
        gact = lax.dot_general(
            rounded,
            dictionary[cols, :],
            (((1,), (1,)), ((), ())),
            preferred_element_type=jnp.float32,
        )
        half = gact.shape[0] // 2
        keep_out[:, cols] = jnp.where(upward, gact[:half, :], gact[half:, :])
        given = jnp.where(upward, gact[half:, :], gact[:half, :])
        for part, give_out in enumerate(give_outs):
            size = give_out.shape[0]
            give_out[:, cols] = given[part * size : (part + 1) * size, :]


def spread_kernel(loss, out):
    out[...] = jnp.zeros_like(out)
    out[:LOSS_ROWS, :BLOCK] = loss[...]


def collect_kernel(keep, *refs):
    parts, out = refs[:-1], refs[-1]
    for i, part in enumerate(parts):
        span = slice(i * part.shape[0], (i + 1) * part.shape[0])
        out[span, :] = keep[span, :] + part[...]


def add_kernel(*refs):
    refs[-1][...] = total_of([ref[...] for ref in refs[:-1]])


def decode_kernel(*refs):
    n = (len(refs) - 1) // 2
    errs, acts, out = refs[:n], refs[n : 2 * n], refs[-1]
    for i in range(errs[0].shape[0]):
        cols = slice(i * BLOCK, (i + 1) * BLOCK)
        err = jnp.concatenate([e[i] for e in errs], axis=0)
        act = jnp.concatenate([a[:, cols] for a in acts], axis=0)
        out[:, cols] = lax.dot_general(
            err, act, (((0,), (0,)), ((), ())), preferred_element_type=jnp.float32
        )


def encode_kernel(items, *refs):
    n, halves = items
    resids, grads, base, out = refs[:n], refs[n:-2], refs[-2], refs[-1]
    half = resids[0].shape[0] // 2
    wid = lax.axis_index("wid")
    spans = [half_of(wid, 2 * half), half_of(1 - wid, 2 * half)]
    resid = jnp.concatenate(
        [resids[q][spans[side], :].astype(jnp.bfloat16) for q, side in halves], axis=0
    )
    grad = jnp.concatenate([g[:half, :].astype(jnp.bfloat16) for g in grads], axis=0)
    total = base[...] + lax.dot_general(
        resid, grad, (((0,), (0,)), ((), ())), preferred_element_type=jnp.float32
    )
    out[...] = total.astype(out.dtype)


def last_kernel(items, scale, n_early, *refs):
    *refs, out, loss_out = refs
    early, refs = refs[:n_early], refs[n_early:]
    encode_kernel(items, *refs, out)
    grads = list(early) + list(refs[items[0] : -1])
    half = refs[0].shape[0] // 2
    lanes = total_of([g[half:, :BLOCK] for g in grads])
    for m in range(LEVELS):
        loss_out[m] = jnp.sum(lanes[m : m + 1, :]) * scale


def pick(index, choices):
    values = sorted(choices)
    result = choices[values[0]]
    for value in values[1:]:
        result = jnp.where(index == value, choices[value], result)
    return result


def body(resid, dictionary, enc_bias, dec_bias, active_blocks, level_bounds):
    rows, half = resid.shape
    lats = dictionary.shape[0]
    n_lat, n_wid, n_tok = lax.axis_size("lat"), lax.axis_size("wid"), lax.axis_size("tok")
    width = half // n_tok
    count = lats // BLOCK

    def across(array, q):
        return lax.ppermute(array, "tok", [(t, t ^ q) for t in range(n_tok)])

    def swap(array):
        return lax.ppermute(array, "wid", [(w, w ^ 1) for w in range(n_wid)])

    partial, dict_here = call(
        pre_kernel,
        [f32(rows, lats), bf16(lats, width)],
        (in_hbm(resid), in_hbm(dictionary)),
        specs=[HBM, HBM],
        scratch=[
            pltpu.VMEM((2 * n_tok, rows, width // 2), jnp.bfloat16),
            pltpu.VMEM((2 * n_tok, lats, width // 2), jnp.bfloat16),
            pltpu.SemaphoreType.DMA((2, 2 * n_tok)),
        ],
    )
    partial_other = swap(partial)
    dict_wide, table = call(
        widen_kernel,
        [f32(lats, width), f32((2 + LEVELS) * count, BLOCK)],
        (dict_here, level_bounds.reshape(1, LEVELS)),
        after=(partial_other,),
    )
    dict_other = swap(dict_wide)
    pre, act, mask = call(
        activate_kernel,
        [f32(rows, lats)] * 3,
        (partial, partial_other, enc_bias.reshape(1, lats), active_blocks.T),
        after=(dict_wide,),
    )
    gathered = [act] + [across(act, q) for q in range(1, n_tok)]
    bias_here, *pieces = call(
        pieces_kernel,
        [f32(1, width)] + [f32(rows, width)] * n_tok,
        (resid, dec_bias.reshape(1, half)),
        after=(act,),
    )
    resids = [piece if q == 0 else across(piece, q) for q, piece in enumerate(pieces)]

    order = [0, 3, 1, 2] if n_tok == 4 else list(range(n_tok))
    steps = n_tok + n_lat - 2
    places = list(range(1, n_lat))
    acts, errs, hands, gives, gacts, loss = {}, {}, [], [], [], ()
    sums, got, sent = ([], []), ([], []), []
    waits = {step: [] for step in range(steps)}
    for place, q in enumerate(order[1:]):
        waits[min(3 + place, steps - 1)].append(resids[q])

    def project(q, dicts):
        shape = [f32(rows, width * len(dicts))]
        return call(project_kernel, shape, (acts[q], table, *dicts))[0]

    for step in range(steps + 1):
        at = [p for p in range(n_lat - 1) if 0 <= step - p < n_tok]
        pairs = []
        for p in at:
            pairs.append((2 * p, 2 * (p + 1)))
            pairs.append((2 * (n_lat - 1 - p) + 1, 2 * (n_lat - 2 - p) + 1))
        if step == 0:
            acts[order[0]] = call(round_kernel, [bf16(rows, lats)], (act,))[0]
            for side, dict_ref in enumerate((dict_here, dict_other)):
                message = project(order[0], (dict_ref,))
                sums[side].append((message, 0))
                got[side].append((lax.ppermute(message, ("lat", "wid"), pairs), 0))
                sent = [message]
        elif step < steps:
            for side in range(2):
                items = [got[side][-1], *[sums[side][step - p] for p in at]]
                message = call(
                    functools.partial(message_kernel, at, [col for _, col in items]),
                    [f32(rows, width)],
                    [array for array, _ in items],
                    after=sent + (waits[step] if side == 0 else []) if step > 1 else (),
                )[0]
                got[side].append((lax.ppermute(message, ("lat", "wid"), pairs), 0))
                sent = [message]
        if step + 1 < n_tok:
            q = order[step + 1]
            acts[q] = call(round_kernel, [bf16(rows, lats)], (gathered[q],), after=sent)[0]
            for side, dict_ref in enumerate((dict_here, dict_other)):
                sums[side].append((project(q, (dict_ref,)), 0))
        ready = []
        c = step - (n_lat - 1)
        if c >= 0:
            chosen = []
            for side in (1, 0) if step < steps else (0, 1):
                items = [got[side][c + p - 1] for p in places]
                if n_lat > 4:
                    items = [a[:, col * width : (col + 1) * width] for a, col in items]
                    items = [(pick(place_in_chain(), dict(zip(places, items))), 0)]
                chosen.append(
                    call(
                        functools.partial(choose_kernel, places, [col for _, col in items]),
                        [f32(rows, width)],
                        [array for array, _ in items],
                        after=sent if step < steps else ready_before + chosen,
                    )[0]
                )
            hand, mine = chosen if step < steps else chosen[::-1]
            hands.append((swap(hand), mine))
            ready += chosen
        stages = [c - 1] if step < steps else [c - 1, c]
        for c in stages:
            if c < 0:
                continue
            q = order[c]
            errs[q], keep, *give, loss_here = call(
                functools.partial(error_kernel, len(loss)),
                [bf16(count, rows, width), f32(rows // 2, lats)]
                + [f32(rows // 2 // GIVE_PARTS, lats)] * GIVE_PARTS
                + [f32(LOSS_ROWS, BLOCK)],
                (acts[q], dict_here, resids[q], bias_here, table, hands[c][1], hands[c][0], *loss),
                after=sent if step < steps else (),
            )
            loss = (loss_here,)
            gives.append((keep, *[swap(g) for g in give]))
            ready.append(errs[q])
        stages = [1] if step == steps - 1 else [0, *range(2, n_tok)] if step == steps else []
        for c in stages:
            if c < 0:
                continue
            q = order[c]
            added = call(
                collect_kernel, [f32(rows // 2, lats)], gives[c], after=sent if step < steps else ()
            )[0]
            gacts.append(across(added, q) if q else added)
            ready.append(added)
        if step + 1 < steps:
            waits[step + 1] += ready
        ready_before = ready

    loss, gap = call(spread_kernel, [f32(rows // LOSS_PART, lats)], loss)[0], 1
    while gap < n_lat:
        other = lax.ppermute(loss, "lat", [(p, p ^ gap) for p in range(n_lat)])
        loss = call(add_kernel, [f32(*loss.shape)], (loss, other))[0]
        gap *= 2

    decoded = call(
        decode_kernel,
        [f32(width, lats)],
        (*[errs[q] for q in order], *[acts[q] for q in order]),
    )[0]
    g_pre = call(
        g_pre_kernel,
        [f32(rows // 2 + LOSS_ROWS, lats)],
        (pre, mask, loss, *gacts),
        after=(decoded,),
    )[0]
    mine = [across(g_pre, q) if q else g_pre for q in range(n_tok)]
    others = [swap(g) for g in mine]
    early = [(q, side) for side in range(2) for q in range(n_tok) if (q, side) != (1, 1)]
    halves = [mine, others]
    early_grads = [halves[side][q] for q, side in early]
    encoded = call(
        functools.partial(encode_kernel, (n_tok, early)),
        [f32(width, lats)],
        (*resids, *early_grads, decoded),
    )[0]
    grad, losses = call(
        functools.partial(
            last_kernel, (1, [(0, 1)]), 1.0 / (rows * n_tok * half * n_wid), len(early)
        ),
        [bf16(width, lats), f32(LEVELS)],
        (*early_grads, resids[1], others[1], encoded),
        out_specs=[VMEM, SMEM],
    )
    return (losses, grad)


def solution(mesh):
    return jax.shard_map(
        body,
        mesh=mesh,
        in_specs=(P("tok", "wid"), P("lat", "wid"), P("lat"), P("wid"), P("tok", None), P()),
        out_specs=(P(), P(("wid", "tok"), "lat")),
        check_vma=False,
    )
```

```python
import functools

import jax
import jax.numpy as jnp
from jax import lax
from jax.experimental import pallas as pl
from jax.experimental.pallas import tpu as pltpu
from jax.sharding import PartitionSpec as P

LEVELS = 4
BLOCK = 128
LOSS_ROWS = 8
GIVE_PARTS = 1
GELU_C = 0.7978845608028654
GELU_A = 0.044715

VMEM = pl.BlockSpec(memory_space=pltpu.VMEM)
SMEM = pl.BlockSpec(memory_space=pltpu.SMEM)
HBM = pl.BlockSpec(memory_space=pltpu.HBM)
ANY = pl.BlockSpec(memory_space=pl.ANY)


def f32(*shape):
    return jax.ShapeDtypeStruct(shape, jnp.float32)


def bf16(*shape):
    return jax.ShapeDtypeStruct(shape, jnp.bfloat16)


def call(kernel, outs, arrays, after=(), specs=None, out_specs=None, scratch=()):
    skip = slice(len(arrays), len(arrays) + len(after))

    def run(*refs):
        kernel(*refs[: skip.start], *refs[skip.stop :])

    return pl.pallas_call(
        run,
        out_shape=outs,
        in_specs=list(specs or [VMEM] * len(arrays)) + [ANY] * len(after),
        out_specs=out_specs or [VMEM] * len(outs),
        scratch_shapes=list(scratch),
        compiler_params=pltpu.CompilerParams(vmem_limit_bytes=12 * 1024 * 1024),
        cost_estimate=pl.CostEstimate(flops=0, bytes_accessed=1 << 10, transcendentals=0),
    )(*arrays, *after)


def in_hbm(array):
    return pltpu.with_memory_space_constraint(array, pltpu.HBM)


def total_of(terms):
    return functools.reduce(jnp.add, terms)


def place_in_chain():
    lat = lax.axis_index("lat")
    return jnp.where(lax.axis_index("wid") == 0, lat, lax.axis_size("lat") - 1 - lat)


def level_table(bounds, count, out):
    lasts = bounds[...] - 1 - lax.axis_index("lat") * count
    upward = lax.axis_index("wid") == 0

    def put(row, value):
        out[row : row + 1, :] = jnp.broadcast_to(value, (1, BLOCK))

    for i in range(count):
        hits = (jnp.minimum(lasts, count - 1) == i).astype(jnp.float32)
        ending = jnp.sum(hits, axis=1, keepdims=True)
        put(i, ending)
        put(count + i, jnp.where(upward, jnp.full_like(ending, float(i == count - 1)), ending))
    for m in range(LEVELS):
        for i in range(count):
            put((2 + m) * count + i, (lasts[:, m : m + 1] == i).astype(jnp.float32))


def pre_kernel(resid, dictionary, partial_out, dict_out, resid_v, dict_v, sems):
    pieces, _, width = dict_v.shape
    copies = []
    for i in range(pieces):
        cols = pl.ds(i * width, width)
        copies.append(
            (
                pltpu.make_async_copy(resid.at[:, cols], resid_v.at[i], sems.at[0, i]),
                pltpu.make_async_copy(dictionary.at[:, cols], dict_v.at[i], sems.at[1, i]),
            )
        )
        for copy in copies[-1]:
            copy.start()
    total = None
    for i in range(pieces):
        for copy in copies[i]:
            copy.wait()
        term = lax.dot_general(
            dict_v[i], resid_v[i], (((1,), (1,)), ((), ())), preferred_element_type=jnp.float32
        )
        total = term if total is None else total + term
    partial_out[...] = total.T
    parts = dict_out.shape[1] // width
    for i in range(parts):
        dict_out[:, i * width : (i + 1) * width] = dict_v[lax.axis_index("tok") * parts + i]


def widen_kernel(array, bounds, out, table_out):
    out[...] = array[...].astype(jnp.float32)
    level_table(bounds, array.shape[0] // BLOCK, table_out)


def pieces_kernel(resid, bias, bias_out, *outs):
    width = outs[0].shape[1]
    tok = lax.axis_index("tok")

    def cols(t):
        return pl.ds(pl.multiple_of(t * width, width), width)

    bias_out[...] = bias[:, cols(tok)]
    for q, out in enumerate(outs):
        out[...] = resid[:, cols(tok ^ q)].astype(jnp.float32)


def block_mask(active, lats):
    count = lats // BLOCK
    ids = lax.axis_index("lat") * count + lax.broadcasted_iota(jnp.int32, (count, 1), 0)
    hits = total_of([(active[q : q + 1, :] == ids).astype(jnp.float32) for q in range(active.shape[0])])
    spread = lax.broadcasted_iota(jnp.int32, (count, lats), 1) // BLOCK
    spread = (spread == lax.broadcasted_iota(jnp.int32, (count, lats), 0)).astype(jnp.bfloat16)
    return lax.dot_general(
        hits.astype(jnp.bfloat16),
        spread,
        (((0,), (0,)), ((), ())),
        preferred_element_type=jnp.float32,
    )


def activate_kernel(mine, other, bias, active, pre_out, act_out, mask_out):
    pre = mine[...] + other[...] + bias[...]
    pre_out[...] = pre
    inner = GELU_C * (pre + GELU_A * (pre * pre * pre))
    gelu = 0.5 * pre * (1.0 + jnp.tanh(inner))
    mask = block_mask(active[...], pre.shape[1])
    mask_out[...] = mask
    act_out[...] = jnp.where(mask > 0.0, gelu, 0.0)


def half_of(wid, rows):
    return pl.ds(pl.multiple_of(wid * (rows // 2), rows // 2), rows // 2)


def g_pre_kernel(n_losses, pre_ref, mask, *refs):
    losses, terms, out = refs[:n_losses], refs[n_losses:-1], refs[-1]
    mine = half_of(lax.axis_index("wid"), pre_ref.shape[0])
    pre = pre_ref[mine, :]
    inner = GELU_C * (pre + GELU_A * (pre * pre * pre))
    slope = GELU_C * (1.0 + 3.0 * GELU_A * (pre * pre))
    bend = jnp.tanh(inner)
    deriv = 0.5 * (1.0 + bend) + 0.5 * pre * (1.0 - bend * bend) * slope
    hit = mask[mine, :] > 0.0
    rows = pre.shape[0]
    out[:rows, :] = jnp.where(hit, deriv * total_of([t[...] for t in terms]), 0.0)
    out[rows:, :] = jnp.zeros_like(out[rows:, :])
    loss = losses[0][...]
    if n_losses > 1:
        loss = jnp.where(lax.axis_index("wid") == 0, loss, 0.0) + losses[1][...] + losses[2][...]
    out[rows:, :BLOCK] = loss


def running_parts(act, dict_ref):
    sums = []
    for i in range(dict_ref.shape[0] // BLOCK):
        span = slice(i * BLOCK, (i + 1) * BLOCK)
        part = jnp.dot(
            act[:, span], dict_ref[span, :].astype(jnp.bfloat16), preferred_element_type=jnp.float32
        )
        sums.append(sums[-1] + part if sums else part)
    return sums


def round_kernel(act, out):
    out[...] = act[...].astype(jnp.bfloat16)


def project_kernel(act, table, *refs):
    dicts, out = refs[:-1], refs[-1]
    for side, dictionary in enumerate(dicts):
        sums = running_parts(act[...], dictionary)
        count = len(sums)
        width = dictionary.shape[1]
        out[:, side * width : (side + 1) * width] = total_of(
            [table[count + i : count + i + 1, :1] * s for i, s in enumerate(sums)]
        )


def columns(ref, col, width):
    return ref[:, col * width : (col + 1) * width]


def message_kernel(places, cols, got, *refs):
    out = refs[-1]
    width = out.shape[1]
    index = place_in_chain()
    for place, piece, col in zip(places, refs[:-1], cols[1:]):

        @pl.when(index == place)
        def _():
            own = columns(piece, col, width)
            out[...] = own + columns(got, cols[0], width) if place else own


def choose_kernel(places, cols, *refs):
    arrived, out = refs[:-1], refs[-1]
    index = place_in_chain()

    @pl.when(index == 0)
    def _():
        out[...] = jnp.zeros_like(out)

    for place, ref, col in zip(places, arrived, cols):

        @pl.when(index == place if len(arrived) > 1 else index > 0)
        def _():
            out[...] = columns(ref, col, out.shape[1])


def square_sums(table, shifted):
    count = len(shifted)
    squares = []
    for v in shifted:
        lanes = jnp.sum(v * v, axis=0, keepdims=True)
        squares.append(total_of([lanes[:, i : i + BLOCK] for i in range(0, lanes.shape[1], BLOCK)]))
    rows = []
    for m in range(LEVELS):
        at = (2 + m) * count
        rows.append(total_of([table[at + i : at + i + 1, :] * s for i, s in enumerate(squares)]))
    return jnp.concatenate(rows + [jnp.zeros((LOSS_ROWS - LEVELS, BLOCK), jnp.float32)], axis=0)


def error_kernel(loss_count, act, dictionary, resid, bias, table, mine, other, *refs):
    before, refs = refs[:loss_count], refs[loss_count:]
    err_out, keep_out, *give_outs, loss_out = refs
    upward = lax.axis_index("wid") == 0
    earlier = jnp.where(upward, mine[...], other[...])
    later = jnp.where(upward, other[...], mine[...])
    base = bias[...] - resid[...] + earlier
    sums = running_parts(act[...], dictionary)
    shifted = [base + s for s in sums]
    loss_out[...] = total_of([square_sums(table, shifted)] + [b[...] for b in before])
    err = later
    for i in reversed(range(len(sums))):
        err = err + table[i : i + 1, :1] * shifted[i]
        rounded = err.astype(jnp.bfloat16)
        err_out[i] = rounded
        cols = slice(i * BLOCK, (i + 1) * BLOCK)
        gact = lax.dot_general(
            rounded,
            dictionary[cols, :],
            (((1,), (1,)), ((), ())),
            preferred_element_type=jnp.float32,
        )
        half = gact.shape[0] // 2
        keep_out[:, cols] = jnp.where(upward, gact[:half, :], gact[half:, :])
        given = jnp.where(upward, gact[half:, :], gact[:half, :])
        for part, give_out in enumerate(give_outs):
            size = give_out.shape[0]
            give_out[:, cols] = given[part * size : (part + 1) * size, :]


def collect_kernel(keep, *refs):
    parts, out = refs[:-1], refs[-1]
    for i, part in enumerate(parts):
        span = slice(i * part.shape[0], (i + 1) * part.shape[0])
        out[span, :] = keep[span, :] + part[...]


def add_kernel(*refs):
    refs[-1][...] = total_of([ref[...] for ref in refs[:-1]])


def decode_kernel(*refs):
    n = (len(refs) - 1) // 2
    errs, acts, out = refs[:n], refs[n : 2 * n], refs[-1]
    for i in range(errs[0].shape[0]):
        cols = slice(i * BLOCK, (i + 1) * BLOCK)
        err = jnp.concatenate([e[i] for e in errs], axis=0)
        act = jnp.concatenate([a[:, cols] for a in acts], axis=0)
        out[:, cols] = lax.dot_general(
            err, act, (((0,), (0,)), ((), ())), preferred_element_type=jnp.float32
        )


def encode_kernel(items, *refs):
    n, halves = items
    resids, grads, base, out = refs[:n], refs[n:-2], refs[-2], refs[-1]
    half = resids[0].shape[0] // 2
    wid = lax.axis_index("wid")
    spans = [half_of(wid, 2 * half), half_of(1 - wid, 2 * half)]
    resid = jnp.concatenate(
        [resids[q][spans[side], :].astype(jnp.bfloat16) for q, side in halves], axis=0
    )
    grad = jnp.concatenate([g[:half, :].astype(jnp.bfloat16) for g in grads], axis=0)
    total = base[...] + lax.dot_general(
        resid, grad, (((0,), (0,)), ((), ())), preferred_element_type=jnp.float32
    )
    out[...] = total.astype(out.dtype)


def last_kernel(items, scale, n_early, *refs):
    *refs, out, loss_out = refs
    early, refs = refs[:n_early], refs[n_early:]
    encode_kernel(items, *refs, out)
    grads = list(early) + list(refs[items[0] : -1])
    half = refs[0].shape[0] // 2
    lanes = total_of([g[half:, :BLOCK] for g in grads])
    for m in range(LEVELS):
        loss_out[m] = jnp.sum(lanes[m : m + 1, :]) * scale


def pick(index, choices):
    values = sorted(choices)
    result = choices[values[0]]
    for value in values[1:]:
        result = jnp.where(index == value, choices[value], result)
    return result


def body(resid, dictionary, enc_bias, dec_bias, active_blocks, level_bounds):
    rows, half = resid.shape
    lats = dictionary.shape[0]
    n_lat, n_wid, n_tok = lax.axis_size("lat"), lax.axis_size("wid"), lax.axis_size("tok")
    width = half // n_tok
    count = lats // BLOCK

    def across(array, q):
        return lax.ppermute(array, "tok", [(t, t ^ q) for t in range(n_tok)])

    def swap(array):
        return lax.ppermute(array, "wid", [(w, w ^ 1) for w in range(n_wid)])

    partial, dict_here = call(
        pre_kernel,
        [f32(rows, lats), bf16(lats, width)],
        (in_hbm(resid), in_hbm(dictionary)),
        specs=[HBM, HBM],
        scratch=[
            pltpu.VMEM((2 * n_tok, rows, width // 2), jnp.bfloat16),
            pltpu.VMEM((2 * n_tok, lats, width // 2), jnp.bfloat16),
            pltpu.SemaphoreType.DMA((2, 2 * n_tok)),
        ],
    )
    partial_other = swap(partial)
    dict_wide, table = call(
        widen_kernel,
        [f32(lats, width), f32((2 + LEVELS) * count, BLOCK)],
        (dict_here, level_bounds.reshape(1, LEVELS)),
        after=(partial_other,),
    )
    dict_other = swap(dict_wide)
    pre, act, mask = call(
        activate_kernel,
        [f32(rows, lats)] * 3,
        (partial, partial_other, enc_bias.reshape(1, lats), active_blocks.T),
        after=(dict_wide,),
    )
    gathered = [act] + [across(act, q) for q in range(1, n_tok)]
    bias_here, *pieces = call(
        pieces_kernel,
        [f32(1, width)] + [f32(rows, width)] * n_tok,
        (resid, dec_bias.reshape(1, half)),
        after=(act,),
    )
    resids = [piece if q == 0 else across(piece, q) for q, piece in enumerate(pieces)]

    order = [0, 1, 3, 2] if n_tok == 4 else list(range(n_tok))
    steps = n_tok + n_lat - 2
    places = list(range(1, n_lat))
    acts, errs, hands, gives, gacts, loss = {}, {}, [], [], [], ()
    sums, got, sent = ([], []), ([], []), []
    waits = {step: [] for step in range(steps)}
    for place, q in enumerate(order[1:]):
        waits[min(3 + place, steps - 1)].append(resids[q])

    def project(q, dicts):
        shape = [f32(rows, width * len(dicts))]
        return call(project_kernel, shape, (acts[q], table, *dicts))[0]

    for step in range(steps + 1):
        at = [p for p in range(n_lat - 1) if 0 <= step - p < n_tok]
        pairs = []
        for p in at:
            pairs.append((2 * p, 2 * (p + 1)))
            pairs.append((2 * (n_lat - 1 - p) + 1, 2 * (n_lat - 2 - p) + 1))
        if step == 0:
            acts[order[0]] = call(round_kernel, [bf16(rows, lats)], (act,))[0]
            for side, dict_ref in enumerate((dict_here, dict_other)):
                message = project(order[0], (dict_ref,))
                sums[side].append((message, 0))
                got[side].append((lax.ppermute(message, ("lat", "wid"), pairs), 0))
                sent = [message]
        elif step < steps:
            for side in range(2):
                items = [got[side][-1], *[sums[side][step - p] for p in at]]
                message = call(
                    functools.partial(message_kernel, at, [col for _, col in items]),
                    [f32(rows, width)],
                    [array for array, _ in items],
                    after=sent + (waits[step] if side == 0 else []) if step > 1 else (),
                )[0]
                got[side].append((lax.ppermute(message, ("lat", "wid"), pairs), 0))
                sent = [message]
        if step + 1 < n_tok:
            q = order[step + 1]
            acts[q] = call(round_kernel, [bf16(rows, lats)], (gathered[q],), after=sent)[0]
            for side, dict_ref in enumerate((dict_here, dict_other)):
                sums[side].append((project(q, (dict_ref,)), 0))
        ready = []
        c = step - (n_lat - 1)
        if c >= 0:
            chosen = []
            for side in (1, 0) if step < steps else (0, 1):
                items = [got[side][c + p - 1] for p in places]
                if n_lat > 4:
                    items = [a[:, col * width : (col + 1) * width] for a, col in items]
                    items = [(pick(place_in_chain(), dict(zip(places, items))), 0)]
                chosen.append(
                    call(
                        functools.partial(choose_kernel, places, [col for _, col in items]),
                        [f32(rows, width)],
                        [array for array, _ in items],
                        after=sent if step < steps else ready_before + chosen,
                    )[0]
                )
            hand, mine = chosen if step < steps else chosen[::-1]
            hands.append((swap(hand), mine))
            ready += chosen
        stages = [c - 1] if step < steps else [c - 1, c]
        for c in stages:
            if c < 0:
                continue
            q = order[c]
            errs[q], keep, *give, loss_here = call(
                functools.partial(error_kernel, len(loss)),
                [bf16(count, rows, width), f32(rows // 2, lats)]
                + [f32(rows // 2 // GIVE_PARTS, lats)] * GIVE_PARTS
                + [f32(LOSS_ROWS, BLOCK)],
                (acts[q], dict_here, resids[q], bias_here, table, hands[c][1], hands[c][0], *loss),
                after=sent if step < steps else (),
            )
            loss = (loss_here,)
            gives.append((keep, *[swap(g) for g in give]))
            ready.append(errs[q])
        stages = [1] if step == steps - 1 else [0, *range(2, n_tok)] if step == steps else []
        for c in stages:
            if c < 0:
                continue
            q = order[c]
            added = call(
                collect_kernel, [f32(rows // 2, lats)], gives[c], after=sent if step < steps else ()
            )[0]
            gacts.append(across(added, q) if q else added)
            ready.append(added)
        if step + 1 < steps:
            waits[step + 1] += ready
        ready_before = ready

    loss, gap = loss[0], 4 if n_lat % 4 == 0 else 1
    while gap < n_lat:
        other = lax.ppermute(loss, "lat", [(p, p ^ gap) for p in range(n_lat)])
        loss = call(add_kernel, [f32(*loss.shape)], (loss, other))[0]
        gap *= 2
    losses = (loss,)
    if n_lat % 4 == 0:
        loss = call(add_kernel, [f32(*loss.shape)], (loss, swap(loss)))[0]
        pairs = [(2 * p + w, 2 * (p ^ (1 + w)) + w) for p in range(n_lat) for w in range(2)]
        near = lax.ppermute(loss, ("lat", "wid"), pairs)
        pairs = [(2 * p + 1, 2 * (p ^ 3) + 1) for p in range(n_lat)]
        losses = (loss, near, lax.ppermute(loss, ("lat", "wid"), pairs))

    decoded = call(
        decode_kernel,
        [f32(width, lats)],
        (*[errs[q] for q in order], *[acts[q] for q in order]),
    )[0]
    g_pre = call(
        functools.partial(g_pre_kernel, len(losses)),
        [f32(rows // 2 + LOSS_ROWS, lats)],
        (pre, mask, *losses, *gacts),
        after=(decoded,),
    )[0]
    mine = [across(g_pre, q) if q else g_pre for q in range(n_tok)]
    others = [swap(g) for g in mine]
    early = [(q, side) for side in range(2) for q in range(n_tok) if (q, side) != (1, 1)]
    halves = [mine, others]
    early_grads = [halves[side][q] for q, side in early]
    encoded = call(
        functools.partial(encode_kernel, (n_tok, early)),
        [f32(width, lats)],
        (*resids, *early_grads, decoded),
    )[0]
    grad, losses = call(
        functools.partial(
            last_kernel, (1, [(0, 1)]), 1.0 / (rows * n_tok * half * n_wid), len(early)
        ),
        [bf16(width, lats), f32(LEVELS)],
        (*early_grads, resids[1], others[1], encoded),
        out_specs=[VMEM, SMEM],
    )
    return (losses, grad)


def solution(mesh):
    return jax.shard_map(
        body,
        mesh=mesh,
        in_specs=(P("tok", "wid"), P("lat", "wid"), P("lat"), P("wid"), P("tok", None), P()),
        out_specs=(P(), P(("wid", "tok"), "lat")),
        check_vma=False,
    )
```

```python
import functools

import jax
import jax.numpy as jnp
from jax import lax
from jax.experimental import pallas as pl
from jax.experimental.pallas import tpu as pltpu
from jax.sharding import PartitionSpec as P

LEVELS = 4
BLOCK = 128
LOSS_ROWS = 8
GIVE_PARTS = 1
GELU_C = 0.7978845608028654
GELU_A = 0.044715

VMEM = pl.BlockSpec(memory_space=pltpu.VMEM)
SMEM = pl.BlockSpec(memory_space=pltpu.SMEM)
HBM = pl.BlockSpec(memory_space=pltpu.HBM)
ANY = pl.BlockSpec(memory_space=pl.ANY)


def f32(*shape):
    return jax.ShapeDtypeStruct(shape, jnp.float32)


def bf16(*shape):
    return jax.ShapeDtypeStruct(shape, jnp.bfloat16)


def call(kernel, outs, arrays, after=(), specs=None, out_specs=None, scratch=()):
    skip = slice(len(arrays), len(arrays) + len(after))

    def run(*refs):
        kernel(*refs[: skip.start], *refs[skip.stop :])

    return pl.pallas_call(
        run,
        out_shape=outs,
        in_specs=list(specs or [VMEM] * len(arrays)) + [ANY] * len(after),
        out_specs=out_specs or [VMEM] * len(outs),
        scratch_shapes=list(scratch),
        compiler_params=pltpu.CompilerParams(vmem_limit_bytes=12 * 1024 * 1024),
        cost_estimate=pl.CostEstimate(flops=0, bytes_accessed=1 << 10, transcendentals=0),
    )(*arrays, *after)


def in_hbm(array):
    return pltpu.with_memory_space_constraint(array, pltpu.HBM)


def total_of(terms):
    return functools.reduce(jnp.add, terms)


def place_in_chain():
    lat = lax.axis_index("lat")
    return jnp.where(lax.axis_index("wid") == 0, lat, lax.axis_size("lat") - 1 - lat)


def level_table(bounds, count, out):
    lasts = bounds[...] - 1 - lax.axis_index("lat") * count
    upward = lax.axis_index("wid") == 0

    def put(row, value):
        out[row : row + 1, :] = jnp.broadcast_to(value, (1, BLOCK))

    for i in range(count):
        hits = (jnp.minimum(lasts, count - 1) == i).astype(jnp.float32)
        ending = jnp.sum(hits, axis=1, keepdims=True)
        put(i, ending)
        put(count + i, jnp.where(upward, jnp.full_like(ending, float(i == count - 1)), ending))
    for m in range(LEVELS):
        for i in range(count):
            put((2 + m) * count + i, (lasts[:, m : m + 1] == i).astype(jnp.float32))


def pre_kernel(resid, dictionary, partial_out, dict_out, resid_v, dict_v, sems):
    pieces, _, width = dict_v.shape
    copies = []
    for i in range(pieces):
        cols = pl.ds(i * width, width)
        copies.append(
            (
                pltpu.make_async_copy(resid.at[:, cols], resid_v.at[i], sems.at[0, i]),
                pltpu.make_async_copy(dictionary.at[:, cols], dict_v.at[i], sems.at[1, i]),
            )
        )
        for copy in copies[-1]:
            copy.start()
    total = None
    for i in range(pieces):
        for copy in copies[i]:
            copy.wait()
        term = lax.dot_general(
            dict_v[i], resid_v[i], (((1,), (1,)), ((), ())), preferred_element_type=jnp.float32
        )
        total = term if total is None else total + term
    partial_out[...] = total.T
    parts = dict_out.shape[1] // width
    for i in range(parts):
        dict_out[:, i * width : (i + 1) * width] = dict_v[lax.axis_index("tok") * parts + i]


def widen_kernel(array, bounds, out, table_out):
    out[...] = array[...].astype(jnp.float32)
    level_table(bounds, array.shape[0] // BLOCK, table_out)


def pieces_kernel(resid, bias, bias_out, *outs):
    width = outs[0].shape[1]
    tok = lax.axis_index("tok")

    def cols(t):
        return pl.ds(pl.multiple_of(t * width, width), width)

    bias_out[...] = bias[:, cols(tok)]
    for q, out in enumerate(outs):
        out[...] = resid[:, cols(tok ^ q)].astype(jnp.float32)


def block_mask(active, lats):
    count = lats // BLOCK
    ids = lax.axis_index("lat") * count + lax.broadcasted_iota(jnp.int32, (count, 1), 0)
    hits = total_of([(active[q : q + 1, :] == ids).astype(jnp.float32) for q in range(active.shape[0])])
    spread = lax.broadcasted_iota(jnp.int32, (count, lats), 1) // BLOCK
    spread = (spread == lax.broadcasted_iota(jnp.int32, (count, lats), 0)).astype(jnp.bfloat16)
    return lax.dot_general(
        hits.astype(jnp.bfloat16),
        spread,
        (((0,), (0,)), ((), ())),
        preferred_element_type=jnp.float32,
    )


def activate_kernel(mine, other, bias, active, pre_out, act_out, mask_out):
    pre = mine[...] + other[...] + bias[...]
    pre_out[...] = pre
    inner = GELU_C * (pre + GELU_A * (pre * pre * pre))
    gelu = 0.5 * pre * (1.0 + jnp.tanh(inner))
    mask = block_mask(active[...], pre.shape[1])
    mask_out[...] = mask
    act_out[...] = jnp.where(mask > 0.0, gelu, 0.0)


def half_of(wid, rows):
    return pl.ds(pl.multiple_of(wid * (rows // 2), rows // 2), rows // 2)


def g_pre_kernel(n_losses, pre_ref, mask, *refs):
    losses, terms, out = refs[:n_losses], refs[n_losses:-1], refs[-1]
    mine = half_of(lax.axis_index("wid"), pre_ref.shape[0])
    pre = pre_ref[mine, :]
    inner = GELU_C * (pre + GELU_A * (pre * pre * pre))
    slope = GELU_C * (1.0 + 3.0 * GELU_A * (pre * pre))
    bend = jnp.tanh(inner)
    deriv = 0.5 * (1.0 + bend) + 0.5 * pre * (1.0 - bend * bend) * slope
    hit = mask[mine, :] > 0.0
    rows = pre.shape[0]
    out[:rows, :] = jnp.where(hit, deriv * total_of([t[...] for t in terms]), 0.0)
    out[rows:, :] = jnp.zeros_like(out[rows:, :])
    loss = losses[0][...]
    if n_losses > 1:
        loss = jnp.where(lax.axis_index("wid") == 0, loss, 0.0) + losses[1][...] + losses[2][...]
    out[rows:, :BLOCK] = loss


def running_parts(act, dict_ref):
    sums = []
    for i in range(dict_ref.shape[0] // BLOCK):
        span = slice(i * BLOCK, (i + 1) * BLOCK)
        part = jnp.dot(
            act[:, span], dict_ref[span, :].astype(jnp.bfloat16), preferred_element_type=jnp.float32
        )
        sums.append(sums[-1] + part if sums else part)
    return sums


def round_kernel(act, out):
    out[...] = act[...].astype(jnp.bfloat16)


def project_kernel(act, table, *refs):
    dicts, out = refs[:-1], refs[-1]
    for side, dictionary in enumerate(dicts):
        sums = running_parts(act[...], dictionary)
        count = len(sums)
        width = dictionary.shape[1]
        out[:, side * width : (side + 1) * width] = total_of(
            [table[count + i : count + i + 1, :1] * s for i, s in enumerate(sums)]
        )


def columns(ref, col, width):
    return ref[:, col * width : (col + 1) * width]


def message_kernel(places, cols, got, *refs):
    out = refs[-1]
    width = out.shape[1]
    index = place_in_chain()
    for place, piece, col in zip(places, refs[:-1], cols[1:]):

        @pl.when(index == place)
        def _():
            own = columns(piece, col, width)
            out[...] = own + columns(got, cols[0], width) if place else own


def choose_kernel(places, cols, *refs):
    arrived, out = refs[:-1], refs[-1]
    index = place_in_chain()

    @pl.when(index == 0)
    def _():
        out[...] = jnp.zeros_like(out)

    for place, ref, col in zip(places, arrived, cols):

        @pl.when(index == place if len(arrived) > 1 else index > 0)
        def _():
            out[...] = columns(ref, col, out.shape[1])


def square_sums(table, shifted):
    count = len(shifted)
    squares = []
    for v in shifted:
        lanes = jnp.sum(v * v, axis=0, keepdims=True)
        squares.append(total_of([lanes[:, i : i + BLOCK] for i in range(0, lanes.shape[1], BLOCK)]))
    rows = []
    for m in range(LEVELS):
        at = (2 + m) * count
        rows.append(total_of([table[at + i : at + i + 1, :] * s for i, s in enumerate(squares)]))
    return jnp.concatenate(rows + [jnp.zeros((LOSS_ROWS - LEVELS, BLOCK), jnp.float32)], axis=0)


def error_kernel(loss_count, act, dictionary, resid, bias, table, mine, other, *refs):
    before, refs = refs[:loss_count], refs[loss_count:]
    err_out, keep_out, *give_outs, loss_out = refs
    upward = lax.axis_index("wid") == 0
    earlier = jnp.where(upward, mine[...], other[...])
    later = jnp.where(upward, other[...], mine[...])
    base = bias[...] - resid[...] + earlier
    sums = running_parts(act[...], dictionary)
    shifted = [base + s for s in sums]
    loss_out[...] = total_of([square_sums(table, shifted)] + [b[...] for b in before])
    err = later
    for i in reversed(range(len(sums))):
        err = err + table[i : i + 1, :1] * shifted[i]
        rounded = err.astype(jnp.bfloat16)
        err_out[i] = rounded
        cols = slice(i * BLOCK, (i + 1) * BLOCK)
        gact = lax.dot_general(
            rounded,
            dictionary[cols, :],
            (((1,), (1,)), ((), ())),
            preferred_element_type=jnp.float32,
        )
        half = gact.shape[0] // 2
        keep_out[:, cols] = jnp.where(upward, gact[:half, :], gact[half:, :])
        given = jnp.where(upward, gact[half:, :], gact[:half, :])
        for part, give_out in enumerate(give_outs):
            size = give_out.shape[0]
            give_out[:, cols] = given[part * size : (part + 1) * size, :]


def collect_kernel(keep, *refs):
    parts, out = refs[:-1], refs[-1]
    for i, part in enumerate(parts):
        span = slice(i * part.shape[0], (i + 1) * part.shape[0])
        out[span, :] = keep[span, :] + part[...]


def add_kernel(*refs):
    refs[-1][...] = total_of([ref[...] for ref in refs[:-1]])


def decode_kernel(*refs):
    n = (len(refs) - 1) // 2
    errs, acts, out = refs[:n], refs[n : 2 * n], refs[-1]
    for i in range(errs[0].shape[0]):
        cols = slice(i * BLOCK, (i + 1) * BLOCK)
        err = jnp.concatenate([e[i] for e in errs], axis=0)
        act = jnp.concatenate([a[:, cols] for a in acts], axis=0)
        out[:, cols] = lax.dot_general(
            err, act, (((0,), (0,)), ((), ())), preferred_element_type=jnp.float32
        )


def encode_kernel(items, *refs):
    n, halves = items
    resids, grads, base, out = refs[:n], refs[n:-2], refs[-2], refs[-1]
    half = resids[0].shape[0] // 2
    wid = lax.axis_index("wid")
    spans = [half_of(wid, 2 * half), half_of(1 - wid, 2 * half)]
    resid = jnp.concatenate(
        [resids[q][spans[side], :].astype(jnp.bfloat16) for q, side in halves], axis=0
    )
    grad = jnp.concatenate([g[:half, :].astype(jnp.bfloat16) for g in grads], axis=0)
    total = base[...] + lax.dot_general(
        resid, grad, (((0,), (0,)), ((), ())), preferred_element_type=jnp.float32
    )
    out[...] = total.astype(out.dtype)


def last_kernel(items, scale, n_early, *refs):
    *refs, out, loss_out = refs
    early, refs = refs[:n_early], refs[n_early:]
    encode_kernel(items, *refs, out)
    grads = list(early) + list(refs[items[0] : -1])
    half = refs[0].shape[0] // 2
    lanes = total_of([g[half:, :BLOCK] for g in grads])
    for m in range(LEVELS):
        loss_out[m] = jnp.sum(lanes[m : m + 1, :]) * scale


def pick(index, choices):
    values = sorted(choices)
    result = choices[values[0]]
    for value in values[1:]:
        result = jnp.where(index == value, choices[value], result)
    return result


def body(resid, dictionary, enc_bias, dec_bias, active_blocks, level_bounds):
    rows, half = resid.shape
    lats = dictionary.shape[0]
    n_lat, n_wid, n_tok = lax.axis_size("lat"), lax.axis_size("wid"), lax.axis_size("tok")
    width = half // n_tok
    count = lats // BLOCK

    def across(array, q):
        return lax.ppermute(array, "tok", [(t, t ^ q) for t in range(n_tok)])

    def swap(array):
        return lax.ppermute(array, "wid", [(w, w ^ 1) for w in range(n_wid)])

    partial, dict_here = call(
        pre_kernel,
        [f32(rows, lats), bf16(lats, width)],
        (in_hbm(resid), in_hbm(dictionary)),
        specs=[HBM, HBM],
        scratch=[
            pltpu.VMEM((2 * n_tok, rows, width // 2), jnp.bfloat16),
            pltpu.VMEM((2 * n_tok, lats, width // 2), jnp.bfloat16),
            pltpu.SemaphoreType.DMA((2, 2 * n_tok)),
        ],
    )
    partial_other = swap(partial)
    dict_wide, table = call(
        widen_kernel,
        [f32(lats, width), f32((2 + LEVELS) * count, BLOCK)],
        (dict_here, level_bounds.reshape(1, LEVELS)),
        after=(partial_other,),
    )
    dict_other = swap(dict_wide)
    pre, act, mask = call(
        activate_kernel,
        [f32(rows, lats)] * 3,
        (partial, partial_other, enc_bias.reshape(1, lats), active_blocks.T),
        after=(dict_wide,),
    )
    gathered = [act] + [across(act, q) for q in range(1, n_tok)]
    bias_here, *pieces = call(
        pieces_kernel,
        [f32(1, width)] + [f32(rows, width)] * n_tok,
        (resid, dec_bias.reshape(1, half)),
        after=(act,),
    )
    resids = [piece if q == 0 else across(piece, q) for q, piece in enumerate(pieces)]

    order = [0, 1, 3, 2] if n_tok == 4 else list(range(n_tok))
    steps = n_tok + n_lat - 2
    places = list(range(1, n_lat))
    acts, errs, hands, gives, gacts, loss = {}, {}, [], [], [], ()
    sums, got, sent = ([], []), ([], []), []
    waits = {step: [] for step in range(steps)}
    for place, q in enumerate(order[1:]):
        waits[min(3 + place, steps - 1)].append(resids[q])

    def project(q, dicts):
        shape = [f32(rows, width * len(dicts))]
        return call(project_kernel, shape, (acts[q], table, *dicts))[0]

    def prepare(step, after):
        if step + 1 >= n_tok:
            return []
        q = order[step + 1]
        acts[q] = call(round_kernel, [bf16(rows, lats)], (gathered[q],), after=after)[0]
        new = [project(q, (dict_ref,)) for dict_ref in (dict_here, dict_other)]
        for side, piece in enumerate(new):
            sums[side].append((piece, 0))
        return new

    for step in range(steps + 1):
        at = [p for p in range(n_lat - 1) if 0 <= step - p < n_tok]
        pairs = []
        for p in at:
            pairs.append((2 * p, 2 * (p + 1)))
            pairs.append((2 * (n_lat - 1 - p) + 1, 2 * (n_lat - 2 - p) + 1))
        if step == 0:
            acts[order[0]] = call(round_kernel, [bf16(rows, lats)], (act,))[0]
            for side, dict_ref in enumerate((dict_here, dict_other)):
                message = project(order[0], (dict_ref,))
                sums[side].append((message, 0))
                got[side].append((lax.ppermute(message, ("lat", "wid"), pairs), 0))
                sent = [message]
        elif step < steps:
            for side in range(2):
                items = [got[side][-1], *[sums[side][step - p] for p in at]]
                message = call(
                    functools.partial(message_kernel, at, [col for _, col in items]),
                    [f32(rows, width)],
                    [array for array, _ in items],
                    after=sent + (waits[step] if side == 0 else []) if step > 1 or side else (),
                )[0]
                got[side].append((lax.ppermute(message, ("lat", "wid"), pairs), 0))
                sent = [message]
                if side == 0:
                    sent += prepare(step, sent)
        if step == 0:
            prepare(step, sent)
        ready = []
        c = step - (n_lat - 1)
        if c >= 0:
            chosen = []
            for side in (1, 0) if step < steps else (0, 1):
                items = [got[side][c + p - 1] for p in places]
                if n_lat > 4:
                    items = [a[:, col * width : (col + 1) * width] for a, col in items]
                    items = [(pick(place_in_chain(), dict(zip(places, items))), 0)]
                chosen.append(
                    call(
                        functools.partial(choose_kernel, places, [col for _, col in items]),
                        [f32(rows, width)],
                        [array for array, _ in items],
                        after=sent if step < steps else ready_before + chosen,
                    )[0]
                )
            hand, mine = chosen if step < steps else chosen[::-1]
            hands.append((swap(hand), mine))
            ready += chosen
        stages = [c - 1] if step < steps else [c - 1, c]
        for c in stages:
            if c < 0:
                continue
            q = order[c]
            errs[q], keep, *give, loss_here = call(
                functools.partial(error_kernel, len(loss)),
                [bf16(count, rows, width), f32(rows // 2, lats)]
                + [f32(rows // 2 // GIVE_PARTS, lats)] * GIVE_PARTS
                + [f32(LOSS_ROWS, BLOCK)],
                (acts[q], dict_here, resids[q], bias_here, table, hands[c][1], hands[c][0], *loss),
                after=sent if step < steps else (),
            )
            loss = (loss_here,)
            gives.append((keep, *[swap(g) for g in give]))
            ready.append(errs[q])
        stages = [1] if step == steps - 1 else [0, *range(2, n_tok)] if step == steps else []
        for c in stages:
            if c < 0:
                continue
            q = order[c]
            added = call(
                collect_kernel, [f32(rows // 2, lats)], gives[c], after=sent if step < steps else ()
            )[0]
            gacts.append(across(added, q) if q else added)
            ready.append(added)
        if step + 1 < steps:
            waits[step + 1] += ready
        ready_before = ready

    loss, gap = loss[0], 4 if n_lat % 4 == 0 else 1
    while gap < n_lat:
        other = lax.ppermute(loss, "lat", [(p, p ^ gap) for p in range(n_lat)])
        loss = call(add_kernel, [f32(*loss.shape)], (loss, other))[0]
        gap *= 2
    losses = (loss,)
    if n_lat % 4 == 0:
        loss = call(add_kernel, [f32(*loss.shape)], (loss, swap(loss)))[0]
        pairs = [(2 * p + w, 2 * (p ^ (1 + w)) + w) for p in range(n_lat) for w in range(2)]
        near = lax.ppermute(loss, ("lat", "wid"), pairs)
        pairs = [(2 * p + 1, 2 * (p ^ 3) + 1) for p in range(n_lat)]
        losses = (loss, near, lax.ppermute(loss, ("lat", "wid"), pairs))

    decoded = call(
        decode_kernel,
        [f32(width, lats)],
        (*[errs[q] for q in order], *[acts[q] for q in order]),
    )[0]
    g_pre = call(
        functools.partial(g_pre_kernel, len(losses)),
        [f32(rows // 2 + LOSS_ROWS, lats)],
        (pre, mask, *losses, *gacts),
        after=(decoded,),
    )[0]
    mine = [across(g_pre, q) if q else g_pre for q in range(n_tok)]
    others = [swap(g) for g in mine]
    early = [(q, side) for side in range(2) for q in range(n_tok) if (q, side) != (1, 1)]
    halves = [mine, others]
    early_grads = [halves[side][q] for q, side in early]
    encoded = call(
        functools.partial(encode_kernel, (n_tok, early)),
        [f32(width, lats)],
        (*resids, *early_grads, decoded),
    )[0]
    grad, losses = call(
        functools.partial(
            last_kernel, (1, [(0, 1)]), 1.0 / (rows * n_tok * half * n_wid), len(early)
        ),
        [bf16(width, lats), f32(LEVELS)],
        (*early_grads, resids[1], others[1], encoded),
        out_specs=[VMEM, SMEM],
    )
    return (losses, grad)


def solution(mesh):
    return jax.shard_map(
        body,
        mesh=mesh,
        in_specs=(P("tok", "wid"), P("lat", "wid"), P("lat"), P("wid"), P("tok", None), P()),
        out_specs=(P(), P(("wid", "tok"), "lat")),
        check_vma=False,
    )
```

```python
import functools

import jax
import jax.numpy as jnp
from jax import lax
from jax.experimental import pallas as pl
from jax.experimental.pallas import tpu as pltpu
from jax.sharding import PartitionSpec as P

LEVELS = 4
BLOCK = 128
LOSS_ROWS = 8
LOSS_PART = 2
GELU_C = 0.7978845608028654
GELU_A = 0.044715

VMEM = pl.BlockSpec(memory_space=pltpu.VMEM)
SMEM = pl.BlockSpec(memory_space=pltpu.SMEM)
HBM = pl.BlockSpec(memory_space=pltpu.HBM)
ANY = pl.BlockSpec(memory_space=pl.ANY)


def f32(*shape):
    return jax.ShapeDtypeStruct(shape, jnp.float32)


def bf16(*shape):
    return jax.ShapeDtypeStruct(shape, jnp.bfloat16)


def call(kernel, outs, arrays, after=(), specs=None, out_specs=None, scratch=()):
    skip = slice(len(arrays), len(arrays) + len(after))

    def run(*refs):
        kernel(*refs[: skip.start], *refs[skip.stop :])

    return pl.pallas_call(
        run,
        out_shape=outs,
        in_specs=list(specs or [VMEM] * len(arrays)) + [ANY] * len(after),
        out_specs=out_specs or [VMEM] * len(outs),
        scratch_shapes=list(scratch),
        compiler_params=pltpu.CompilerParams(vmem_limit_bytes=12 * 1024 * 1024),
        cost_estimate=pl.CostEstimate(flops=0, bytes_accessed=1 << 10, transcendentals=0),
    )(*arrays, *after)


def in_hbm(array):
    return pltpu.with_memory_space_constraint(array, pltpu.HBM)


def total_of(terms):
    return functools.reduce(jnp.add, terms)


def place_in_chain():
    lat = lax.axis_index("lat")
    return jnp.where(lax.axis_index("wid") == 0, lat, lax.axis_size("lat") - 1 - lat)


def level_table(bounds, count, out):
    lasts = bounds[...] - 1 - lax.axis_index("lat") * count
    upward = lax.axis_index("wid") == 0

    def put(row, value):
        out[row : row + 1, :] = jnp.broadcast_to(value, (1, BLOCK))

    for i in range(count):
        hits = (jnp.minimum(lasts, count - 1) == i).astype(jnp.float32)
        ending = jnp.sum(hits, axis=1, keepdims=True)
        put(i, ending)
        put(count + i, jnp.where(upward, jnp.full_like(ending, float(i == count - 1)), ending))
    for m in range(LEVELS):
        for i in range(count):
            put((2 + m) * count + i, (lasts[:, m : m + 1] == i).astype(jnp.float32))


def pre_kernel(resid, dictionary, partial_out, dict_out, resid_v, dict_v, sems):
    pieces, _, width = dict_v.shape
    copies = []
    for i in range(pieces):
        cols = pl.ds(i * width, width)
        copies.append(
            (
                pltpu.make_async_copy(resid.at[:, cols], resid_v.at[i], sems.at[0, i]),
                pltpu.make_async_copy(dictionary.at[:, cols], dict_v.at[i], sems.at[1, i]),
            )
        )
        for copy in copies[-1]:
            copy.start()
    total = None
    for i in range(pieces):
        for copy in copies[i]:
            copy.wait()
        term = lax.dot_general(
            dict_v[i], resid_v[i], (((1,), (1,)), ((), ())), preferred_element_type=jnp.float32
        )
        total = term if total is None else total + term
    partial_out[...] = total.T
    parts = dict_out.shape[1] // width
    for i in range(parts):
        dict_out[:, i * width : (i + 1) * width] = dict_v[lax.axis_index("tok") * parts + i]


def widen_kernel(array, bounds, out, table_out):
    out[...] = array[...].astype(jnp.float32)
    level_table(bounds, array.shape[0] // BLOCK, table_out)


def pieces_kernel(resid, bias, bias_out, *outs):
    width = outs[0].shape[1]
    tok = lax.axis_index("tok")

    def cols(t):
        return pl.ds(pl.multiple_of(t * width, width), width)

    bias_out[...] = bias[:, cols(tok)]
    for q, out in enumerate(outs):
        out[...] = resid[:, cols(tok ^ q)].astype(jnp.float32)


def block_mask(active, lats):
    count = lats // BLOCK
    ids = lax.axis_index("lat") * count + lax.broadcasted_iota(jnp.int32, (count, 1), 0)
    hits = total_of([(active[q : q + 1, :] == ids).astype(jnp.float32) for q in range(active.shape[0])])
    spread = lax.broadcasted_iota(jnp.int32, (count, lats), 1) // BLOCK
    spread = (spread == lax.broadcasted_iota(jnp.int32, (count, lats), 0)).astype(jnp.bfloat16)
    return lax.dot_general(
        hits.astype(jnp.bfloat16),
        spread,
        (((0,), (0,)), ((), ())),
        preferred_element_type=jnp.float32,
    )


def activate_kernel(mine, other, bias, active, pre_out, act_out, mask_out):
    pre = mine[...] + other[...] + bias[...]
    pre_out[...] = pre
    inner = GELU_C * (pre + GELU_A * (pre * pre * pre))
    gelu = 0.5 * pre * (1.0 + jnp.tanh(inner))
    mask = block_mask(active[...], pre.shape[1])
    mask_out[...] = mask
    act_out[...] = jnp.where(mask > 0.0, gelu, 0.0)


def half_of(wid, rows):
    return pl.ds(pl.multiple_of(wid * (rows // 2), rows // 2), rows // 2)


def stacked(parts, extra, out):
    rows, cols = parts.shape
    for i in range(cols // BLOCK):
        out[i * rows : (i + 1) * rows, :] = parts[:, i * BLOCK : (i + 1) * BLOCK]
    out[-LOSS_ROWS:, :] = extra


def unstacked(ref, cols):
    rows = (ref.shape[0] - LOSS_ROWS) // (cols // BLOCK)
    return jnp.concatenate(
        [ref[i * rows : (i + 1) * rows, :] for i in range(cols // BLOCK)], axis=1
    )


def g_pre_kernel(pre_ref, mask, loss, keep, give, *refs):
    *arrived, out, loss_out = refs
    mine = half_of(lax.axis_index("wid"), pre_ref.shape[0])
    pre = pre_ref[mine, :]
    inner = GELU_C * (pre + GELU_A * (pre * pre * pre))
    slope = GELU_C * (1.0 + 3.0 * GELU_A * (pre * pre))
    bend = jnp.tanh(inner)
    deriv = 0.5 * (1.0 + bend) + 0.5 * pre * (1.0 - bend * bend) * slope
    hit = mask[mine, :] > 0.0
    total = keep[...] + give[...] + total_of([unstacked(a, pre.shape[1]) for a in arrived])
    out[...] = jnp.where(hit, deriv * total, 0.0)
    loss_out[...] = jnp.zeros_like(loss_out)
    loss_out[:LOSS_ROWS, :BLOCK] = loss[...] + total_of([a[-LOSS_ROWS:, :] for a in arrived])


def running_parts(act, dict_ref):
    sums = []
    for i in range(dict_ref.shape[0] // BLOCK):
        span = slice(i * BLOCK, (i + 1) * BLOCK)
        part = jnp.dot(
            act[:, span], dict_ref[span, :].astype(jnp.bfloat16), preferred_element_type=jnp.float32
        )
        sums.append(sums[-1] + part if sums else part)
    return sums


def round_kernel(act, out):
    out[...] = act[...].astype(jnp.bfloat16)


def project_kernel(act, table, *refs):
    dicts, out = refs[:-1], refs[-1]
    for side, dictionary in enumerate(dicts):
        sums = running_parts(act[...], dictionary)
        count = len(sums)
        width = dictionary.shape[1]
        out[:, side * width : (side + 1) * width] = total_of(
            [table[count + i : count + i + 1, :1] * s for i, s in enumerate(sums)]
        )


def columns(ref, col, width):
    return ref[:, col * width : (col + 1) * width]


def message_kernel(places, cols, got, *refs):
    out = refs[-1]
    width = out.shape[1]
    index = place_in_chain()
    for place, piece, col in zip(places, refs[:-1], cols[1:]):

        @pl.when(index == place)
        def _():
            own = columns(piece, col, width)
            out[...] = own + columns(got, cols[0], width) if place else own


def choose_kernel(places, cols, *refs):
    arrived, out = refs[:-1], refs[-1]
    index = place_in_chain()

    @pl.when(index == 0)
    def _():
        out[...] = jnp.zeros_like(out)

    for place, ref, col in zip(places, arrived, cols):

        @pl.when(index == place if len(arrived) > 1 else index > 0)
        def _():
            out[...] = columns(ref, col, out.shape[1])


def square_sums(table, shifted):
    count = len(shifted)
    squares = []
    for v in shifted:
        lanes = jnp.sum(v * v, axis=0, keepdims=True)
        squares.append(total_of([lanes[:, i : i + BLOCK] for i in range(0, lanes.shape[1], BLOCK)]))
    rows = []
    for m in range(LEVELS):
        at = (2 + m) * count
        rows.append(total_of([table[at + i : at + i + 1, :] * s for i, s in enumerate(squares)]))
    return jnp.concatenate(rows + [jnp.zeros((LOSS_ROWS - LEVELS, BLOCK), jnp.float32)], axis=0)


def error_kernel(loss_count, act, dictionary, resid, bias, table, mine, other, *refs):
    before, refs = refs[:loss_count], refs[loss_count:]
    err_out, keep_out, give_out, loss_out = refs
    upward = lax.axis_index("wid") == 0
    earlier = jnp.where(upward, mine[...], other[...])
    later = jnp.where(upward, other[...], mine[...])
    base = bias[...] - resid[...] + earlier
    sums = running_parts(act[...], dictionary)
    shifted = [base + s for s in sums]
    loss_out[...] = total_of([square_sums(table, shifted)] + [b[...] for b in before])
    err = later
    for i in reversed(range(len(sums))):
        err = err + table[i : i + 1, :1] * shifted[i]
        rounded = err.astype(jnp.bfloat16)
        err_out[i] = rounded
        cols = slice(i * BLOCK, (i + 1) * BLOCK)
        gact = lax.dot_general(
            rounded,
            dictionary[cols, :],
            (((1,), (1,)), ((), ())),
            preferred_element_type=jnp.float32,
        )
        half = gact.shape[0] // 2
        keep_out[:, cols] = jnp.where(upward, gact[:half, :], gact[half:, :])
        give_out[:, cols] = jnp.where(upward, gact[half:, :], gact[:half, :])


def collect_kernel(keep, give, loss, out):
    stacked(keep[...] + give[...], loss[...], out)


def chip_losses_kernel(own, near, far, out):
    first = jnp.where(lax.axis_index("wid") == 0, own[...], 0.0)
    out[...] = first + near[...] + far[...]


def add_kernel(*refs):
    refs[-1][...] = total_of([ref[...] for ref in refs[:-1]])


def decode_kernel(*refs):
    n = (len(refs) - 1) // 2
    errs, acts, out = refs[:n], refs[n : 2 * n], refs[-1]
    for i in range(errs[0].shape[0]):
        cols = slice(i * BLOCK, (i + 1) * BLOCK)
        err = jnp.concatenate([e[i] for e in errs], axis=0)
        act = jnp.concatenate([a[:, cols] for a in acts], axis=0)
        out[:, cols] = lax.dot_general(
            err, act, (((0,), (0,)), ((), ())), preferred_element_type=jnp.float32
        )


def encode_kernel(items, *refs):
    n, halves = items
    resids, grads, base, out = refs[:n], refs[n:-2], refs[-2], refs[-1]
    half = resids[0].shape[0] // 2
    wid = lax.axis_index("wid")
    spans = [half_of(wid, 2 * half), half_of(1 - wid, 2 * half)]
    resid = jnp.concatenate(
        [resids[q][spans[side], :].astype(jnp.bfloat16) for q, side in halves], axis=0
    )
    grad = jnp.concatenate([g[...].astype(jnp.bfloat16) for g in grads], axis=0)
    total = base[...] + lax.dot_general(
        resid, grad, (((0,), (0,)), ((), ())), preferred_element_type=jnp.float32
    )
    out[...] = total.astype(out.dtype)


def last_kernel(items, scale, one, two, *refs):
    *refs, out, loss_out = refs
    encode_kernel(items, *refs, out)
    for m in range(LEVELS):
        loss_out[m] = jnp.sum(one[m : m + 1, :BLOCK] + two[m : m + 1, :BLOCK]) * scale


def pick(index, choices):
    values = sorted(choices)
    result = choices[values[0]]
    for value in values[1:]:
        result = jnp.where(index == value, choices[value], result)
    return result


def body(resid, dictionary, enc_bias, dec_bias, active_blocks, level_bounds):
    rows, half = resid.shape
    lats = dictionary.shape[0]
    n_lat, n_wid, n_tok = lax.axis_size("lat"), lax.axis_size("wid"), lax.axis_size("tok")
    width = half // n_tok
    count = lats // BLOCK

    def across(array, q):
        return lax.ppermute(array, "tok", [(t, t ^ q) for t in range(n_tok)])

    def swap(array):
        return lax.ppermute(array, "wid", [(w, w ^ 1) for w in range(n_wid)])

    partial, dict_here = call(
        pre_kernel,
        [f32(rows, lats), bf16(lats, width)],
        (in_hbm(resid), in_hbm(dictionary)),
        specs=[HBM, HBM],
        scratch=[
            pltpu.VMEM((2 * n_tok, rows, width // 2), jnp.bfloat16),
            pltpu.VMEM((2 * n_tok, lats, width // 2), jnp.bfloat16),
            pltpu.SemaphoreType.DMA((2, 2 * n_tok)),
        ],
    )
    partial_other = swap(partial)
    dict_wide, table = call(
        widen_kernel,
        [f32(lats, width), f32((2 + LEVELS) * count, BLOCK)],
        (dict_here, level_bounds.reshape(1, LEVELS)),
        after=(partial_other,),
    )
    dict_other = swap(dict_wide)
    pre, act, mask = call(
        activate_kernel,
        [f32(rows, lats)] * 3,
        (partial, partial_other, enc_bias.reshape(1, lats), active_blocks.T),
        after=(dict_wide,),
    )
    gathered = [act] + [across(act, q) for q in range(1, n_tok)]
    bias_here, *pieces = call(
        pieces_kernel,
        [f32(1, width)] + [f32(rows, width)] * n_tok,
        (resid, dec_bias.reshape(1, half)),
        after=(act,),
    )
    resids = [piece if q == 0 else across(piece, q) for q, piece in enumerate(pieces)]

    order = [0, 1, 3, 2] if n_tok == 4 else list(range(n_tok))
    steps = n_tok + n_lat - 2
    places = list(range(1, n_lat))
    acts, errs, hands, gives, gacts, loss = {}, {}, [], [], [], ()
    sums, got, sent = ([], []), ([], []), []
    waits = {step: [] for step in range(steps)}
    for place, q in enumerate(order[1:]):
        waits[min(3 + place, steps - 1)].append(resids[q])

    def project(q, dicts):
        shape = [f32(rows, width * len(dicts))]
        return call(project_kernel, shape, (acts[q], table, *dicts))[0]

    for step in range(steps + 1):
        at = [p for p in range(n_lat - 1) if 0 <= step - p < n_tok]
        pairs = []
        for p in at:
            pairs.append((2 * p, 2 * (p + 1)))
            pairs.append((2 * (n_lat - 1 - p) + 1, 2 * (n_lat - 2 - p) + 1))
        if step == 0:
            acts[order[0]] = call(round_kernel, [bf16(rows, lats)], (act,))[0]
            for side, dict_ref in enumerate((dict_here, dict_other)):
                message = project(order[0], (dict_ref,))
                sums[side].append((message, 0))
                got[side].append((lax.ppermute(message, ("lat", "wid"), pairs), 0))
                sent = [message]
        elif step < steps:
            for side in range(2):
                items = [got[side][-1], *[sums[side][step - p] for p in at]]
                message = call(
                    functools.partial(message_kernel, at, [col for _, col in items]),
                    [f32(rows, width)],
                    [array for array, _ in items],
                    after=sent + (waits[step] if side == 0 else []) if step > 1 else (),
                )[0]
                got[side].append((lax.ppermute(message, ("lat", "wid"), pairs), 0))
                sent = [message]
        if step + 1 < n_tok:
            q = order[step + 1]
            acts[q] = call(round_kernel, [bf16(rows, lats)], (gathered[q],), after=sent)[0]
            for side, dict_ref in enumerate((dict_here, dict_other)):
                sums[side].append((project(q, (dict_ref,)), 0))
        ready = []
        c = step - (n_lat - 1)
        if c >= 0:
            chosen = []
            for side in (1, 0) if step < steps else (0, 1):
                items = [got[side][c + p - 1] for p in places]
                if n_lat > 4:
                    items = [a[:, col * width : (col + 1) * width] for a, col in items]
                    items = [(pick(place_in_chain(), dict(zip(places, items))), 0)]
                chosen.append(
                    call(
                        functools.partial(choose_kernel, places, [col for _, col in items]),
                        [f32(rows, width)],
                        [array for array, _ in items],
                        after=sent if step < steps else ready_before + chosen,
                    )[0]
                )
            hand, mine = chosen if step < steps else chosen[::-1]
            hands.append((swap(hand), mine))
            ready += chosen
        stages = [c - 1] if step < steps else [c - 1, c]
        for c in stages:
            if c < 0:
                continue
            q = order[c]
            errs[q], keep, give, loss_here = call(
                functools.partial(error_kernel, len(loss)),
                [bf16(count, rows, width)] + [f32(rows // 2, lats)] * 2 + [f32(LOSS_ROWS, BLOCK)],
                (acts[q], dict_here, resids[q], bias_here, table, hands[c][1], hands[c][0], *loss),
                after=sent if step < steps else (),
            )
            loss = (loss_here,)
            gives.append((keep, swap(give)))
            ready.append(errs[q])
        if step + 1 < steps:
            waits[step + 1] += ready
        ready_before = ready

    arrived = []
    for c, q in enumerate(order[1:], 1):
        message = call(
            collect_kernel, [f32(rows // 2 * count + LOSS_ROWS, BLOCK)], (*gives[c], *loss)
        )[0]
        arrived.append(across(message, q))
    decoded = call(
        decode_kernel,
        [f32(width, lats)],
        (*[errs[q] for q in order], *[acts[q] for q in order]),
    )[0]
    g_pre, losses = call(
        g_pre_kernel,
        [f32(rows // 2, lats), f32(rows // LOSS_PART, lats)],
        (pre, mask, *loss, *gives[0], *arrived),
        after=(decoded,),
    )
    mine = [across(g_pre, q) if q else g_pre for q in range(n_tok)]
    others = [swap(g) for g in mine]

    def add(*arrays):
        return call(add_kernel, [f32(*arrays[0].shape)], arrays)[0]

    gap = 4 if n_lat % 4 == 0 else 1
    while gap < n_lat:
        losses = add(losses, lax.ppermute(losses, "lat", [(p, p ^ gap) for p in range(n_lat)]))
        gap *= 2
    if n_lat % 4 == 0:
        losses = add(losses, swap(losses))
        pairs = [(2 * p + w, 2 * (p ^ (1 + w)) + w) for p in range(n_lat) for w in range(2)]
        near = lax.ppermute(losses, ("lat", "wid"), pairs)
        pairs = [(2 * p + 1, 2 * (p ^ 3) + 1) for p in range(n_lat)]
        far = lax.ppermute(losses, ("lat", "wid"), pairs)
        losses = call(chip_losses_kernel, [f32(*losses.shape)], (losses, near, far))[0]
    losses = (losses, swap(losses))
    early = [(q, side) for side in range(2) for q in range(n_tok) if (q, side) != (1, 1)]
    halves = [mine, others]
    early_grads = [halves[side][q] for q, side in early]
    encoded = call(
        functools.partial(encode_kernel, (n_tok, early)),
        [f32(width, lats)],
        (*resids, *early_grads, decoded),
    )[0]
    grad, level_losses = call(
        functools.partial(last_kernel, (1, [(0, 1)]), 1.0 / (rows * n_tok * half * n_wid)),
        [bf16(width, lats), f32(LEVELS)],
        (*losses, resids[1], others[1], encoded),
        out_specs=[VMEM, SMEM],
    )
    return (level_losses, grad)


def solution(mesh):
    return jax.shard_map(
        body,
        mesh=mesh,
        in_specs=(P("tok", "wid"), P("lat", "wid"), P("lat"), P("wid"), P("tok", None), P()),
        out_specs=(P(), P(("wid", "tok"), "lat")),
        check_vma=False,
    )
```

```python
import functools

import jax
import jax.numpy as jnp
from jax import lax
from jax.experimental import pallas as pl
from jax.experimental.pallas import tpu as pltpu
from jax.sharding import PartitionSpec as P

LEVELS = 4
BLOCK = 128
LOSS_ROWS = 8
GELU_C = 0.7978845608028654
GELU_A = 0.044715

VMEM = pl.BlockSpec(memory_space=pltpu.VMEM)
SMEM = pl.BlockSpec(memory_space=pltpu.SMEM)
HBM = pl.BlockSpec(memory_space=pltpu.HBM)
ANY = pl.BlockSpec(memory_space=pl.ANY)


def f32(*shape):
    return jax.ShapeDtypeStruct(shape, jnp.float32)


def bf16(*shape):
    return jax.ShapeDtypeStruct(shape, jnp.bfloat16)


def call(kernel, outs, arrays, after=(), specs=None, out_specs=None, scratch=()):
    skip = slice(len(arrays), len(arrays) + len(after))

    def run(*refs):
        kernel(*refs[: skip.start], *refs[skip.stop :])

    return pl.pallas_call(
        run,
        out_shape=outs,
        in_specs=list(specs or [VMEM] * len(arrays)) + [ANY] * len(after),
        out_specs=out_specs or [VMEM] * len(outs),
        scratch_shapes=list(scratch),
        compiler_params=pltpu.CompilerParams(vmem_limit_bytes=12 * 1024 * 1024),
        cost_estimate=pl.CostEstimate(flops=0, bytes_accessed=1 << 10, transcendentals=0),
    )(*arrays, *after)


def in_hbm(array):
    return pltpu.with_memory_space_constraint(array, pltpu.HBM)


def total_of(terms):
    return functools.reduce(jnp.add, terms)


def place_in_chain():
    lat = lax.axis_index("lat")
    return jnp.where(lax.axis_index("wid") == 0, lat, lax.axis_size("lat") - 1 - lat)


def level_table(bounds, count, out):
    lasts = bounds[...] - 1 - lax.axis_index("lat") * count
    upward = lax.axis_index("wid") == 0

    def put(row, value):
        out[row : row + 1, :] = jnp.broadcast_to(value, (1, BLOCK))

    for i in range(count):
        hits = (jnp.minimum(lasts, count - 1) == i).astype(jnp.float32)
        ending = jnp.sum(hits, axis=1, keepdims=True)
        put(i, ending)
        put(count + i, jnp.where(upward, jnp.full_like(ending, float(i == count - 1)), ending))
    for m in range(LEVELS):
        for i in range(count):
            put((2 + m) * count + i, (lasts[:, m : m + 1] == i).astype(jnp.float32))


def pre_kernel(resid, dictionary, partial_out, dict_out, resid_v, dict_v, sems):
    pieces, _, width = dict_v.shape
    copies = []
    for i in range(pieces):
        cols = pl.ds(i * width, width)
        copies.append(
            (
                pltpu.make_async_copy(resid.at[:, cols], resid_v.at[i], sems.at[0, i]),
                pltpu.make_async_copy(dictionary.at[:, cols], dict_v.at[i], sems.at[1, i]),
            )
        )
        for copy in copies[-1]:
            copy.start()
    total = None
    for i in range(pieces):
        for copy in copies[i]:
            copy.wait()
        term = lax.dot_general(
            dict_v[i], resid_v[i], (((1,), (1,)), ((), ())), preferred_element_type=jnp.float32
        )
        total = term if total is None else total + term
    partial_out[...] = total.T
    parts = dict_out.shape[1] // width
    for i in range(parts):
        dict_out[:, i * width : (i + 1) * width] = dict_v[lax.axis_index("tok") * parts + i]


def widen_kernel(array, bounds, out, table_out):
    out[...] = array[...].astype(jnp.float32)
    level_table(bounds, array.shape[0] // BLOCK, table_out)


def pieces_kernel(resid, bias, bias_out, *outs):
    width = outs[0].shape[1]
    tok = lax.axis_index("tok")

    def cols(t):
        return pl.ds(pl.multiple_of(t * width, width), width)

    bias_out[...] = bias[:, cols(tok)]
    for q, out in enumerate(outs):
        out[...] = resid[:, cols(tok ^ q)].astype(jnp.float32)


def block_mask(active, lats):
    count = lats // BLOCK
    ids = lax.axis_index("lat") * count + lax.broadcasted_iota(jnp.int32, (count, 1), 0)
    hits = total_of([(active[q : q + 1, :] == ids).astype(jnp.float32) for q in range(active.shape[0])])
    spread = lax.broadcasted_iota(jnp.int32, (count, lats), 1) // BLOCK
    spread = (spread == lax.broadcasted_iota(jnp.int32, (count, lats), 0)).astype(jnp.bfloat16)
    return lax.dot_general(
        hits.astype(jnp.bfloat16),
        spread,
        (((0,), (0,)), ((), ())),
        preferred_element_type=jnp.float32,
    )


def activate_kernel(mine, other, bias, active, pre_out, act_out, mask_out):
    pre = mine[...] + other[...] + bias[...]
    pre_out[...] = pre
    inner = GELU_C * (pre + GELU_A * (pre * pre * pre))
    gelu = 0.5 * pre * (1.0 + jnp.tanh(inner))
    mask = block_mask(active[...], pre.shape[1])
    mask_out[...] = mask
    act_out[...] = jnp.where(mask > 0.0, gelu, 0.0)


def half_of(wid, rows):
    return pl.ds(pl.multiple_of(wid * (rows // 2), rows // 2), rows // 2)


def stacked(parts, extra, out):
    rows, cols = parts.shape
    for i in range(cols // BLOCK):
        out[i * rows : (i + 1) * rows, :] = parts[:, i * BLOCK : (i + 1) * BLOCK]
    out[-LOSS_ROWS:, :] = extra


def unstacked(ref, count):
    rows = (ref.shape[0] - LOSS_ROWS) // count
    return jnp.concatenate([ref[i * rows : (i + 1) * rows, :] for i in range(count)], axis=1)


def g_pre_kernel(pre_ref, mask, loss, *refs):
    terms, out = refs[:-1], refs[-1]
    mine = half_of(lax.axis_index("wid"), pre_ref.shape[0])
    pre = pre_ref[mine, :]
    inner = GELU_C * (pre + GELU_A * (pre * pre * pre))
    slope = GELU_C * (1.0 + 3.0 * GELU_A * (pre * pre))
    bend = jnp.tanh(inner)
    deriv = 0.5 * (1.0 + bend) + 0.5 * pre * (1.0 - bend * bend) * slope
    hit = mask[mine, :] > 0.0
    stacked(jnp.where(hit, deriv * total_of([t[...] for t in terms]), 0.0), loss[...], out)


def running_parts(act, dict_ref):
    sums = []
    for i in range(dict_ref.shape[0] // BLOCK):
        span = slice(i * BLOCK, (i + 1) * BLOCK)
        part = jnp.dot(
            act[:, span], dict_ref[span, :].astype(jnp.bfloat16), preferred_element_type=jnp.float32
        )
        sums.append(sums[-1] + part if sums else part)
    return sums


def round_kernel(act, out):
    out[...] = act[...].astype(jnp.bfloat16)


def project_kernel(act, table, *refs):
    dicts, out = refs[:-1], refs[-1]
    for side, dictionary in enumerate(dicts):
        sums = running_parts(act[...], dictionary)
        count = len(sums)
        width = dictionary.shape[1]
        out[:, side * width : (side + 1) * width] = total_of(
            [table[count + i : count + i + 1, :1] * s for i, s in enumerate(sums)]
        )


def columns(ref, col, width):
    return ref[:, col * width : (col + 1) * width]


def message_kernel(places, cols, got, *refs):
    out = refs[-1]
    width = out.shape[1]
    index = place_in_chain()
    for place, piece, col in zip(places, refs[:-1], cols[1:]):

        @pl.when(index == place)
        def _():
            own = columns(piece, col, width)
            out[...] = own + columns(got, cols[0], width) if place else own


def choose_kernel(places, cols, *refs):
    arrived, out = refs[:-1], refs[-1]
    index = place_in_chain()

    @pl.when(index == 0)
    def _():
        out[...] = jnp.zeros_like(out)

    for place, ref, col in zip(places, arrived, cols):

        @pl.when(index == place if len(arrived) > 1 else index > 0)
        def _():
            out[...] = columns(ref, col, out.shape[1])


def square_sums(table, shifted):
    count = len(shifted)
    squares = []
    for v in shifted:
        lanes = jnp.sum(v * v, axis=0, keepdims=True)
        squares.append(total_of([lanes[:, i : i + BLOCK] for i in range(0, lanes.shape[1], BLOCK)]))
    rows = []
    for m in range(LEVELS):
        at = (2 + m) * count
        rows.append(total_of([table[at + i : at + i + 1, :] * s for i, s in enumerate(squares)]))
    return jnp.concatenate(rows + [jnp.zeros((LOSS_ROWS - LEVELS, BLOCK), jnp.float32)], axis=0)


def error_kernel(loss_count, act, dictionary, resid, bias, table, mine, other, *refs):
    before, refs = refs[:loss_count], refs[loss_count:]
    err_out, keep_out, give_out, loss_out = refs
    upward = lax.axis_index("wid") == 0
    earlier = jnp.where(upward, mine[...], other[...])
    later = jnp.where(upward, other[...], mine[...])
    base = bias[...] - resid[...] + earlier
    sums = running_parts(act[...], dictionary)
    shifted = [base + s for s in sums]
    loss_out[...] = total_of([square_sums(table, shifted)] + [b[...] for b in before])
    err = later
    for i in reversed(range(len(sums))):
        err = err + table[i : i + 1, :1] * shifted[i]
        rounded = err.astype(jnp.bfloat16)
        err_out[i] = rounded
        cols = slice(i * BLOCK, (i + 1) * BLOCK)
        gact = lax.dot_general(
            rounded,
            dictionary[cols, :],
            (((1,), (1,)), ((), ())),
            preferred_element_type=jnp.float32,
        )
        half = gact.shape[0] // 2
        keep_out[:, cols] = jnp.where(upward, gact[:half, :], gact[half:, :])
        give_out[:, cols] = jnp.where(upward, gact[half:, :], gact[:half, :])


def collect_kernel(keep, give, out):
    out[...] = keep[...] + give[...]


def add_kernel(*refs):
    refs[-1][...] = total_of([ref[...] for ref in refs[:-1]])


def decode_kernel(*refs):
    n = (len(refs) - 1) // 2
    errs, acts, out = refs[:n], refs[n : 2 * n], refs[-1]
    for i in range(errs[0].shape[0]):
        cols = slice(i * BLOCK, (i + 1) * BLOCK)
        err = jnp.concatenate([e[i] for e in errs], axis=0)
        act = jnp.concatenate([a[:, cols] for a in acts], axis=0)
        out[:, cols] = lax.dot_general(
            err, act, (((0,), (0,)), ((), ())), preferred_element_type=jnp.float32
        )


def encode_kernel(items, *refs):
    n, halves = items
    resids, grads, base, out = refs[:n], refs[n:-2], refs[-2], refs[-1]
    half = resids[0].shape[0] // 2
    count = out.shape[1] // BLOCK
    wid = lax.axis_index("wid")
    spans = [half_of(wid, 2 * half), half_of(1 - wid, 2 * half)]
    resid = jnp.concatenate(
        [resids[q][spans[side], :].astype(jnp.bfloat16) for q, side in halves], axis=0
    )
    grad = jnp.concatenate([unstacked(g, count).astype(jnp.bfloat16) for g in grads], axis=0)
    total = base[...] + lax.dot_general(
        resid, grad, (((0,), (0,)), ((), ())), preferred_element_type=jnp.float32
    )
    out[...] = total.astype(out.dtype)


def last_kernel(items, scale, n_early, *refs):
    *refs, out, loss_out = refs
    early, refs = refs[:n_early], refs[n_early:]
    encode_kernel(items, *refs, out)
    grads = list(early) + list(refs[items[0] : -1])
    lanes = total_of([g[-LOSS_ROWS:, :] for g in grads])
    for m in range(LEVELS):
        loss_out[m] = jnp.sum(lanes[m : m + 1, :]) * scale


def pick(index, choices):
    values = sorted(choices)
    result = choices[values[0]]
    for value in values[1:]:
        result = jnp.where(index == value, choices[value], result)
    return result


def body(resid, dictionary, enc_bias, dec_bias, active_blocks, level_bounds):
    rows, half = resid.shape
    lats = dictionary.shape[0]
    n_lat, n_wid, n_tok = lax.axis_size("lat"), lax.axis_size("wid"), lax.axis_size("tok")
    width = half // n_tok
    count = lats // BLOCK

    def across(array, q):
        return lax.ppermute(array, "tok", [(t, t ^ q) for t in range(n_tok)])

    def swap(array):
        return lax.ppermute(array, "wid", [(w, w ^ 1) for w in range(n_wid)])

    partial, dict_here = call(
        pre_kernel,
        [f32(rows, lats), bf16(lats, width)],
        (in_hbm(resid), in_hbm(dictionary)),
        specs=[HBM, HBM],
        scratch=[
            pltpu.VMEM((2 * n_tok, rows, width // 2), jnp.bfloat16),
            pltpu.VMEM((2 * n_tok, lats, width // 2), jnp.bfloat16),
            pltpu.SemaphoreType.DMA((2, 2 * n_tok)),
        ],
    )
    partial_other = swap(partial)
    dict_wide, table = call(
        widen_kernel,
        [f32(lats, width), f32((2 + LEVELS) * count, BLOCK)],
        (dict_here, level_bounds.reshape(1, LEVELS)),
        after=(partial_other,),
    )
    dict_other = swap(dict_wide)
    pre, act, mask = call(
        activate_kernel,
        [f32(rows, lats)] * 3,
        (partial, partial_other, enc_bias.reshape(1, lats), active_blocks.T),
        after=(dict_wide,),
    )
    gathered = [act] + [across(act, q) for q in range(1, n_tok)]
    bias_here, *pieces = call(
        pieces_kernel,
        [f32(1, width)] + [f32(rows, width)] * n_tok,
        (resid, dec_bias.reshape(1, half)),
        after=(act,),
    )
    resids = [piece if q == 0 else across(piece, q) for q, piece in enumerate(pieces)]

    order = [0, 1, 3, 2] if n_tok == 4 else list(range(n_tok))
    steps = n_tok + n_lat - 2
    places = list(range(1, n_lat))
    acts, errs, hands, gives, gacts, loss = {}, {}, [], [], [], ()
    sums, got, sent = ([], []), ([], []), []
    waits = {step: [] for step in range(steps)}
    for place, q in enumerate(order[1:]):
        waits[min(3 + place, steps - 1)].append(resids[q])

    def project(q, dicts):
        shape = [f32(rows, width * len(dicts))]
        return call(project_kernel, shape, (acts[q], table, *dicts))[0]

    for step in range(steps + 1):
        at = [p for p in range(n_lat - 1) if 0 <= step - p < n_tok]
        pairs = []
        for p in at:
            pairs.append((2 * p, 2 * (p + 1)))
            pairs.append((2 * (n_lat - 1 - p) + 1, 2 * (n_lat - 2 - p) + 1))
        if step == 0:
            acts[order[0]] = call(round_kernel, [bf16(rows, lats)], (act,))[0]
            for side, dict_ref in enumerate((dict_here, dict_other)):
                message = project(order[0], (dict_ref,))
                sums[side].append((message, 0))
                got[side].append((lax.ppermute(message, ("lat", "wid"), pairs), 0))
                sent = [message]
        elif step < steps:
            for side in range(2):
                items = [got[side][-1], *[sums[side][step - p] for p in at]]
                message = call(
                    functools.partial(message_kernel, at, [col for _, col in items]),
                    [f32(rows, width)],
                    [array for array, _ in items],
                    after=sent + (waits[step] if side == 0 else []) if step > 1 else (),
                )[0]
                got[side].append((lax.ppermute(message, ("lat", "wid"), pairs), 0))
                sent = [message]
        if step + 1 < n_tok:
            q = order[step + 1]
            acts[q] = call(round_kernel, [bf16(rows, lats)], (gathered[q],), after=sent)[0]
            for side, dict_ref in enumerate((dict_here, dict_other)):
                sums[side].append((project(q, (dict_ref,)), 0))
        ready = []
        c = step - (n_lat - 1)
        if c >= 0:
            chosen = []
            for side in (1, 0) if step < steps else (0, 1):
                items = [got[side][c + p - 1] for p in places]
                if n_lat > 4:
                    items = [a[:, col * width : (col + 1) * width] for a, col in items]
                    items = [(pick(place_in_chain(), dict(zip(places, items))), 0)]
                chosen.append(
                    call(
                        functools.partial(choose_kernel, places, [col for _, col in items]),
                        [f32(rows, width)],
                        [array for array, _ in items],
                        after=sent if step < steps else ready_before + chosen,
                    )[0]
                )
            hand, mine = chosen if step < steps else chosen[::-1]
            hands.append((swap(hand), mine))
            ready += chosen
        stages = [c - 1] if step < steps else [c - 1, c]
        for c in stages:
            if c < 0:
                continue
            q = order[c]
            errs[q], keep, give, loss_here = call(
                functools.partial(error_kernel, len(loss)),
                [bf16(count, rows, width)] + [f32(rows // 2, lats)] * 2 + [f32(LOSS_ROWS, BLOCK)],
                (acts[q], dict_here, resids[q], bias_here, table, hands[c][1], hands[c][0], *loss),
                after=sent if step < steps else (),
            )
            loss = (loss_here,)
            gives.append((keep, swap(give)))
            ready.append(errs[q])
        stages = [1] if step == steps - 1 else [0, *range(2, n_tok)] if step == steps else []
        for c in stages:
            if c < 0:
                continue
            q = order[c]
            added = call(
                collect_kernel, [f32(rows // 2, lats)], gives[c], after=sent if step < steps else ()
            )[0]
            gacts.append(across(added, q) if q else added)
            ready.append(added)
        if step + 1 < steps:
            waits[step + 1] += ready
        ready_before = ready

    loss, gap = loss[0], 1
    while gap < n_lat:
        other = lax.ppermute(loss, "lat", [(p, p ^ gap) for p in range(n_lat)])
        loss = call(add_kernel, [f32(*loss.shape)], (loss, other))[0]
        gap *= 2

    decoded = call(
        decode_kernel,
        [f32(width, lats)],
        (*[errs[q] for q in order], *[acts[q] for q in order]),
    )[0]
    g_pre = call(
        g_pre_kernel,
        [f32(rows // 2 * count + LOSS_ROWS, BLOCK)],
        (pre, mask, loss, *gacts),
        after=(decoded,),
    )[0]
    mine = [across(g_pre, q) if q else g_pre for q in range(n_tok)]
    others = [swap(g) for g in mine]
    early = [(q, side) for side in range(2) for q in range(n_tok) if (q, side) != (1, 1)]
    halves = [mine, others]
    early_grads = [halves[side][q] for q, side in early]
    encoded = call(
        functools.partial(encode_kernel, (n_tok, early)),
        [f32(width, lats)],
        (*resids, *early_grads, decoded),
    )[0]
    grad, losses = call(
        functools.partial(
            last_kernel, (1, [(0, 1)]), 1.0 / (rows * n_tok * half * n_wid), len(early)
        ),
        [bf16(width, lats), f32(LEVELS)],
        (*early_grads, resids[1], others[1], encoded),
        out_specs=[VMEM, SMEM],
    )
    return (losses, grad)


def solution(mesh):
    return jax.shard_map(
        body,
        mesh=mesh,
        in_specs=(P("tok", "wid"), P("lat", "wid"), P("lat"), P("wid"), P("tok", None), P()),
        out_specs=(P(), P(("wid", "tok"), "lat")),
        check_vma=False,
    )
```

```python
import functools

import jax
import jax.numpy as jnp
from jax import lax
from jax.experimental import pallas as pl
from jax.experimental.pallas import tpu as pltpu
from jax.sharding import PartitionSpec as P

LEVELS = 4
BLOCK = 128
LOSS_ROWS = 8
GELU_C = 0.7978845608028654
GELU_A = 0.044715

VMEM = pl.BlockSpec(memory_space=pltpu.VMEM)
SMEM = pl.BlockSpec(memory_space=pltpu.SMEM)
HBM = pl.BlockSpec(memory_space=pltpu.HBM)
ANY = pl.BlockSpec(memory_space=pl.ANY)


def f32(*shape):
    return jax.ShapeDtypeStruct(shape, jnp.float32)


def bf16(*shape):
    return jax.ShapeDtypeStruct(shape, jnp.bfloat16)


def call(kernel, outs, arrays, after=(), specs=None, out_specs=None, scratch=()):
    skip = slice(len(arrays), len(arrays) + len(after))

    def run(*refs):
        kernel(*refs[: skip.start], *refs[skip.stop :])

    return pl.pallas_call(
        run,
        out_shape=outs,
        in_specs=list(specs or [VMEM] * len(arrays)) + [ANY] * len(after),
        out_specs=out_specs or [VMEM] * len(outs),
        scratch_shapes=list(scratch),
        compiler_params=pltpu.CompilerParams(vmem_limit_bytes=12 * 1024 * 1024),
        cost_estimate=pl.CostEstimate(flops=0, bytes_accessed=1 << 10, transcendentals=0),
    )(*arrays, *after)


def in_hbm(array):
    return pltpu.with_memory_space_constraint(array, pltpu.HBM)


def total_of(terms):
    return functools.reduce(jnp.add, terms)


def place_in_chain():
    lat = lax.axis_index("lat")
    return jnp.where(lax.axis_index("wid") == 0, lat, lax.axis_size("lat") - 1 - lat)


def level_table(bounds, count, out):
    lasts = bounds[...] - 1 - lax.axis_index("lat") * count
    upward = lax.axis_index("wid") == 0

    def put(row, value):
        out[row : row + 1, :] = jnp.broadcast_to(value, (1, BLOCK))

    for i in range(count):
        hits = (jnp.minimum(lasts, count - 1) == i).astype(jnp.float32)
        ending = jnp.sum(hits, axis=1, keepdims=True)
        put(i, ending)
        put(count + i, jnp.where(upward, jnp.full_like(ending, float(i == count - 1)), ending))
    for m in range(LEVELS):
        for i in range(count):
            put((2 + m) * count + i, (lasts[:, m : m + 1] == i).astype(jnp.float32))


def pre_kernel(resid, dictionary, partial_out, dict_out, resid_v, dict_v, sems):
    pieces, _, width = dict_v.shape
    copies = []
    for i in range(pieces):
        cols = pl.ds(i * width, width)
        copies.append(
            (
                pltpu.make_async_copy(resid.at[:, cols], resid_v.at[i], sems.at[0, i]),
                pltpu.make_async_copy(dictionary.at[:, cols], dict_v.at[i], sems.at[1, i]),
            )
        )
        for copy in copies[-1]:
            copy.start()
    total = None
    for i in range(pieces):
        for copy in copies[i]:
            copy.wait()
        term = lax.dot_general(
            dict_v[i], resid_v[i], (((1,), (1,)), ((), ())), preferred_element_type=jnp.float32
        )
        total = term if total is None else total + term
    partial_out[...] = total.T
    parts = dict_out.shape[1] // width
    for i in range(parts):
        dict_out[:, i * width : (i + 1) * width] = dict_v[lax.axis_index("tok") * parts + i]


def widen_kernel(array, bounds, out, table_out):
    out[...] = array[...].astype(jnp.float32)
    level_table(bounds, array.shape[0] // BLOCK, table_out)


def pieces_kernel(resid, bias, bias_out, *outs):
    width = outs[0].shape[1]
    tok = lax.axis_index("tok")

    def cols(t):
        return pl.ds(pl.multiple_of(t * width, width), width)

    bias_out[...] = bias[:, cols(tok)]
    for q, out in enumerate(outs):
        out[...] = resid[:, cols(tok ^ q)].astype(jnp.float32)


def block_mask(active, lats):
    count = lats // BLOCK
    ids = lax.axis_index("lat") * count + lax.broadcasted_iota(jnp.int32, (count, 1), 0)
    hits = total_of([(active[q : q + 1, :] == ids).astype(jnp.float32) for q in range(active.shape[0])])
    spread = lax.broadcasted_iota(jnp.int32, (count, lats), 1) // BLOCK
    spread = (spread == lax.broadcasted_iota(jnp.int32, (count, lats), 0)).astype(jnp.bfloat16)
    return lax.dot_general(
        hits.astype(jnp.bfloat16),
        spread,
        (((0,), (0,)), ((), ())),
        preferred_element_type=jnp.float32,
    )


def activate_kernel(mine, other, bias, active, pre_out, act_out, mask_out):
    pre = mine[...] + other[...] + bias[...]
    pre_out[...] = pre
    inner = GELU_C * (pre + GELU_A * (pre * pre * pre))
    gelu = 0.5 * pre * (1.0 + jnp.tanh(inner))
    mask = block_mask(active[...], pre.shape[1])
    mask_out[...] = mask
    act_out[...] = jnp.where(mask > 0.0, gelu, 0.0)


def half_of(wid, rows):
    return pl.ds(pl.multiple_of(wid * (rows // 2), rows // 2), rows // 2)


def stacked(parts, extra, out):
    rows, cols = parts.shape
    for i in range(cols // BLOCK):
        out[i * rows : (i + 1) * rows, :] = parts[:, i * BLOCK : (i + 1) * BLOCK]
    out[-LOSS_ROWS:, :] = extra


def unstacked(ref, count):
    rows = (ref.shape[0] - LOSS_ROWS) // count
    return jnp.concatenate([ref[i * rows : (i + 1) * rows, :] for i in range(count)], axis=1)


def g_pre_kernel(pre_ref, mask, loss, *refs):
    terms, out = refs[:-1], refs[-1]
    mine = half_of(lax.axis_index("wid"), pre_ref.shape[0])
    pre = pre_ref[mine, :]
    inner = GELU_C * (pre + GELU_A * (pre * pre * pre))
    slope = GELU_C * (1.0 + 3.0 * GELU_A * (pre * pre))
    bend = jnp.tanh(inner)
    deriv = 0.5 * (1.0 + bend) + 0.5 * pre * (1.0 - bend * bend) * slope
    hit = mask[mine, :] > 0.0
    stacked(jnp.where(hit, deriv * total_of([t[...] for t in terms]), 0.0), loss[...], out)


def running_parts(act, dict_ref):
    sums = []
    for i in range(dict_ref.shape[0] // BLOCK):
        span = slice(i * BLOCK, (i + 1) * BLOCK)
        part = jnp.dot(
            act[:, span], dict_ref[span, :].astype(jnp.bfloat16), preferred_element_type=jnp.float32
        )
        sums.append(sums[-1] + part if sums else part)
    return sums


def round_kernel(act, out):
    out[...] = act[...].astype(jnp.bfloat16)


def project_kernel(act, table, *refs):
    dicts, out = refs[:-1], refs[-1]
    for side, dictionary in enumerate(dicts):
        sums = running_parts(act[...], dictionary)
        count = len(sums)
        width = dictionary.shape[1]
        out[:, side * width : (side + 1) * width] = total_of(
            [table[count + i : count + i + 1, :1] * s for i, s in enumerate(sums)]
        )


def columns(ref, col, width):
    return ref[:, col * width : (col + 1) * width]


def message_kernel(places, cols, got, *refs):
    out = refs[-1]
    width = out.shape[1]
    index = place_in_chain()
    for place, piece, col in zip(places, refs[:-1], cols[1:]):

        @pl.when(index == place)
        def _():
            own = columns(piece, col, width)
            out[...] = own + columns(got, cols[0], width) if place else own


def choose_kernel(places, cols, *refs):
    arrived, out = refs[:-1], refs[-1]
    index = place_in_chain()

    @pl.when(index == 0)
    def _():
        out[...] = jnp.zeros_like(out)

    for place, ref, col in zip(places, arrived, cols):

        @pl.when(index == place if len(arrived) > 1 else index > 0)
        def _():
            out[...] = columns(ref, col, out.shape[1])


def square_sums(table, shifted):
    count = len(shifted)
    squares = []
    for v in shifted:
        lanes = jnp.sum(v * v, axis=0, keepdims=True)
        squares.append(total_of([lanes[:, i : i + BLOCK] for i in range(0, lanes.shape[1], BLOCK)]))
    rows = []
    for m in range(LEVELS):
        at = (2 + m) * count
        rows.append(total_of([table[at + i : at + i + 1, :] * s for i, s in enumerate(squares)]))
    return jnp.concatenate(rows + [jnp.zeros((LOSS_ROWS - LEVELS, BLOCK), jnp.float32)], axis=0)


def error_kernel(loss_count, act, dictionary, resid, bias, table, mine, other, *refs):
    before, refs = refs[:loss_count], refs[loss_count:]
    err_out, keep_out, give_out, loss_out = refs
    upward = lax.axis_index("wid") == 0
    earlier = jnp.where(upward, mine[...], other[...])
    later = jnp.where(upward, other[...], mine[...])
    base = bias[...] - resid[...] + earlier
    sums = running_parts(act[...], dictionary)
    shifted = [base + s for s in sums]
    loss_out[...] = total_of([square_sums(table, shifted)] + [b[...] for b in before])
    err = later
    for i in reversed(range(len(sums))):
        err = err + table[i : i + 1, :1] * shifted[i]
        rounded = err.astype(jnp.bfloat16)
        err_out[i] = rounded
        cols = slice(i * BLOCK, (i + 1) * BLOCK)
        gact = lax.dot_general(
            rounded,
            dictionary[cols, :],
            (((1,), (1,)), ((), ())),
            preferred_element_type=jnp.float32,
        )
        half = gact.shape[0] // 2
        keep_out[:, cols] = jnp.where(upward, gact[:half, :], gact[half:, :])
        give_out[:half, cols] = jnp.where(upward, gact[half:, :], gact[:half, :])
    if give_out.shape[0] > half:
        give_out[half:, :] = jnp.zeros_like(give_out[half:, :])
        give_out[half:, :BLOCK] = loss_out[...]


def collect_kernel(keep, give, out):
    out[...] = keep[...] + give[: keep.shape[0], :]


def chip_losses_kernel(loss, give, out):
    total = loss[...] + give[-LOSS_ROWS:, :BLOCK]
    out[...] = jnp.where(lax.axis_index("wid") == 1, total, 0.0)


def add_kernel(*refs):
    refs[-1][...] = total_of([ref[...] for ref in refs[:-1]])


def decode_kernel(*refs):
    n = (len(refs) - 1) // 2
    errs, acts, out = refs[:n], refs[n : 2 * n], refs[-1]
    for i in range(errs[0].shape[0]):
        cols = slice(i * BLOCK, (i + 1) * BLOCK)
        err = jnp.concatenate([e[i] for e in errs], axis=0)
        act = jnp.concatenate([a[:, cols] for a in acts], axis=0)
        out[:, cols] = lax.dot_general(
            err, act, (((0,), (0,)), ((), ())), preferred_element_type=jnp.float32
        )


def encode_kernel(items, *refs):
    n, halves = items
    resids, grads, base, out = refs[:n], refs[n:-2], refs[-2], refs[-1]
    half = resids[0].shape[0] // 2
    count = out.shape[1] // BLOCK
    wid = lax.axis_index("wid")
    spans = [half_of(wid, 2 * half), half_of(1 - wid, 2 * half)]
    resid = jnp.concatenate(
        [resids[q][spans[side], :].astype(jnp.bfloat16) for q, side in halves], axis=0
    )
    grad = jnp.concatenate([unstacked(g, count).astype(jnp.bfloat16) for g in grads], axis=0)
    total = base[...] + lax.dot_general(
        resid, grad, (((0,), (0,)), ((), ())), preferred_element_type=jnp.float32
    )
    out[...] = total.astype(out.dtype)


def last_kernel(items, scale, n_early, *refs):
    *refs, out, loss_out = refs
    early, refs = refs[:n_early], refs[n_early:]
    encode_kernel(items, *refs, out)
    grads = list(early) + list(refs[items[0] : -1])
    lanes = total_of([g[-LOSS_ROWS:, :] for g in grads])
    for m in range(LEVELS):
        loss_out[m] = jnp.sum(lanes[m : m + 1, :]) * scale


def pick(index, choices):
    values = sorted(choices)
    result = choices[values[0]]
    for value in values[1:]:
        result = jnp.where(index == value, choices[value], result)
    return result


def body(resid, dictionary, enc_bias, dec_bias, active_blocks, level_bounds):
    rows, half = resid.shape
    lats = dictionary.shape[0]
    n_lat, n_wid, n_tok = lax.axis_size("lat"), lax.axis_size("wid"), lax.axis_size("tok")
    width = half // n_tok
    count = lats // BLOCK

    def across(array, q):
        return lax.ppermute(array, "tok", [(t, t ^ q) for t in range(n_tok)])

    def swap(array):
        return lax.ppermute(array, "wid", [(w, w ^ 1) for w in range(n_wid)])

    partial, dict_here = call(
        pre_kernel,
        [f32(rows, lats), bf16(lats, width)],
        (in_hbm(resid), in_hbm(dictionary)),
        specs=[HBM, HBM],
        scratch=[
            pltpu.VMEM((2 * n_tok, rows, width // 2), jnp.bfloat16),
            pltpu.VMEM((2 * n_tok, lats, width // 2), jnp.bfloat16),
            pltpu.SemaphoreType.DMA((2, 2 * n_tok)),
        ],
    )
    partial_other = swap(partial)
    dict_wide, table = call(
        widen_kernel,
        [f32(lats, width), f32((2 + LEVELS) * count, BLOCK)],
        (dict_here, level_bounds.reshape(1, LEVELS)),
        after=(partial_other,),
    )
    dict_other = swap(dict_wide)
    pre, act, mask = call(
        activate_kernel,
        [f32(rows, lats)] * 3,
        (partial, partial_other, enc_bias.reshape(1, lats), active_blocks.T),
        after=(dict_wide,),
    )
    gathered = [act] + [across(act, q) for q in range(1, n_tok)]
    bias_here, *pieces = call(
        pieces_kernel,
        [f32(1, width)] + [f32(rows, width)] * n_tok,
        (resid, dec_bias.reshape(1, half)),
        after=(act,),
    )
    resids = [piece if q == 0 else across(piece, q) for q, piece in enumerate(pieces)]

    order = [0, 1, 3, 2] if n_tok == 4 else list(range(n_tok))
    steps = n_tok + n_lat - 2
    places = list(range(1, n_lat))
    acts, errs, hands, gives, gacts, loss = {}, {}, [], [], [], ()
    sums, got, sent = ([], []), ([], []), []
    waits = {step: [] for step in range(steps)}
    for place, q in enumerate(order[1:]):
        waits[min(3 + place, steps - 1)].append(resids[q])

    def project(q, dicts):
        shape = [f32(rows, width * len(dicts))]
        return call(project_kernel, shape, (acts[q], table, *dicts))[0]

    for step in range(steps + 1):
        at = [p for p in range(n_lat - 1) if 0 <= step - p < n_tok]
        pairs = []
        for p in at:
            pairs.append((2 * p, 2 * (p + 1)))
            pairs.append((2 * (n_lat - 1 - p) + 1, 2 * (n_lat - 2 - p) + 1))
        if step == 0:
            acts[order[0]] = call(round_kernel, [bf16(rows, lats)], (act,))[0]
            for side, dict_ref in enumerate((dict_here, dict_other)):
                message = project(order[0], (dict_ref,))
                sums[side].append((message, 0))
                got[side].append((lax.ppermute(message, ("lat", "wid"), pairs), 0))
                sent = [message]
        elif step < steps:
            for side in range(2):
                items = [got[side][-1], *[sums[side][step - p] for p in at]]
                message = call(
                    functools.partial(message_kernel, at, [col for _, col in items]),
                    [f32(rows, width)],
                    [array for array, _ in items],
                    after=sent + (waits[step] if side == 0 else []) if step > 1 else (),
                )[0]
                got[side].append((lax.ppermute(message, ("lat", "wid"), pairs), 0))
                sent = [message]
        if step + 1 < n_tok:
            q = order[step + 1]
            acts[q] = call(round_kernel, [bf16(rows, lats)], (gathered[q],), after=sent)[0]
            for side, dict_ref in enumerate((dict_here, dict_other)):
                sums[side].append((project(q, (dict_ref,)), 0))
        ready = []
        c = step - (n_lat - 1)
        if c >= 0:
            chosen = []
            for side in (1, 0) if step < steps else (0, 1):
                items = [got[side][c + p - 1] for p in places]
                if n_lat > 4:
                    items = [a[:, col * width : (col + 1) * width] for a, col in items]
                    items = [(pick(place_in_chain(), dict(zip(places, items))), 0)]
                chosen.append(
                    call(
                        functools.partial(choose_kernel, places, [col for _, col in items]),
                        [f32(rows, width)],
                        [array for array, _ in items],
                        after=sent if step < steps else ready_before + chosen,
                    )[0]
                )
            hand, mine = chosen if step < steps else chosen[::-1]
            hands.append((swap(hand), mine))
            ready += chosen
        stages = [c - 1] if step < steps else [c - 1, c]
        for c in stages:
            if c < 0:
                continue
            q = order[c]
            errs[q], keep, give, loss_here = call(
                functools.partial(error_kernel, len(loss)),
                [
                    bf16(count, rows, width),
                    f32(rows // 2, lats),
                    f32(rows // 2 + (LOSS_ROWS if c == n_tok - 1 else 0), lats),
                    f32(LOSS_ROWS, BLOCK),
                ],
                (acts[q], dict_here, resids[q], bias_here, table, hands[c][1], hands[c][0], *loss),
                after=sent if step < steps else (),
            )
            loss = (loss_here,)
            gives.append((keep, swap(give)))
            ready.append(errs[q])
        stages = [1] if step == steps - 1 else [0, *range(2, n_tok)] if step == steps else []
        for c in stages:
            if c < 0:
                continue
            q = order[c]
            added = call(
                collect_kernel, [f32(rows // 2, lats)], gives[c], after=sent if step < steps else ()
            )[0]
            gacts.append(across(added, q) if q else added)
            ready.append(added)
        if step + 1 < steps:
            waits[step + 1] += ready
        ready_before = ready

    loss = call(chip_losses_kernel, [f32(LOSS_ROWS, BLOCK)], (loss[0], gives[-1][1]))[0]
    gap = 1
    while gap < n_lat:
        pairs = [(2 * p + 1, 2 * (p ^ gap) + 1) for p in range(n_lat)]
        other = lax.ppermute(loss, ("lat", "wid"), pairs)
        loss = call(add_kernel, [f32(*loss.shape)], (loss, other))[0]
        gap *= 2

    decoded = call(
        decode_kernel,
        [f32(width, lats)],
        (*[errs[q] for q in order], *[acts[q] for q in order]),
    )[0]
    g_pre = call(
        g_pre_kernel,
        [f32(rows // 2 * count + LOSS_ROWS, BLOCK)],
        (pre, mask, loss, *gacts),
        after=(decoded,),
    )[0]
    mine = [across(g_pre, q) if q else g_pre for q in range(n_tok)]
    others = [swap(g) for g in mine]
    early = [(q, side) for side in range(2) for q in range(n_tok) if (q, side) != (1, 1)]
    halves = [mine, others]
    early_grads = [halves[side][q] for q, side in early]
    encoded = call(
        functools.partial(encode_kernel, (n_tok, early)),
        [f32(width, lats)],
        (*resids, *early_grads, decoded),
    )[0]
    grad, losses = call(
        functools.partial(
            last_kernel, (1, [(0, 1)]), 1.0 / (rows * n_tok * half * n_wid), len(early)
        ),
        [bf16(width, lats), f32(LEVELS)],
        (*early_grads, resids[1], others[1], encoded),
        out_specs=[VMEM, SMEM],
    )
    return (losses, grad)


def solution(mesh):
    return jax.shard_map(
        body,
        mesh=mesh,
        in_specs=(P("tok", "wid"), P("lat", "wid"), P("lat"), P("wid"), P("tok", None), P()),
        out_specs=(P(), P(("wid", "tok"), "lat")),
        check_vma=False,
    )
```

```python
import functools

import jax
import jax.numpy as jnp
from jax import lax
from jax.experimental import pallas as pl
from jax.experimental.pallas import tpu as pltpu
from jax.sharding import PartitionSpec as P

LEVELS = 4
BLOCK = 128
LOSS_ROWS = 8
LOSS_AREA = 128
GELU_C = 0.7978845608028654
GELU_A = 0.044715

VMEM = pl.BlockSpec(memory_space=pltpu.VMEM)
SMEM = pl.BlockSpec(memory_space=pltpu.SMEM)
HBM = pl.BlockSpec(memory_space=pltpu.HBM)
ANY = pl.BlockSpec(memory_space=pl.ANY)


def f32(*shape):
    return jax.ShapeDtypeStruct(shape, jnp.float32)


def bf16(*shape):
    return jax.ShapeDtypeStruct(shape, jnp.bfloat16)


def call(kernel, outs, arrays, after=(), specs=None, out_specs=None, scratch=()):
    skip = slice(len(arrays), len(arrays) + len(after))

    def run(*refs):
        kernel(*refs[: skip.start], *refs[skip.stop :])

    return pl.pallas_call(
        run,
        out_shape=outs,
        in_specs=list(specs or [VMEM] * len(arrays)) + [ANY] * len(after),
        out_specs=out_specs or [VMEM] * len(outs),
        scratch_shapes=list(scratch),
        compiler_params=pltpu.CompilerParams(vmem_limit_bytes=12 * 1024 * 1024),
        cost_estimate=pl.CostEstimate(flops=0, bytes_accessed=1 << 10, transcendentals=0),
    )(*arrays, *after)


def in_hbm(array):
    return pltpu.with_memory_space_constraint(array, pltpu.HBM)


def total_of(terms):
    return functools.reduce(jnp.add, terms)


def place_in_chain():
    lat = lax.axis_index("lat")
    return jnp.where(lax.axis_index("wid") == 0, lat, lax.axis_size("lat") - 1 - lat)


def level_table(bounds, count, out):
    lasts = bounds[...] - 1 - lax.axis_index("lat") * count
    upward = lax.axis_index("wid") == 0

    def put(row, value):
        out[row : row + 1, :] = jnp.broadcast_to(value, (1, BLOCK))

    for i in range(count):
        hits = (jnp.minimum(lasts, count - 1) == i).astype(jnp.float32)
        ending = jnp.sum(hits, axis=1, keepdims=True)
        put(i, ending)
        put(count + i, jnp.where(upward, jnp.full_like(ending, float(i == count - 1)), ending))
    for m in range(LEVELS):
        for i in range(count):
            put((2 + m) * count + i, (lasts[:, m : m + 1] == i).astype(jnp.float32))


def pre_kernel(resid, dictionary, partial_out, dict_out, resid_v, dict_v, sems):
    pieces, _, width = dict_v.shape
    copies = []
    for i in range(pieces):
        cols = pl.ds(i * width, width)
        copies.append(
            (
                pltpu.make_async_copy(resid.at[:, cols], resid_v.at[i], sems.at[0, i]),
                pltpu.make_async_copy(dictionary.at[:, cols], dict_v.at[i], sems.at[1, i]),
            )
        )
        for copy in copies[-1]:
            copy.start()
    total = None
    for i in range(pieces):
        for copy in copies[i]:
            copy.wait()
        term = lax.dot_general(
            dict_v[i], resid_v[i], (((1,), (1,)), ((), ())), preferred_element_type=jnp.float32
        )
        total = term if total is None else total + term
    partial_out[...] = total.T
    parts = dict_out.shape[1] // width
    for i in range(parts):
        dict_out[:, i * width : (i + 1) * width] = dict_v[lax.axis_index("tok") * parts + i]


def widen_kernel(array, bounds, out, table_out):
    out[...] = array[...].astype(jnp.float32)
    level_table(bounds, array.shape[0] // BLOCK, table_out)


def pieces_kernel(resid, bias, bias_out, *outs):
    width = outs[0].shape[1]
    tok = lax.axis_index("tok")

    def cols(t):
        return pl.ds(pl.multiple_of(t * width, width), width)

    bias_out[...] = bias[:, cols(tok)]
    for q, out in enumerate(outs):
        out[...] = resid[:, cols(tok ^ q)].astype(jnp.float32)


def block_mask(active, lats):
    count = lats // BLOCK
    ids = lax.axis_index("lat") * count + lax.broadcasted_iota(jnp.int32, (count, 1), 0)
    hits = total_of([(active[q : q + 1, :] == ids).astype(jnp.float32) for q in range(active.shape[0])])
    spread = lax.broadcasted_iota(jnp.int32, (count, lats), 1) // BLOCK
    spread = (spread == lax.broadcasted_iota(jnp.int32, (count, lats), 0)).astype(jnp.bfloat16)
    return lax.dot_general(
        hits.astype(jnp.bfloat16),
        spread,
        (((0,), (0,)), ((), ())),
        preferred_element_type=jnp.float32,
    )


def activate_kernel(mine, other, bias, active, pre_out, act_out, mask_out):
    pre = mine[...] + other[...] + bias[...]
    pre_out[...] = pre
    inner = GELU_C * (pre + GELU_A * (pre * pre * pre))
    gelu = 0.5 * pre * (1.0 + jnp.tanh(inner))
    mask = block_mask(active[...], pre.shape[1])
    mask_out[...] = mask
    act_out[...] = jnp.where(mask > 0.0, gelu, 0.0)


def half_of(wid, rows):
    return pl.ds(pl.multiple_of(wid * (rows // 2), rows // 2), rows // 2)


def stacked(parts, extra, out):
    rows, cols = parts.shape
    for i in range(cols // BLOCK):
        out[i * rows : (i + 1) * rows, :] = parts[:, i * BLOCK : (i + 1) * BLOCK]
    out[-LOSS_ROWS:, :] = extra


def unstacked(ref, count):
    rows = (ref.shape[0] - LOSS_ROWS) // count
    return jnp.concatenate([ref[i * rows : (i + 1) * rows, :] for i in range(count)], axis=1)


def g_pre_kernel(pre_ref, mask, loss, *refs):
    terms, out = refs[:-1], refs[-1]
    mine = half_of(lax.axis_index("wid"), pre_ref.shape[0])
    pre = pre_ref[mine, :]
    inner = GELU_C * (pre + GELU_A * (pre * pre * pre))
    slope = GELU_C * (1.0 + 3.0 * GELU_A * (pre * pre))
    bend = jnp.tanh(inner)
    deriv = 0.5 * (1.0 + bend) + 0.5 * pre * (1.0 - bend * bend) * slope
    hit = mask[mine, :] > 0.0
    stacked(
        jnp.where(hit, deriv * total_of([t[...] for t in terms]), 0.0), loss[:LOSS_ROWS, :], out
    )


def running_parts(act, dict_ref):
    sums = []
    for i in range(dict_ref.shape[0] // BLOCK):
        span = slice(i * BLOCK, (i + 1) * BLOCK)
        part = jnp.dot(
            act[:, span], dict_ref[span, :].astype(jnp.bfloat16), preferred_element_type=jnp.float32
        )
        sums.append(sums[-1] + part if sums else part)
    return sums


def round_kernel(act, out):
    out[...] = act[...].astype(jnp.bfloat16)


def project_kernel(act, table, *refs):
    dicts, out = refs[:-1], refs[-1]
    for side, dictionary in enumerate(dicts):
        sums = running_parts(act[...], dictionary)
        count = len(sums)
        width = dictionary.shape[1]
        out[:, side * width : (side + 1) * width] = total_of(
            [table[count + i : count + i + 1, :1] * s for i, s in enumerate(sums)]
        )


def columns(ref, col, width):
    return ref[:, col * width : (col + 1) * width]


def message_kernel(places, cols, got, *refs):
    out = refs[-1]
    width = out.shape[1]
    index = place_in_chain()
    for place, piece, col in zip(places, refs[:-1], cols[1:]):

        @pl.when(index == place)
        def _():
            own = columns(piece, col, width)
            out[...] = own + columns(got, cols[0], width) if place else own


def choose_kernel(places, cols, *refs):
    arrived, out = refs[:-1], refs[-1]
    index = place_in_chain()

    @pl.when(index == 0)
    def _():
        out[...] = jnp.zeros_like(out)

    for place, ref, col in zip(places, arrived, cols):

        @pl.when(index == place if len(arrived) > 1 else index > 0)
        def _():
            out[...] = columns(ref, col, out.shape[1])


def square_sums(table, shifted):
    count = len(shifted)
    squares = []
    for v in shifted:
        lanes = jnp.sum(v * v, axis=0, keepdims=True)
        squares.append(total_of([lanes[:, i : i + BLOCK] for i in range(0, lanes.shape[1], BLOCK)]))
    rows = []
    for m in range(LEVELS):
        at = (2 + m) * count
        rows.append(total_of([table[at + i : at + i + 1, :] * s for i, s in enumerate(squares)]))
    return jnp.concatenate(rows + [jnp.zeros((LOSS_ROWS - LEVELS, BLOCK), jnp.float32)], axis=0)


def error_kernel(loss_count, act, dictionary, resid, bias, table, mine, other, *refs):
    before, refs = refs[:loss_count], refs[loss_count:]
    err_out, keep_out, give_out, loss_out = refs
    upward = lax.axis_index("wid") == 0
    earlier = jnp.where(upward, mine[...], other[...])
    later = jnp.where(upward, other[...], mine[...])
    base = bias[...] - resid[...] + earlier
    sums = running_parts(act[...], dictionary)
    shifted = [base + s for s in sums]
    loss_out[...] = total_of([square_sums(table, shifted)] + [b[...] for b in before])
    err = later
    for i in reversed(range(len(sums))):
        err = err + table[i : i + 1, :1] * shifted[i]
        rounded = err.astype(jnp.bfloat16)
        err_out[i] = rounded
        cols = slice(i * BLOCK, (i + 1) * BLOCK)
        gact = lax.dot_general(
            rounded,
            dictionary[cols, :],
            (((1,), (1,)), ((), ())),
            preferred_element_type=jnp.float32,
        )
        half = gact.shape[0] // 2
        keep_out[:, cols] = jnp.where(upward, gact[:half, :], gact[half:, :])
        give_out[:half, cols] = jnp.where(upward, gact[half:, :], gact[:half, :])
    if give_out.shape[0] > half:
        give_out[half:, :] = jnp.zeros_like(give_out[half:, :])
        give_out[half:, :BLOCK] = loss_out[...]


def collect_kernel(keep, give, out):
    out[...] = keep[...] + give[: keep.shape[0], :]


def chip_losses_kernel(loss, give, out):
    total = loss[...] + give[-LOSS_ROWS:, :BLOCK]
    out[...] = jnp.zeros_like(out)
    out[:LOSS_ROWS, :] = jnp.where(lax.axis_index("wid") == 1, total, 0.0)


def add_kernel(*refs):
    refs[-1][...] = total_of([ref[...] for ref in refs[:-1]])


def decode_kernel(*refs):
    n = (len(refs) - 1) // 2
    errs, acts, out = refs[:n], refs[n : 2 * n], refs[-1]
    for i in range(errs[0].shape[0]):
        cols = slice(i * BLOCK, (i + 1) * BLOCK)
        err = jnp.concatenate([e[i] for e in errs], axis=0)
        act = jnp.concatenate([a[:, cols] for a in acts], axis=0)
        out[:, cols] = lax.dot_general(
            err, act, (((0,), (0,)), ((), ())), preferred_element_type=jnp.float32
        )


def encode_kernel(items, *refs):
    n, halves = items
    resids, grads, base, out = refs[:n], refs[n:-2], refs[-2], refs[-1]
    half = resids[0].shape[0] // 2
    count = out.shape[1] // BLOCK
    wid = lax.axis_index("wid")
    spans = [half_of(wid, 2 * half), half_of(1 - wid, 2 * half)]
    resid = jnp.concatenate(
        [resids[q][spans[side], :].astype(jnp.bfloat16) for q, side in halves], axis=0
    )
    grad = jnp.concatenate([unstacked(g, count).astype(jnp.bfloat16) for g in grads], axis=0)
    total = base[...] + lax.dot_general(
        resid, grad, (((0,), (0,)), ((), ())), preferred_element_type=jnp.float32
    )
    out[...] = total.astype(out.dtype)


def last_kernel(items, scale, n_early, *refs):
    *refs, out, loss_out = refs
    early, refs = refs[:n_early], refs[n_early:]
    encode_kernel(items, *refs, out)
    grads = list(early) + list(refs[items[0] : -1])
    lanes = total_of([g[-LOSS_ROWS:, :] for g in grads])
    for m in range(LEVELS):
        loss_out[m] = jnp.sum(lanes[m : m + 1, :]) * scale


def pick(index, choices):
    values = sorted(choices)
    result = choices[values[0]]
    for value in values[1:]:
        result = jnp.where(index == value, choices[value], result)
    return result


def body(resid, dictionary, enc_bias, dec_bias, active_blocks, level_bounds):
    rows, half = resid.shape
    lats = dictionary.shape[0]
    n_lat, n_wid, n_tok = lax.axis_size("lat"), lax.axis_size("wid"), lax.axis_size("tok")
    width = half // n_tok
    count = lats // BLOCK

    def across(array, q):
        return lax.ppermute(array, "tok", [(t, t ^ q) for t in range(n_tok)])

    def swap(array):
        return lax.ppermute(array, "wid", [(w, w ^ 1) for w in range(n_wid)])

    partial, dict_here = call(
        pre_kernel,
        [f32(rows, lats), bf16(lats, width)],
        (in_hbm(resid), in_hbm(dictionary)),
        specs=[HBM, HBM],
        scratch=[
            pltpu.VMEM((2 * n_tok, rows, width // 2), jnp.bfloat16),
            pltpu.VMEM((2 * n_tok, lats, width // 2), jnp.bfloat16),
            pltpu.SemaphoreType.DMA((2, 2 * n_tok)),
        ],
    )
    partial_other = swap(partial)
    dict_wide, table = call(
        widen_kernel,
        [f32(lats, width), f32((2 + LEVELS) * count, BLOCK)],
        (dict_here, level_bounds.reshape(1, LEVELS)),
        after=(partial_other,),
    )
    dict_other = swap(dict_wide)
    pre, act, mask = call(
        activate_kernel,
        [f32(rows, lats)] * 3,
        (partial, partial_other, enc_bias.reshape(1, lats), active_blocks.T),
        after=(dict_wide,),
    )
    gathered = [act] + [across(act, q) for q in range(1, n_tok)]
    bias_here, *pieces = call(
        pieces_kernel,
        [f32(1, width)] + [f32(rows, width)] * n_tok,
        (resid, dec_bias.reshape(1, half)),
        after=(act,),
    )
    resids = [piece if q == 0 else across(piece, q) for q, piece in enumerate(pieces)]

    order = [0, 1, 3, 2] if n_tok == 4 else list(range(n_tok))
    steps = n_tok + n_lat - 2
    places = list(range(1, n_lat))
    acts, errs, hands, gives, gacts, loss = {}, {}, [], [], [], ()
    sums, got, sent = ([], []), ([], []), []
    waits = {step: [] for step in range(steps)}
    for place, q in enumerate(order[1:]):
        waits[min(3 + place, steps - 1)].append(resids[q])

    def project(q, dicts):
        shape = [f32(rows, width * len(dicts))]
        return call(project_kernel, shape, (acts[q], table, *dicts))[0]

    for step in range(steps + 1):
        at = [p for p in range(n_lat - 1) if 0 <= step - p < n_tok]
        pairs = []
        for p in at:
            pairs.append((2 * p, 2 * (p + 1)))
            pairs.append((2 * (n_lat - 1 - p) + 1, 2 * (n_lat - 2 - p) + 1))
        if step == 0:
            acts[order[0]] = call(round_kernel, [bf16(rows, lats)], (act,))[0]
            for side, dict_ref in enumerate((dict_here, dict_other)):
                message = project(order[0], (dict_ref,))
                sums[side].append((message, 0))
                got[side].append((lax.ppermute(message, ("lat", "wid"), pairs), 0))
                sent = [message]
        elif step < steps:
            for side in range(2):
                items = [got[side][-1], *[sums[side][step - p] for p in at]]
                message = call(
                    functools.partial(message_kernel, at, [col for _, col in items]),
                    [f32(rows, width)],
                    [array for array, _ in items],
                    after=sent + (waits[step] if side == 0 else []) if step > 1 else (),
                )[0]
                got[side].append((lax.ppermute(message, ("lat", "wid"), pairs), 0))
                sent = [message]
        if step + 1 < n_tok:
            q = order[step + 1]
            acts[q] = call(round_kernel, [bf16(rows, lats)], (gathered[q],), after=sent)[0]
            for side, dict_ref in enumerate((dict_here, dict_other)):
                sums[side].append((project(q, (dict_ref,)), 0))
        ready = []
        c = step - (n_lat - 1)
        if c >= 0:
            chosen = []
            for side in (1, 0) if step < steps else (0, 1):
                items = [got[side][c + p - 1] for p in places]
                if n_lat > 4:
                    items = [a[:, col * width : (col + 1) * width] for a, col in items]
                    items = [(pick(place_in_chain(), dict(zip(places, items))), 0)]
                chosen.append(
                    call(
                        functools.partial(choose_kernel, places, [col for _, col in items]),
                        [f32(rows, width)],
                        [array for array, _ in items],
                        after=sent if step < steps else ready_before + chosen,
                    )[0]
                )
            hand, mine = chosen if step < steps else chosen[::-1]
            hands.append((swap(hand), mine))
            ready += chosen
        stages = [c - 1] if step < steps else [c - 1, c]
        for c in stages:
            if c < 0:
                continue
            q = order[c]
            errs[q], keep, give, loss_here = call(
                functools.partial(error_kernel, len(loss)),
                [
                    bf16(count, rows, width),
                    f32(rows // 2, lats),
                    f32(rows // 2 + (LOSS_ROWS if c == n_tok - 1 else 0), lats),
                    f32(LOSS_ROWS, BLOCK),
                ],
                (acts[q], dict_here, resids[q], bias_here, table, hands[c][1], hands[c][0], *loss),
                after=sent if step < steps else (),
            )
            loss = (loss_here,)
            gives.append((keep, swap(give)))
            ready.append(errs[q])
        stages = [1] if step == steps - 1 else [0, *range(2, n_tok)] if step == steps else []
        for c in stages:
            if c < 0:
                continue
            q = order[c]
            added = call(
                collect_kernel, [f32(rows // 2, lats)], gives[c], after=sent if step < steps else ()
            )[0]
            gacts.append(across(added, q) if q else added)
            ready.append(added)
        if step + 1 < steps:
            waits[step + 1] += ready
        ready_before = ready

    loss = call(chip_losses_kernel, [f32(LOSS_AREA, BLOCK)], (loss[0], gives[-1][1]))[0]
    gap = 1
    while gap < n_lat:
        pairs = [(2 * p + 1, 2 * (p ^ gap) + 1) for p in range(n_lat)]
        other = lax.ppermute(loss, ("lat", "wid"), pairs)
        loss = call(add_kernel, [f32(*loss.shape)], (loss, other))[0]
        gap *= 2

    decoded = call(
        decode_kernel,
        [f32(width, lats)],
        (*[errs[q] for q in order], *[acts[q] for q in order]),
    )[0]
    g_pre = call(
        g_pre_kernel,
        [f32(rows // 2 * count + LOSS_ROWS, BLOCK)],
        (pre, mask, loss, *gacts),
        after=(decoded,),
    )[0]
    mine = [across(g_pre, q) if q else g_pre for q in range(n_tok)]
    others = [swap(g) for g in mine]
    early = [(q, side) for side in range(2) for q in range(n_tok) if (q, side) != (1, 1)]
    halves = [mine, others]
    early_grads = [halves[side][q] for q, side in early]
    encoded = call(
        functools.partial(encode_kernel, (n_tok, early)),
        [f32(width, lats)],
        (*resids, *early_grads, decoded),
    )[0]
    grad, losses = call(
        functools.partial(
            last_kernel, (1, [(0, 1)]), 1.0 / (rows * n_tok * half * n_wid), len(early)
        ),
        [bf16(width, lats), f32(LEVELS)],
        (*early_grads, resids[1], others[1], encoded),
        out_specs=[VMEM, SMEM],
    )
    return (losses, grad)


def solution(mesh):
    return jax.shard_map(
        body,
        mesh=mesh,
        in_specs=(P("tok", "wid"), P("lat", "wid"), P("lat"), P("wid"), P("tok", None), P()),
        out_specs=(P(), P(("wid", "tok"), "lat")),
        check_vma=False,
    )
```

```python
import functools

import jax
import jax.numpy as jnp
from jax import lax
from jax.experimental import pallas as pl
from jax.experimental.pallas import tpu as pltpu
from jax.sharding import PartitionSpec as P

LEVELS = 4
BLOCK = 128
LOSS_ROWS = 8
GELU_C = 0.7978845608028654
GELU_A = 0.044715

VMEM = pl.BlockSpec(memory_space=pltpu.VMEM)
SMEM = pl.BlockSpec(memory_space=pltpu.SMEM)
HBM = pl.BlockSpec(memory_space=pltpu.HBM)
ANY = pl.BlockSpec(memory_space=pl.ANY)


def f32(*shape):
    return jax.ShapeDtypeStruct(shape, jnp.float32)


def bf16(*shape):
    return jax.ShapeDtypeStruct(shape, jnp.bfloat16)


def call(kernel, outs, arrays, after=(), specs=None, out_specs=None, scratch=()):
    skip = slice(len(arrays), len(arrays) + len(after))

    def run(*refs):
        kernel(*refs[: skip.start], *refs[skip.stop :])

    return pl.pallas_call(
        run,
        out_shape=outs,
        in_specs=list(specs or [VMEM] * len(arrays)) + [ANY] * len(after),
        out_specs=out_specs or [VMEM] * len(outs),
        scratch_shapes=list(scratch),
        compiler_params=pltpu.CompilerParams(vmem_limit_bytes=12 * 1024 * 1024),
        cost_estimate=pl.CostEstimate(flops=0, bytes_accessed=1 << 10, transcendentals=0),
    )(*arrays, *after)


def in_hbm(array):
    return pltpu.with_memory_space_constraint(array, pltpu.HBM)


def total_of(terms):
    return functools.reduce(jnp.add, terms)


def place_in_chain():
    lat = lax.axis_index("lat")
    return jnp.where(lax.axis_index("wid") == 0, lat, lax.axis_size("lat") - 1 - lat)


def level_table(bounds, count, out):
    lasts = bounds[...] - 1 - lax.axis_index("lat") * count
    upward = lax.axis_index("wid") == 0

    def put(row, value):
        out[row : row + 1, :] = jnp.broadcast_to(value, (1, BLOCK))

    for i in range(count):
        hits = (jnp.minimum(lasts, count - 1) == i).astype(jnp.float32)
        ending = jnp.sum(hits, axis=1, keepdims=True)
        put(i, ending)
        put(count + i, jnp.where(upward, jnp.full_like(ending, float(i == count - 1)), ending))
    for m in range(LEVELS):
        for i in range(count):
            put((2 + m) * count + i, (lasts[:, m : m + 1] == i).astype(jnp.float32))


def pre_kernel(resid, dictionary, partial_out, dict_out, resid_v, dict_v, sems):
    pieces, _, width = dict_v.shape
    copies = []
    for i in range(pieces):
        cols = pl.ds(i * width, width)
        copies.append(
            (
                pltpu.make_async_copy(resid.at[:, cols], resid_v.at[i], sems.at[0, i]),
                pltpu.make_async_copy(dictionary.at[:, cols], dict_v.at[i], sems.at[1, i]),
            )
        )
        for copy in copies[-1]:
            copy.start()
    total = None
    for i in range(pieces):
        for copy in copies[i]:
            copy.wait()
        term = lax.dot_general(
            dict_v[i], resid_v[i], (((1,), (1,)), ((), ())), preferred_element_type=jnp.float32
        )
        total = term if total is None else total + term
    partial_out[...] = total.T
    parts = dict_out.shape[1] // width
    for i in range(parts):
        dict_out[:, i * width : (i + 1) * width] = dict_v[lax.axis_index("tok") * parts + i]


def widen_kernel(array, bounds, out, table_out):
    out[...] = array[...].astype(jnp.float32)
    level_table(bounds, array.shape[0] // BLOCK, table_out)


def pieces_kernel(resid, bias, bias_out, *outs):
    width = outs[0].shape[1]
    tok = lax.axis_index("tok")

    def cols(t):
        return pl.ds(pl.multiple_of(t * width, width), width)

    bias_out[...] = bias[:, cols(tok)]
    for q, out in enumerate(outs):
        out[...] = resid[:, cols(tok ^ q)].astype(jnp.float32)


def block_mask(active, lats):
    count = lats // BLOCK
    ids = lax.axis_index("lat") * count + lax.broadcasted_iota(jnp.int32, (count, 1), 0)
    hits = total_of([(active[q : q + 1, :] == ids).astype(jnp.float32) for q in range(active.shape[0])])
    spread = lax.broadcasted_iota(jnp.int32, (count, lats), 1) // BLOCK
    spread = (spread == lax.broadcasted_iota(jnp.int32, (count, lats), 0)).astype(jnp.bfloat16)
    return lax.dot_general(
        hits.astype(jnp.bfloat16),
        spread,
        (((0,), (0,)), ((), ())),
        preferred_element_type=jnp.float32,
    )


def activate_kernel(mine, other, bias, active, pre_out, act_out, mask_out):
    pre = mine[...] + other[...] + bias[...]
    pre_out[...] = pre
    inner = GELU_C * (pre + GELU_A * (pre * pre * pre))
    gelu = 0.5 * pre * (1.0 + jnp.tanh(inner))
    mask = block_mask(active[...], pre.shape[1])
    mask_out[...] = mask
    act_out[...] = jnp.where(mask > 0.0, gelu, 0.0)


def half_of(wid, rows):
    return pl.ds(pl.multiple_of(wid * (rows // 2), rows // 2), rows // 2)


def stacked(parts, extra, out):
    rows, cols = parts.shape
    for i in range(cols // BLOCK):
        out[i * rows : (i + 1) * rows, :] = parts[:, i * BLOCK : (i + 1) * BLOCK]
    out[-LOSS_ROWS:, :] = extra


def unstacked(ref, count):
    rows = (ref.shape[0] - LOSS_ROWS) // count
    return jnp.concatenate([ref[i * rows : (i + 1) * rows, :] for i in range(count)], axis=1)


def g_pre_kernel(pre_ref, mask, loss, *refs):
    terms, out = refs[:-1], refs[-1]
    mine = half_of(lax.axis_index("wid"), pre_ref.shape[0])
    pre = pre_ref[mine, :]
    inner = GELU_C * (pre + GELU_A * (pre * pre * pre))
    slope = GELU_C * (1.0 + 3.0 * GELU_A * (pre * pre))
    bend = jnp.tanh(inner)
    deriv = 0.5 * (1.0 + bend) + 0.5 * pre * (1.0 - bend * bend) * slope
    hit = mask[mine, :] > 0.0
    stacked(jnp.where(hit, deriv * total_of([t[...] for t in terms]), 0.0), loss[...], out)


def running_parts(act, dict_ref):
    sums = []
    for i in range(dict_ref.shape[0] // BLOCK):
        span = slice(i * BLOCK, (i + 1) * BLOCK)
        part = jnp.dot(
            act[:, span], dict_ref[span, :].astype(jnp.bfloat16), preferred_element_type=jnp.float32
        )
        sums.append(sums[-1] + part if sums else part)
    return sums


def round_kernel(act, out):
    out[...] = act[...].astype(jnp.bfloat16)


def project_kernel(act, table, *refs):
    dicts, out = refs[:-1], refs[-1]
    for side, dictionary in enumerate(dicts):
        sums = running_parts(act[...], dictionary)
        count = len(sums)
        width = dictionary.shape[1]
        out[:, side * width : (side + 1) * width] = total_of(
            [table[count + i : count + i + 1, :1] * s for i, s in enumerate(sums)]
        )


def columns(ref, col, width):
    return ref[:, col * width : (col + 1) * width]


def message_kernel(places, cols, got, *refs):
    out = refs[-1]
    width = out.shape[1]
    index = place_in_chain()
    for place, piece, col in zip(places, refs[:-1], cols[1:]):

        @pl.when(index == place)
        def _():
            own = columns(piece, col, width)
            out[...] = own + columns(got, cols[0], width) if place else own


def choose_kernel(places, cols, *refs):
    arrived, out = refs[:-1], refs[-1]
    index = place_in_chain()

    @pl.when(index == 0)
    def _():
        out[...] = jnp.zeros_like(out)

    for place, ref, col in zip(places, arrived, cols):

        @pl.when(index == place if len(arrived) > 1 else index > 0)
        def _():
            out[...] = columns(ref, col, out.shape[1])


def square_sums(table, shifted):
    count = len(shifted)
    squares = []
    for v in shifted:
        lanes = jnp.sum(v * v, axis=0, keepdims=True)
        squares.append(total_of([lanes[:, i : i + BLOCK] for i in range(0, lanes.shape[1], BLOCK)]))
    rows = []
    for m in range(LEVELS):
        at = (2 + m) * count
        rows.append(total_of([table[at + i : at + i + 1, :] * s for i, s in enumerate(squares)]))
    return jnp.concatenate(rows + [jnp.zeros((LOSS_ROWS - LEVELS, BLOCK), jnp.float32)], axis=0)


def error_kernel(loss_count, act, dictionary, resid, bias, table, mine, other, *refs):
    before, refs = refs[:loss_count], refs[loss_count:]
    err_out, keep_out, give_out, loss_out = refs
    upward = lax.axis_index("wid") == 0
    earlier = jnp.where(upward, mine[...], other[...])
    later = jnp.where(upward, other[...], mine[...])
    base = bias[...] - resid[...] + earlier
    sums = running_parts(act[...], dictionary)
    shifted = [base + s for s in sums]
    loss_out[...] = total_of([square_sums(table, shifted)] + [b[...] for b in before])
    err = later
    for i in reversed(range(len(sums))):
        err = err + table[i : i + 1, :1] * shifted[i]
        rounded = err.astype(jnp.bfloat16)
        err_out[i] = rounded
        cols = slice(i * BLOCK, (i + 1) * BLOCK)
        gact = lax.dot_general(
            rounded,
            dictionary[cols, :],
            (((1,), (1,)), ((), ())),
            preferred_element_type=jnp.float32,
        )
        half = gact.shape[0] // 2
        keep_out[:, cols] = jnp.where(upward, gact[:half, :], gact[half:, :])
        give_out[:, cols] = jnp.where(upward, gact[half:, :], gact[:half, :])


def collect_kernel(keep, give, out):
    out[...] = keep[...] + give[...]


def add_kernel(*refs):
    refs[-1][...] = total_of([ref[...] for ref in refs[:-1]])


def decode_kernel(*refs):
    n = (len(refs) - 1) // 2
    errs, acts, out = refs[:n], refs[n : 2 * n], refs[-1]
    for i in range(errs[0].shape[0]):
        cols = slice(i * BLOCK, (i + 1) * BLOCK)
        err = jnp.concatenate([e[i] for e in errs], axis=0)
        act = jnp.concatenate([a[:, cols] for a in acts], axis=0)
        out[:, cols] = lax.dot_general(
            err, act, (((0,), (0,)), ((), ())), preferred_element_type=jnp.float32
        )


def encode_kernel(items, *refs):
    n, halves = items
    resids, grads, base, out = refs[:n], refs[n:-2], refs[-2], refs[-1]
    half = resids[0].shape[0] // 2
    count = out.shape[1] // BLOCK
    wid = lax.axis_index("wid")
    spans = [half_of(wid, 2 * half), half_of(1 - wid, 2 * half)]
    resid = jnp.concatenate(
        [resids[q][spans[side], :].astype(jnp.bfloat16) for q, side in halves], axis=0
    )
    grad = jnp.concatenate([unstacked(g, count).astype(jnp.bfloat16) for g in grads], axis=0)
    total = base[...] + lax.dot_general(
        resid, grad, (((0,), (0,)), ((), ())), preferred_element_type=jnp.float32
    )
    out[...] = total.astype(out.dtype)


def last_kernel(items, scale, n_early, *refs):
    *refs, out, loss_out = refs
    early, refs = refs[:n_early], refs[n_early:]
    encode_kernel(items, *refs, out)
    grads = list(early) + list(refs[items[0] : -1])
    lanes = total_of([g[-LOSS_ROWS:, :] for g in grads])
    for m in range(LEVELS):
        loss_out[m] = jnp.sum(lanes[m : m + 1, :]) * scale


def pick(index, choices):
    values = sorted(choices)
    result = choices[values[0]]
    for value in values[1:]:
        result = jnp.where(index == value, choices[value], result)
    return result


def body(resid, dictionary, enc_bias, dec_bias, active_blocks, level_bounds):
    rows, half = resid.shape
    lats = dictionary.shape[0]
    n_lat, n_wid, n_tok = lax.axis_size("lat"), lax.axis_size("wid"), lax.axis_size("tok")
    width = half // n_tok
    count = lats // BLOCK

    def across(array, q):
        return lax.ppermute(array, "tok", [(t, t ^ q) for t in range(n_tok)])

    def swap(array):
        return lax.ppermute(array, "wid", [(w, w ^ 1) for w in range(n_wid)])

    partial, dict_here = call(
        pre_kernel,
        [f32(rows, lats), bf16(lats, width)],
        (in_hbm(resid), in_hbm(dictionary)),
        specs=[HBM, HBM],
        scratch=[
            pltpu.VMEM((2 * n_tok, rows, width // 2), jnp.bfloat16),
            pltpu.VMEM((2 * n_tok, lats, width // 2), jnp.bfloat16),
            pltpu.SemaphoreType.DMA((2, 2 * n_tok)),
        ],
    )
    partial_other = swap(partial)
    dict_wide, table = call(
        widen_kernel,
        [f32(lats, width), f32((2 + LEVELS) * count, BLOCK)],
        (dict_here, level_bounds.reshape(1, LEVELS)),
        after=(partial_other,),
    )
    dict_other = swap(dict_wide)
    pre, act, mask = call(
        activate_kernel,
        [f32(rows, lats)] * 3,
        (partial, partial_other, enc_bias.reshape(1, lats), active_blocks.T),
        after=(dict_wide,),
    )
    gathered = [act] + [across(act, q) for q in range(1, n_tok)]
    bias_here, *pieces = call(
        pieces_kernel,
        [f32(1, width)] + [f32(rows, width)] * n_tok,
        (resid, dec_bias.reshape(1, half)),
        after=(act,),
    )
    resids = [piece if q == 0 else across(piece, q) for q, piece in enumerate(pieces)]

    order = [0, 1, 3, 2] if n_tok == 4 else list(range(n_tok))
    steps = n_tok + n_lat - 2
    places = list(range(1, n_lat))
    acts, errs, hands, gives, gacts, loss = {}, {}, [], [], [], ()
    sums, got, sent = ([], []), ([], []), []
    waits = {step: [] for step in range(steps)}
    for place, q in enumerate(order[1:]):
        waits[min(3 + place, steps - 1)].append(resids[q])

    def project(q, dicts):
        shape = [f32(rows, width * len(dicts))]
        return call(project_kernel, shape, (acts[q], table, *dicts))[0]

    for step in range(steps + 1):
        at = [p for p in range(n_lat - 1) if 0 <= step - p < n_tok]
        pairs = []
        for p in at:
            pairs.append((2 * p, 2 * (p + 1)))
            pairs.append((2 * (n_lat - 1 - p) + 1, 2 * (n_lat - 2 - p) + 1))
        if step == 0:
            acts[order[0]] = call(round_kernel, [bf16(rows, lats)], (act,))[0]
            for side, dict_ref in enumerate((dict_other, dict_here)):
                message = project(order[0], (dict_ref,))
                sums[side].append((message, 0))
                got[side].append((lax.ppermute(message, ("lat", "wid"), pairs), 0))
                sent = [message]
        elif step < steps:
            for side in range(2):
                items = [got[side][-1], *[sums[side][step - p] for p in at]]
                message = call(
                    functools.partial(message_kernel, at, [col for _, col in items]),
                    [f32(rows, width)],
                    [array for array, _ in items],
                    after=sent + (waits[step] if side == 0 else []) if step > 1 else (),
                )[0]
                got[side].append((lax.ppermute(message, ("lat", "wid"), pairs), 0))
                sent = [message]
        if step + 1 < n_tok:
            q = order[step + 1]
            acts[q] = call(round_kernel, [bf16(rows, lats)], (gathered[q],), after=sent)[0]
            for side, dict_ref in enumerate((dict_other, dict_here)):
                sums[side].append((project(q, (dict_ref,)), 0))
        ready = []
        c = step - (n_lat - 1)
        if c >= 0:
            chosen = []
            for side in range(2):
                items = [got[side][c + p - 1] for p in places]
                if n_lat > 4:
                    items = [a[:, col * width : (col + 1) * width] for a, col in items]
                    items = [(pick(place_in_chain(), dict(zip(places, items))), 0)]
                chosen.append(
                    call(
                        functools.partial(choose_kernel, places, [col for _, col in items]),
                        [f32(rows, width)],
                        [array for array, _ in items],
                        after=sent if step < steps else ready_before + chosen,
                    )[0]
                )
            hands.append((swap(chosen[0]), chosen[1]))
            ready += chosen
        stages = [c - 1] if step < steps else [c - 1, c]
        for c in stages:
            if c < 0:
                continue
            q = order[c]
            errs[q], keep, give, loss_here = call(
                functools.partial(error_kernel, len(loss)),
                [bf16(count, rows, width)] + [f32(rows // 2, lats)] * 2 + [f32(LOSS_ROWS, BLOCK)],
                (acts[q], dict_here, resids[q], bias_here, table, hands[c][1], hands[c][0], *loss),
                after=sent if step < steps else (),
            )
            loss = (loss_here,)
            gives.append((keep, swap(give)))
            ready.append(errs[q])
        stages = range(n_tok) if step == steps else []
        for c in stages:
            if c < 0:
                continue
            q = order[c]
            added = call(
                collect_kernel, [f32(rows // 2, lats)], gives[c], after=sent if step < steps else ()
            )[0]
            gacts.append(across(added, q) if q else added)
            ready.append(added)
        if step + 1 < steps:
            waits[step + 1] += ready
        ready_before = ready

    loss, gap = loss[0], 1
    while gap < n_lat:
        other = lax.ppermute(loss, "lat", [(p, p ^ gap) for p in range(n_lat)])
        loss = call(add_kernel, [f32(*loss.shape)], (loss, other))[0]
        gap *= 2

    decoded = call(
        decode_kernel,
        [f32(width, lats)],
        (*[errs[q] for q in order], *[acts[q] for q in order]),
    )[0]
    g_pre = call(
        g_pre_kernel,
        [f32(rows // 2 * count + LOSS_ROWS, BLOCK)],
        (pre, mask, loss, *gacts),
        after=(decoded,),
    )[0]
    mine = [across(g_pre, q) if q else g_pre for q in range(n_tok)]
    others = [swap(g) for g in mine]
    early = [(q, side) for side in range(2) for q in range(n_tok) if (q, side) != (1, 1)]
    halves = [mine, others]
    early_grads = [halves[side][q] for q, side in early]
    encoded = call(
        functools.partial(encode_kernel, (n_tok, early)),
        [f32(width, lats)],
        (*resids, *early_grads, decoded),
    )[0]
    grad, losses = call(
        functools.partial(
            last_kernel, (1, [(0, 1)]), 1.0 / (rows * n_tok * half * n_wid), len(early)
        ),
        [bf16(width, lats), f32(LEVELS)],
        (*early_grads, resids[1], others[1], encoded),
        out_specs=[VMEM, SMEM],
    )
    return (losses, grad)


def solution(mesh):
    return jax.shard_map(
        body,
        mesh=mesh,
        in_specs=(P("tok", "wid"), P("lat", "wid"), P("lat"), P("wid"), P("tok", None), P()),
        out_specs=(P(), P(("wid", "tok"), "lat")),
        check_vma=False,
    )
```

```python
import functools

import jax
import jax.numpy as jnp
from jax import lax
from jax.experimental import pallas as pl
from jax.experimental.pallas import tpu as pltpu
from jax.sharding import PartitionSpec as P

LEVELS = 4
BLOCK = 128
LOSS_ROWS = 8
LOSS_AREA = 192
GELU_C = 0.7978845608028654
GELU_A = 0.044715

VMEM = pl.BlockSpec(memory_space=pltpu.VMEM)
SMEM = pl.BlockSpec(memory_space=pltpu.SMEM)
HBM = pl.BlockSpec(memory_space=pltpu.HBM)
ANY = pl.BlockSpec(memory_space=pl.ANY)


def f32(*shape):
    return jax.ShapeDtypeStruct(shape, jnp.float32)


def bf16(*shape):
    return jax.ShapeDtypeStruct(shape, jnp.bfloat16)


def call(kernel, outs, arrays, after=(), specs=None, out_specs=None, scratch=()):
    skip = slice(len(arrays), len(arrays) + len(after))

    def run(*refs):
        kernel(*refs[: skip.start], *refs[skip.stop :])

    return pl.pallas_call(
        run,
        out_shape=outs,
        in_specs=list(specs or [VMEM] * len(arrays)) + [ANY] * len(after),
        out_specs=out_specs or [VMEM] * len(outs),
        scratch_shapes=list(scratch),
        compiler_params=pltpu.CompilerParams(vmem_limit_bytes=12 * 1024 * 1024),
        cost_estimate=pl.CostEstimate(flops=0, bytes_accessed=1 << 10, transcendentals=0),
    )(*arrays, *after)


def in_hbm(array):
    return pltpu.with_memory_space_constraint(array, pltpu.HBM)


def total_of(terms):
    return functools.reduce(jnp.add, terms)


def place_in_chain():
    lat = lax.axis_index("lat")
    return jnp.where(lax.axis_index("wid") == 0, lat, lax.axis_size("lat") - 1 - lat)


def level_table(bounds, count, out):
    lasts = bounds[...] - 1 - lax.axis_index("lat") * count
    upward = lax.axis_index("wid") == 0

    def put(row, value):
        out[row : row + 1, :] = jnp.broadcast_to(value, (1, BLOCK))

    for i in range(count):
        hits = (jnp.minimum(lasts, count - 1) == i).astype(jnp.float32)
        ending = jnp.sum(hits, axis=1, keepdims=True)
        put(i, ending)
        put(count + i, jnp.where(upward, jnp.full_like(ending, float(i == count - 1)), ending))
    for m in range(LEVELS):
        for i in range(count):
            put((2 + m) * count + i, (lasts[:, m : m + 1] == i).astype(jnp.float32))


def pre_kernel(resid, dictionary, partial_out, dict_out, resid_v, dict_v, sems):
    pieces, _, width = dict_v.shape
    copies = []
    for i in range(pieces):
        cols = pl.ds(i * width, width)
        copies.append(
            (
                pltpu.make_async_copy(resid.at[:, cols], resid_v.at[i], sems.at[0, i]),
                pltpu.make_async_copy(dictionary.at[:, cols], dict_v.at[i], sems.at[1, i]),
            )
        )
        for copy in copies[-1]:
            copy.start()
    total = None
    for i in range(pieces):
        for copy in copies[i]:
            copy.wait()
        term = lax.dot_general(
            dict_v[i], resid_v[i], (((1,), (1,)), ((), ())), preferred_element_type=jnp.float32
        )
        total = term if total is None else total + term
    partial_out[...] = total.T
    parts = dict_out.shape[1] // width
    for i in range(parts):
        dict_out[:, i * width : (i + 1) * width] = dict_v[lax.axis_index("tok") * parts + i]


def widen_kernel(array, bounds, out, table_out):
    out[...] = array[...].astype(jnp.float32)
    level_table(bounds, array.shape[0] // BLOCK, table_out)


def pieces_kernel(resid, bias, bias_out, *outs):
    width = outs[0].shape[1]
    tok = lax.axis_index("tok")

    def cols(t):
        return pl.ds(pl.multiple_of(t * width, width), width)

    bias_out[...] = bias[:, cols(tok)]
    for q, out in enumerate(outs):
        out[...] = resid[:, cols(tok ^ q)].astype(jnp.float32)


def block_mask(active, lats):
    count = lats // BLOCK
    ids = lax.axis_index("lat") * count + lax.broadcasted_iota(jnp.int32, (count, 1), 0)
    hits = total_of([(active[q : q + 1, :] == ids).astype(jnp.float32) for q in range(active.shape[0])])
    spread = lax.broadcasted_iota(jnp.int32, (count, lats), 1) // BLOCK
    spread = (spread == lax.broadcasted_iota(jnp.int32, (count, lats), 0)).astype(jnp.bfloat16)
    return lax.dot_general(
        hits.astype(jnp.bfloat16),
        spread,
        (((0,), (0,)), ((), ())),
        preferred_element_type=jnp.float32,
    )


def activate_kernel(mine, other, bias, active, pre_out, act_out, mask_out):
    pre = mine[...] + other[...] + bias[...]
    pre_out[...] = pre
    inner = GELU_C * (pre + GELU_A * (pre * pre * pre))
    gelu = 0.5 * pre * (1.0 + jnp.tanh(inner))
    mask = block_mask(active[...], pre.shape[1])
    mask_out[...] = mask
    act_out[...] = jnp.where(mask > 0.0, gelu, 0.0)


def half_of(wid, rows):
    return pl.ds(pl.multiple_of(wid * (rows // 2), rows // 2), rows // 2)


def stacked(parts, extra, out):
    rows, cols = parts.shape
    for i in range(cols // BLOCK):
        out[i * rows : (i + 1) * rows, :] = parts[:, i * BLOCK : (i + 1) * BLOCK]
    out[-LOSS_ROWS:, :] = extra


def unstacked(ref, count):
    rows = (ref.shape[0] - LOSS_ROWS) // count
    return jnp.concatenate([ref[i * rows : (i + 1) * rows, :] for i in range(count)], axis=1)


def g_pre_kernel(pre_ref, mask, loss, *refs):
    terms, out = refs[:-1], refs[-1]
    mine = half_of(lax.axis_index("wid"), pre_ref.shape[0])
    pre = pre_ref[mine, :]
    inner = GELU_C * (pre + GELU_A * (pre * pre * pre))
    slope = GELU_C * (1.0 + 3.0 * GELU_A * (pre * pre))
    bend = jnp.tanh(inner)
    deriv = 0.5 * (1.0 + bend) + 0.5 * pre * (1.0 - bend * bend) * slope
    hit = mask[mine, :] > 0.0
    total = total_of([t[...] for t in terms])
    stacked(jnp.where(hit, deriv * total, 0.0), loss[:LOSS_ROWS, :], out)


def running_parts(act, dict_ref):
    sums = []
    for i in range(dict_ref.shape[0] // BLOCK):
        span = slice(i * BLOCK, (i + 1) * BLOCK)
        part = jnp.dot(
            act[:, span], dict_ref[span, :].astype(jnp.bfloat16), preferred_element_type=jnp.float32
        )
        sums.append(sums[-1] + part if sums else part)
    return sums


def round_kernel(act, out):
    out[...] = act[...].astype(jnp.bfloat16)


def project_kernel(act, table, *refs):
    dicts, out = refs[:-1], refs[-1]
    for side, dictionary in enumerate(dicts):
        sums = running_parts(act[...], dictionary)
        count = len(sums)
        width = dictionary.shape[1]
        out[:, side * width : (side + 1) * width] = total_of(
            [table[count + i : count + i + 1, :1] * s for i, s in enumerate(sums)]
        )


def columns(ref, col, width):
    return ref[:, col * width : (col + 1) * width]


def message_kernel(places, cols, got, *refs):
    out = refs[-1]
    width = out.shape[1]
    index = place_in_chain()
    for place, piece, col in zip(places, refs[:-1], cols[1:]):

        @pl.when(index == place)
        def _():
            own = columns(piece, col, width)
            out[...] = own + columns(got, cols[0], width) if place else own


def choose_kernel(places, cols, *refs):
    arrived, out = refs[:-1], refs[-1]
    index = place_in_chain()

    @pl.when(index == 0)
    def _():
        out[...] = jnp.zeros_like(out)

    for place, ref, col in zip(places, arrived, cols):

        @pl.when(index == place if len(arrived) > 1 else index > 0)
        def _():
            out[...] = columns(ref, col, out.shape[1])


def square_sums(table, shifted):
    count = len(shifted)
    squares = []
    for v in shifted:
        lanes = jnp.sum(v * v, axis=0, keepdims=True)
        squares.append(total_of([lanes[:, i : i + BLOCK] for i in range(0, lanes.shape[1], BLOCK)]))
    rows = []
    for m in range(LEVELS):
        at = (2 + m) * count
        rows.append(total_of([table[at + i : at + i + 1, :] * s for i, s in enumerate(squares)]))
    return jnp.concatenate(rows + [jnp.zeros((LOSS_ROWS - LEVELS, BLOCK), jnp.float32)], axis=0)


def error_kernel(loss_count, act, dictionary, resid, bias, table, mine, other, *refs):
    before, refs = refs[:loss_count], refs[loss_count:]
    err_out, keep_out, give_out, loss_out = refs
    upward = lax.axis_index("wid") == 0
    earlier = jnp.where(upward, mine[...], other[...])
    later = jnp.where(upward, other[...], mine[...])
    base = bias[...] - resid[...] + earlier
    sums = running_parts(act[...], dictionary)
    shifted = [base + s for s in sums]
    loss_out[...] = total_of([square_sums(table, shifted)] + [b[...] for b in before])
    err = later
    for i in reversed(range(len(sums))):
        err = err + table[i : i + 1, :1] * shifted[i]
        rounded = err.astype(jnp.bfloat16)
        err_out[i] = rounded
        cols = slice(i * BLOCK, (i + 1) * BLOCK)
        gact = lax.dot_general(
            rounded,
            dictionary[cols, :],
            (((1,), (1,)), ((), ())),
            preferred_element_type=jnp.float32,
        )
        half = gact.shape[0] // 2
        keep_out[:, cols] = jnp.where(upward, gact[:half, :], gact[half:, :])
        give_out[:, cols] = jnp.where(upward, gact[half:, :], gact[:half, :])


def collect_kernel(keep, give, out):
    out[...] = keep[...] + give[...]


def spread_kernel(loss, out):
    out[...] = jnp.zeros_like(out)
    out[:LOSS_ROWS, :] = loss[...]


def add_kernel(*refs):
    refs[-1][...] = total_of([ref[...] for ref in refs[:-1]])


def decode_kernel(*refs):
    n = (len(refs) - 1) // 2
    errs, acts, out = refs[:n], refs[n : 2 * n], refs[-1]
    for i in range(errs[0].shape[0]):
        cols = slice(i * BLOCK, (i + 1) * BLOCK)
        err = jnp.concatenate([e[i] for e in errs], axis=0)
        act = jnp.concatenate([a[:, cols] for a in acts], axis=0)
        out[:, cols] = lax.dot_general(
            err, act, (((0,), (0,)), ((), ())), preferred_element_type=jnp.float32
        )


def encode_kernel(items, *refs):
    n, halves = items
    resids, grads, base, out = refs[:n], refs[n:-2], refs[-2], refs[-1]
    half = resids[0].shape[0] // 2
    count = out.shape[1] // BLOCK
    wid = lax.axis_index("wid")
    spans = [half_of(wid, 2 * half), half_of(1 - wid, 2 * half)]
    resid = jnp.concatenate(
        [resids[q][spans[side], :].astype(jnp.bfloat16) for q, side in halves], axis=0
    )
    grad = jnp.concatenate([unstacked(g, count).astype(jnp.bfloat16) for g in grads], axis=0)
    total = base[...] + lax.dot_general(
        resid, grad, (((0,), (0,)), ((), ())), preferred_element_type=jnp.float32
    )
    out[...] = total.astype(out.dtype)


def last_kernel(items, scale, n_early, *refs):
    *refs, out, loss_out = refs
    early, refs = refs[:n_early], refs[n_early:]
    encode_kernel(items, *refs, out)
    grads = list(early) + list(refs[items[0] : -1])
    lanes = total_of([g[-LOSS_ROWS:, :] for g in grads])
    for m in range(LEVELS):
        loss_out[m] = jnp.sum(lanes[m : m + 1, :]) * scale


def pick(index, choices):
    values = sorted(choices)
    result = choices[values[0]]
    for value in values[1:]:
        result = jnp.where(index == value, choices[value], result)
    return result


def body(resid, dictionary, enc_bias, dec_bias, active_blocks, level_bounds):
    rows, half = resid.shape
    lats = dictionary.shape[0]
    n_lat, n_wid, n_tok = lax.axis_size("lat"), lax.axis_size("wid"), lax.axis_size("tok")
    width = half // n_tok
    count = lats // BLOCK

    def across(array, q):
        return lax.ppermute(array, "tok", [(t, t ^ q) for t in range(n_tok)])

    def swap(array):
        return lax.ppermute(array, "wid", [(w, w ^ 1) for w in range(n_wid)])

    partial, dict_here = call(
        pre_kernel,
        [f32(rows, lats), bf16(lats, width)],
        (in_hbm(resid), in_hbm(dictionary)),
        specs=[HBM, HBM],
        scratch=[
            pltpu.VMEM((2 * n_tok, rows, width // 2), jnp.bfloat16),
            pltpu.VMEM((2 * n_tok, lats, width // 2), jnp.bfloat16),
            pltpu.SemaphoreType.DMA((2, 2 * n_tok)),
        ],
    )
    partial_other = swap(partial)
    dict_wide, table = call(
        widen_kernel,
        [f32(lats, width), f32((2 + LEVELS) * count, BLOCK)],
        (dict_here, level_bounds.reshape(1, LEVELS)),
        after=(partial_other,),
    )
    dict_other = swap(dict_wide)
    pre, act, mask = call(
        activate_kernel,
        [f32(rows, lats)] * 3,
        (partial, partial_other, enc_bias.reshape(1, lats), active_blocks.T),
        after=(dict_wide,),
    )
    gathered = [act] + [across(act, q) for q in range(1, n_tok)]
    bias_here, *pieces = call(
        pieces_kernel,
        [f32(1, width)] + [f32(rows, width)] * n_tok,
        (resid, dec_bias.reshape(1, half)),
        after=(act,),
    )
    resids = [piece if q == 0 else across(piece, q) for q, piece in enumerate(pieces)]

    order = [0, 1, 3, 2] if n_tok == 4 else list(range(n_tok))
    steps = n_tok + n_lat - 2
    places = list(range(1, n_lat))
    acts, errs, hands, gives, gacts, loss = {}, {}, [], [], [], ()
    sums, got, sent = ([], []), ([], []), []
    waits = {step: [] for step in range(steps)}
    for place, q in enumerate(order[1:]):
        waits[min(3 + place, steps - 1)].append(resids[q])

    def project(q, dicts):
        shape = [f32(rows, width * len(dicts))]
        return call(project_kernel, shape, (acts[q], table, *dicts))[0]

    for step in range(steps + 1):
        at = [p for p in range(n_lat - 1) if 0 <= step - p < n_tok]
        pairs = []
        for p in at:
            pairs.append((2 * p, 2 * (p + 1)))
            pairs.append((2 * (n_lat - 1 - p) + 1, 2 * (n_lat - 2 - p) + 1))
        if step == 0:
            acts[order[0]] = call(round_kernel, [bf16(rows, lats)], (act,))[0]
            for side, dict_ref in enumerate((dict_other, dict_here)):
                message = project(order[0], (dict_ref,))
                sums[side].append((message, 0))
                got[side].append((lax.ppermute(message, ("lat", "wid"), pairs), 0))
                sent = [message]
        elif step < steps:
            for side in range(2):
                items = [got[side][-1], *[sums[side][step - p] for p in at]]
                message = call(
                    functools.partial(message_kernel, at, [col for _, col in items]),
                    [f32(rows, width)],
                    [array for array, _ in items],
                    after=sent + (waits[step] if side == 0 else []) if step > 1 else (),
                )[0]
                got[side].append((lax.ppermute(message, ("lat", "wid"), pairs), 0))
                sent = [message]
        if step + 1 < n_tok:
            q = order[step + 1]
            acts[q] = call(round_kernel, [bf16(rows, lats)], (gathered[q],), after=sent)[0]
            for side, dict_ref in enumerate((dict_other, dict_here)):
                sums[side].append((project(q, (dict_ref,)), 0))
        ready = []
        c = step - (n_lat - 1)
        if c >= 0:
            chosen = []
            for side in range(2):
                items = [got[side][c + p - 1] for p in places]
                if n_lat > 4:
                    items = [a[:, col * width : (col + 1) * width] for a, col in items]
                    items = [(pick(place_in_chain(), dict(zip(places, items))), 0)]
                chosen.append(
                    call(
                        functools.partial(choose_kernel, places, [col for _, col in items]),
                        [f32(rows, width)],
                        [array for array, _ in items],
                        after=sent if step < steps else ready_before + chosen,
                    )[0]
                )
            hands.append((swap(chosen[0]), chosen[1]))
            ready += chosen
        stages = [c - 1] if step < steps else [c - 1, c]
        for c in stages:
            if c < 0:
                continue
            q = order[c]
            errs[q], keep, give, loss_here = call(
                functools.partial(error_kernel, len(loss)),
                [bf16(count, rows, width)] + [f32(rows // 2, lats)] * 2 + [f32(LOSS_ROWS, BLOCK)],
                (acts[q], dict_here, resids[q], bias_here, table, hands[c][1], hands[c][0], *loss),
                after=sent if step < steps else (),
            )
            loss = (loss_here,)
            gives.append((keep, swap(give)))
            ready.append(errs[q])
        stages = range(n_tok) if step == steps else []
        for c in stages:
            if c < 0:
                continue
            q = order[c]
            added = call(
                collect_kernel,
                [f32(rows // 2, lats)],
                gives[c],
                after=gacts[1:2] if c == n_tok - 1 else (),
            )[0]
            gacts.append(across(added, q) if q else added)
            ready.append(added)
        if step + 1 < steps:
            waits[step + 1] += ready
        ready_before = ready

    loss, gap = call(spread_kernel, [f32(LOSS_AREA, BLOCK)], loss)[0], 1
    while gap < n_lat:
        other = lax.ppermute(loss, "lat", [(p, p ^ gap) for p in range(n_lat)])
        loss = call(add_kernel, [f32(*loss.shape)], (loss, other))[0]
        gap *= 2

    decoded = call(
        decode_kernel,
        [f32(width, lats)],
        (*[errs[q] for q in order], *[acts[q] for q in order]),
    )[0]
    g_pre = call(
        g_pre_kernel,
        [f32(rows // 2 * count + LOSS_ROWS, BLOCK)],
        (pre, mask, loss, *gacts),
        after=(decoded,),
    )[0]
    mine = [across(g_pre, q) if q else g_pre for q in range(n_tok)]
    others = [swap(g) for g in mine]
    early = [(q, side) for side in range(2) for q in range(n_tok) if (q, side) != (1, 1)]
    halves = [mine, others]
    early_grads = [halves[side][q] for q, side in early]
    encoded = call(
        functools.partial(encode_kernel, (n_tok, early)),
        [f32(width, lats)],
        (*resids, *early_grads, decoded),
    )[0]
    grad, losses = call(
        functools.partial(
            last_kernel, (1, [(0, 1)]), 1.0 / (rows * n_tok * half * n_wid), len(early)
        ),
        [bf16(width, lats), f32(LEVELS)],
        (*early_grads, resids[1], others[1], encoded),
        out_specs=[VMEM, SMEM],
    )
    return (losses, grad)


def solution(mesh):
    return jax.shard_map(
        body,
        mesh=mesh,
        in_specs=(P("tok", "wid"), P("lat", "wid"), P("lat"), P("wid"), P("tok", None), P()),
        out_specs=(P(), P(("wid", "tok"), "lat")),
        check_vma=False,
    )
```

```python
import functools

import jax
import jax.numpy as jnp
from jax import lax
from jax.experimental import pallas as pl
from jax.experimental.pallas import tpu as pltpu
from jax.sharding import PartitionSpec as P

LEVELS = 4
BLOCK = 128
LOSS_ROWS = 8
GELU_C = 0.7978845608028654
GELU_A = 0.044715

VMEM = pl.BlockSpec(memory_space=pltpu.VMEM)
SMEM = pl.BlockSpec(memory_space=pltpu.SMEM)
HBM = pl.BlockSpec(memory_space=pltpu.HBM)
ANY = pl.BlockSpec(memory_space=pl.ANY)


def f32(*shape):
    return jax.ShapeDtypeStruct(shape, jnp.float32)


def bf16(*shape):
    return jax.ShapeDtypeStruct(shape, jnp.bfloat16)


def call(kernel, outs, arrays, after=(), specs=None, out_specs=None, scratch=()):
    skip = slice(len(arrays), len(arrays) + len(after))

    def run(*refs):
        kernel(*refs[: skip.start], *refs[skip.stop :])

    return pl.pallas_call(
        run,
        out_shape=outs,
        in_specs=list(specs or [VMEM] * len(arrays)) + [ANY] * len(after),
        out_specs=out_specs or [VMEM] * len(outs),
        scratch_shapes=list(scratch),
        compiler_params=pltpu.CompilerParams(vmem_limit_bytes=12 * 1024 * 1024),
        cost_estimate=pl.CostEstimate(flops=0, bytes_accessed=1 << 10, transcendentals=0),
    )(*arrays, *after)


def in_hbm(array):
    return pltpu.with_memory_space_constraint(array, pltpu.HBM)


def total_of(terms):
    return functools.reduce(jnp.add, terms)


def place_in_chain():
    lat = lax.axis_index("lat")
    return jnp.where(lax.axis_index("wid") == 0, lat, lax.axis_size("lat") - 1 - lat)


def level_table(bounds, count, out):
    lasts = bounds[...] - 1 - lax.axis_index("lat") * count
    upward = lax.axis_index("wid") == 0

    def put(row, value):
        out[row : row + 1, :] = jnp.broadcast_to(value, (1, BLOCK))

    for i in range(count):
        hits = (jnp.minimum(lasts, count - 1) == i).astype(jnp.float32)
        ending = jnp.sum(hits, axis=1, keepdims=True)
        put(i, ending)
        put(count + i, jnp.where(upward, jnp.full_like(ending, float(i == count - 1)), ending))
    for m in range(LEVELS):
        for i in range(count):
            put((2 + m) * count + i, (lasts[:, m : m + 1] == i).astype(jnp.float32))


def pre_kernel(resid, dictionary, partial_out, dict_out, resid_v, dict_v, sems):
    pieces, _, width = dict_v.shape
    copies = []
    for i in range(pieces):
        cols = pl.ds(i * width, width)
        copies.append(
            (
                pltpu.make_async_copy(resid.at[:, cols], resid_v.at[i], sems.at[0, i]),
                pltpu.make_async_copy(dictionary.at[:, cols], dict_v.at[i], sems.at[1, i]),
            )
        )
        for copy in copies[-1]:
            copy.start()
    total = None
    for i in range(pieces):
        for copy in copies[i]:
            copy.wait()
        term = lax.dot_general(
            dict_v[i], resid_v[i], (((1,), (1,)), ((), ())), preferred_element_type=jnp.float32
        )
        total = term if total is None else total + term
    partial_out[...] = total.T
    parts = dict_out.shape[1] // width
    for i in range(parts):
        dict_out[:, i * width : (i + 1) * width] = dict_v[lax.axis_index("tok") * parts + i]


def widen_kernel(array, bounds, out, table_out):
    out[...] = array[...].astype(jnp.float32)
    level_table(bounds, array.shape[0] // BLOCK, table_out)


def pieces_kernel(resid, bias, bias_out, *outs):
    width = outs[0].shape[1]
    tok = lax.axis_index("tok")

    def cols(t):
        return pl.ds(pl.multiple_of(t * width, width), width)

    bias_out[...] = bias[:, cols(tok)]
    for q, out in enumerate(outs):
        out[...] = resid[:, cols(tok ^ q)].astype(jnp.float32)


def block_mask(active, lats):
    count = lats // BLOCK
    ids = lax.axis_index("lat") * count + lax.broadcasted_iota(jnp.int32, (count, 1), 0)
    hits = total_of([(active[q : q + 1, :] == ids).astype(jnp.float32) for q in range(active.shape[0])])
    spread = lax.broadcasted_iota(jnp.int32, (count, lats), 1) // BLOCK
    spread = (spread == lax.broadcasted_iota(jnp.int32, (count, lats), 0)).astype(jnp.bfloat16)
    return lax.dot_general(
        hits.astype(jnp.bfloat16),
        spread,
        (((0,), (0,)), ((), ())),
        preferred_element_type=jnp.float32,
    )


def activate_kernel(mine, other, bias, active, pre_out, act_out, mask_out):
    pre = mine[...] + other[...] + bias[...]
    pre_out[...] = pre
    inner = GELU_C * (pre + GELU_A * (pre * pre * pre))
    gelu = 0.5 * pre * (1.0 + jnp.tanh(inner))
    mask = block_mask(active[...], pre.shape[1])
    mask_out[...] = mask
    act_out[...] = jnp.where(mask > 0.0, gelu, 0.0)


def half_of(wid, rows):
    return pl.ds(pl.multiple_of(wid * (rows // 2), rows // 2), rows // 2)


def stacked(parts, extra, out):
    rows, cols = parts.shape
    for i in range(cols // BLOCK):
        out[i * rows : (i + 1) * rows, :] = parts[:, i * BLOCK : (i + 1) * BLOCK]
    out[-LOSS_ROWS:, :] = extra


def unstacked(ref, count):
    rows = (ref.shape[0] - LOSS_ROWS) // count
    return jnp.concatenate([ref[i * rows : (i + 1) * rows, :] for i in range(count)], axis=1)


def g_pre_kernel(pre_ref, mask, loss, *refs):
    terms, out = refs[:-1], refs[-1]
    mine = half_of(lax.axis_index("wid"), pre_ref.shape[0])
    pre = pre_ref[mine, :]
    inner = GELU_C * (pre + GELU_A * (pre * pre * pre))
    slope = GELU_C * (1.0 + 3.0 * GELU_A * (pre * pre))
    bend = jnp.tanh(inner)
    deriv = 0.5 * (1.0 + bend) + 0.5 * pre * (1.0 - bend * bend) * slope
    hit = mask[mine, :] > 0.0
    stacked(jnp.where(hit, deriv * total_of([t[...] for t in terms]), 0.0), loss[...], out)


def running_parts(act, dict_ref):
    sums = []
    for i in range(dict_ref.shape[0] // BLOCK):
        span = slice(i * BLOCK, (i + 1) * BLOCK)
        part = jnp.dot(
            act[:, span], dict_ref[span, :].astype(jnp.bfloat16), preferred_element_type=jnp.float32
        )
        sums.append(sums[-1] + part if sums else part)
    return sums


def round_kernel(act, out):
    out[...] = act[...].astype(jnp.bfloat16)


def project_kernel(act, table, *refs):
    dicts, out = refs[:-1], refs[-1]
    for side, dictionary in enumerate(dicts):
        sums = running_parts(act[...], dictionary)
        count = len(sums)
        width = dictionary.shape[1]
        out[:, side * width : (side + 1) * width] = total_of(
            [table[count + i : count + i + 1, :1] * s for i, s in enumerate(sums)]
        )


def columns(ref, col, width):
    return ref[:, col * width : (col + 1) * width]


def message_kernel(places, cols, got, *refs):
    out = refs[-1]
    width = out.shape[1]
    index = place_in_chain()
    for place, piece, col in zip(places, refs[:-1], cols[1:]):

        @pl.when(index == place)
        def _():
            own = columns(piece, col, width)
            out[...] = own + columns(got, cols[0], width) if place else own


def choose_kernel(places, cols, *refs):
    arrived, out = refs[:-1], refs[-1]
    index = place_in_chain()

    @pl.when(index == 0)
    def _():
        out[...] = jnp.zeros_like(out)

    for place, ref, col in zip(places, arrived, cols):

        @pl.when(index == place if len(arrived) > 1 else index > 0)
        def _():
            out[...] = columns(ref, col, out.shape[1])


def square_sums(table, shifted):
    count = len(shifted)
    squares = []
    for v in shifted:
        lanes = jnp.sum(v * v, axis=0, keepdims=True)
        squares.append(total_of([lanes[:, i : i + BLOCK] for i in range(0, lanes.shape[1], BLOCK)]))
    rows = []
    for m in range(LEVELS):
        at = (2 + m) * count
        rows.append(total_of([table[at + i : at + i + 1, :] * s for i, s in enumerate(squares)]))
    return jnp.concatenate(rows + [jnp.zeros((LOSS_ROWS - LEVELS, BLOCK), jnp.float32)], axis=0)


def error_kernel(loss_count, act, dictionary, resid, bias, table, mine, other, *refs):
    before, refs = refs[:loss_count], refs[loss_count:]
    err_out, keep_out, give_out, loss_out = refs
    upward = lax.axis_index("wid") == 0
    earlier = jnp.where(upward, mine[...], other[...])
    later = jnp.where(upward, other[...], mine[...])
    base = bias[...] - resid[...] + earlier
    sums = running_parts(act[...], dictionary)
    shifted = [base + s for s in sums]
    loss_out[...] = total_of([square_sums(table, shifted)] + [b[...] for b in before])
    err = later
    for i in reversed(range(len(sums))):
        err = err + table[i : i + 1, :1] * shifted[i]
        rounded = err.astype(jnp.bfloat16)
        err_out[i] = rounded
        cols = slice(i * BLOCK, (i + 1) * BLOCK)
        gact = lax.dot_general(
            rounded,
            dictionary[cols, :],
            (((1,), (1,)), ((), ())),
            preferred_element_type=jnp.float32,
        )
        half = gact.shape[0] // 2
        keep_out[:, cols] = jnp.where(upward, gact[:half, :], gact[half:, :])
        give_out[:, cols] = jnp.where(upward, gact[half:, :], gact[:half, :])


def collect_kernel(keep, give, out):
    out[...] = keep[...] + give[...]


def add_kernel(*refs):
    refs[-1][...] = total_of([ref[...] for ref in refs[:-1]])


def decode_kernel(*refs):
    n = (len(refs) - 1) // 2
    errs, acts, out = refs[:n], refs[n : 2 * n], refs[-1]
    for i in range(errs[0].shape[0]):
        cols = slice(i * BLOCK, (i + 1) * BLOCK)
        err = jnp.concatenate([e[i] for e in errs], axis=0)
        act = jnp.concatenate([a[:, cols] for a in acts], axis=0)
        out[:, cols] = lax.dot_general(
            err, act, (((0,), (0,)), ((), ())), preferred_element_type=jnp.float32
        )


def encode_kernel(items, *refs):
    n, halves = items
    resids, grads, base, out = refs[:n], refs[n:-2], refs[-2], refs[-1]
    half = resids[0].shape[0] // 2
    count = out.shape[1] // BLOCK
    wid = lax.axis_index("wid")
    spans = [half_of(wid, 2 * half), half_of(1 - wid, 2 * half)]
    resid = jnp.concatenate(
        [resids[q][spans[side], :].astype(jnp.bfloat16) for q, side in halves], axis=0
    )
    grad = jnp.concatenate([unstacked(g, count).astype(jnp.bfloat16) for g in grads], axis=0)
    total = base[...] + lax.dot_general(
        resid, grad, (((0,), (0,)), ((), ())), preferred_element_type=jnp.float32
    )
    out[...] = total.astype(out.dtype)


def last_kernel(items, scale, n_early, *refs):
    *refs, out, loss_out = refs
    early, refs = refs[:n_early], refs[n_early:]
    encode_kernel(items, *refs, out)
    grads = list(early) + list(refs[items[0] : -1])
    lanes = total_of([g[-LOSS_ROWS:, :] for g in grads])
    for m in range(LEVELS):
        loss_out[m] = jnp.sum(lanes[m : m + 1, :]) * scale


def pick(index, choices):
    values = sorted(choices)
    result = choices[values[0]]
    for value in values[1:]:
        result = jnp.where(index == value, choices[value], result)
    return result


def body(resid, dictionary, enc_bias, dec_bias, active_blocks, level_bounds):
    rows, half = resid.shape
    lats = dictionary.shape[0]
    n_lat, n_wid, n_tok = lax.axis_size("lat"), lax.axis_size("wid"), lax.axis_size("tok")
    width = half // n_tok
    count = lats // BLOCK

    def across(array, q):
        return lax.ppermute(array, "tok", [(t, t ^ q) for t in range(n_tok)])

    def swap(array):
        return lax.ppermute(array, "wid", [(w, w ^ 1) for w in range(n_wid)])

    partial, dict_here = call(
        pre_kernel,
        [f32(rows, lats), bf16(lats, width)],
        (in_hbm(resid), in_hbm(dictionary)),
        specs=[HBM, HBM],
        scratch=[
            pltpu.VMEM((2 * n_tok, rows, width // 2), jnp.bfloat16),
            pltpu.VMEM((2 * n_tok, lats, width // 2), jnp.bfloat16),
            pltpu.SemaphoreType.DMA((2, 2 * n_tok)),
        ],
    )
    partial_other = swap(partial)
    dict_wide, table = call(
        widen_kernel,
        [f32(lats, width), f32((2 + LEVELS) * count, BLOCK)],
        (dict_here, level_bounds.reshape(1, LEVELS)),
        after=(partial_other,),
    )
    dict_other = swap(dict_wide)
    pre, act, mask = call(
        activate_kernel,
        [f32(rows, lats)] * 3,
        (partial, partial_other, enc_bias.reshape(1, lats), active_blocks.T),
        after=(dict_wide,),
    )
    gathered = [act] + [across(act, q) for q in range(1, n_tok)]
    bias_here, *pieces = call(
        pieces_kernel,
        [f32(1, width)] + [f32(rows, width)] * n_tok,
        (resid, dec_bias.reshape(1, half)),
        after=(act,),
    )
    resids = [piece if q == 0 else across(piece, q) for q, piece in enumerate(pieces)]

    order = [0, 1, 3, 2] if n_tok == 4 else list(range(n_tok))
    steps = n_tok + n_lat - 2
    places = list(range(1, n_lat))
    acts, errs, hands, gives, gacts, loss = {}, {}, [], [], [], ()
    sums, got, sent = ([], []), ([], []), []
    waits = {step: ([], []) for step in range(steps)}
    for place, q in enumerate(order[1:]):
        waits[min(3 + place, steps - 1)][0].append(resids[q])
    waits[2][0].append(gathered[order[-1]])

    def project(q, dicts):
        shape = [f32(rows, width * len(dicts))]
        return call(project_kernel, shape, (acts[q], table, *dicts))[0]

    for step in range(steps + 1):
        at = [p for p in range(n_lat - 1) if 0 <= step - p < n_tok]
        pairs = []
        for p in at:
            pairs.append((2 * p, 2 * (p + 1)))
            pairs.append((2 * (n_lat - 1 - p) + 1, 2 * (n_lat - 2 - p) + 1))
        if step == 0:
            acts[order[0]] = call(round_kernel, [bf16(rows, lats)], (act,))[0]
            for side, dict_ref in enumerate((dict_other, dict_here)):
                message = project(order[0], (dict_ref,))
                sums[side].append((message, 0))
                got[side].append((lax.ppermute(message, ("lat", "wid"), pairs), 0))
                sent = [message]
        elif step < steps:
            for side in range(2):
                items = [got[side][-1], *[sums[side][step - p] for p in at]]
                message = call(
                    functools.partial(message_kernel, at, [col for _, col in items]),
                    [f32(rows, width)],
                    [array for array, _ in items],
                    after=sent + waits[step][side] if step > 1 else (),
                )[0]
                got[side].append((lax.ppermute(message, ("lat", "wid"), pairs), 0))
                sent = [message]
        if step + 1 < n_tok:
            q = order[step + 1]
            acts[q] = call(round_kernel, [bf16(rows, lats)], (gathered[q],), after=sent)[0]
            for side, dict_ref in enumerate((dict_other, dict_here)):
                sums[side].append((project(q, (dict_ref,)), 0))
        ready = []
        c = step - (n_lat - 1)
        if c >= 0:
            chosen = []
            for side in range(2):
                items = [got[side][c + p - 1] for p in places]
                if n_lat > 4:
                    items = [a[:, col * width : (col + 1) * width] for a, col in items]
                    items = [(pick(place_in_chain(), dict(zip(places, items))), 0)]
                chosen.append(
                    call(
                        functools.partial(choose_kernel, places, [col for _, col in items]),
                        [f32(rows, width)],
                        [array for array, _ in items],
                        after=sent if step < steps else ready_before + chosen,
                    )[0]
                )
            hands.append((swap(chosen[0]), chosen[1]))
            ready += chosen
        stages = [c - 1] if step < steps else [c - 1, c]
        for c in stages:
            if c < 0:
                continue
            q = order[c]
            errs[q], keep, give, loss_here = call(
                functools.partial(error_kernel, len(loss)),
                [bf16(count, rows, width)] + [f32(rows // 2, lats)] * 2 + [f32(LOSS_ROWS, BLOCK)],
                (acts[q], dict_here, resids[q], bias_here, table, hands[c][1], hands[c][0], *loss),
                after=sent if step < steps else (),
            )
            loss = (loss_here,)
            gives.append((keep, swap(give)))
            ready.append(errs[q])
        stages = range(n_tok) if step == steps else []
        for c in stages:
            if c < 0:
                continue
            q = order[c]
            added = call(
                collect_kernel, [f32(rows // 2, lats)], gives[c], after=sent if step < steps else ()
            )[0]
            gacts.append(across(added, q) if q else added)
            ready.append(added)
        if step + 1 < steps:
            waits[step + 1][0].extend(ready)
        ready_before = ready

    loss, gap = loss[0], 1
    while gap < n_lat:
        other = lax.ppermute(loss, "lat", [(p, p ^ gap) for p in range(n_lat)])
        loss = call(add_kernel, [f32(*loss.shape)], (loss, other))[0]
        gap *= 2

    decoded = call(
        decode_kernel,
        [f32(width, lats)],
        (*[errs[q] for q in order], *[acts[q] for q in order]),
    )[0]
    g_pre = call(
        g_pre_kernel,
        [f32(rows // 2 * count + LOSS_ROWS, BLOCK)],
        (pre, mask, loss, *gacts),
        after=(decoded,),
    )[0]
    mine = [across(g_pre, q) if q else g_pre for q in range(n_tok)]
    others = [swap(g) for g in mine]
    early = [(q, side) for side in range(2) for q in range(n_tok) if (q, side) != (1, 1)]
    halves = [mine, others]
    early_grads = [halves[side][q] for q, side in early]
    encoded = call(
        functools.partial(encode_kernel, (n_tok, early)),
        [f32(width, lats)],
        (*resids, *early_grads, decoded),
    )[0]
    grad, losses = call(
        functools.partial(
            last_kernel, (1, [(0, 1)]), 1.0 / (rows * n_tok * half * n_wid), len(early)
        ),
        [bf16(width, lats), f32(LEVELS)],
        (*early_grads, resids[1], others[1], encoded),
        out_specs=[VMEM, SMEM],
    )
    return (losses, grad)


def solution(mesh):
    return jax.shard_map(
        body,
        mesh=mesh,
        in_specs=(P("tok", "wid"), P("lat", "wid"), P("lat"), P("wid"), P("tok", None), P()),
        out_specs=(P(), P(("wid", "tok"), "lat")),
        check_vma=False,
    )
```

```python
import functools

import jax
import jax.numpy as jnp
from jax import lax
from jax.experimental import pallas as pl
from jax.experimental.pallas import tpu as pltpu
from jax.sharding import PartitionSpec as P

LEVELS = 4
BLOCK = 128
LOSS_ROWS = 8
GELU_C = 0.7978845608028654
GELU_A = 0.044715

VMEM = pl.BlockSpec(memory_space=pltpu.VMEM)
SMEM = pl.BlockSpec(memory_space=pltpu.SMEM)
HBM = pl.BlockSpec(memory_space=pltpu.HBM)
ANY = pl.BlockSpec(memory_space=pl.ANY)


def f32(*shape):
    return jax.ShapeDtypeStruct(shape, jnp.float32)


def bf16(*shape):
    return jax.ShapeDtypeStruct(shape, jnp.bfloat16)


def call(kernel, outs, arrays, after=(), specs=None, out_specs=None, scratch=()):
    skip = slice(len(arrays), len(arrays) + len(after))

    def run(*refs):
        kernel(*refs[: skip.start], *refs[skip.stop :])

    return pl.pallas_call(
        run,
        out_shape=outs,
        in_specs=list(specs or [VMEM] * len(arrays)) + [ANY] * len(after),
        out_specs=out_specs or [VMEM] * len(outs),
        scratch_shapes=list(scratch),
        compiler_params=pltpu.CompilerParams(vmem_limit_bytes=12 * 1024 * 1024),
        cost_estimate=pl.CostEstimate(flops=0, bytes_accessed=1 << 10, transcendentals=0),
    )(*arrays, *after)


def in_hbm(array):
    return pltpu.with_memory_space_constraint(array, pltpu.HBM)


def total_of(terms):
    return functools.reduce(jnp.add, terms)


def place_in_chain():
    lat = lax.axis_index("lat")
    return jnp.where(lax.axis_index("wid") == 0, lat, lax.axis_size("lat") - 1 - lat)


def level_table(bounds, count, out):
    lasts = bounds[...] - 1 - lax.axis_index("lat") * count
    upward = lax.axis_index("wid") == 0

    def put(row, value):
        out[row : row + 1, :] = jnp.broadcast_to(value, (1, BLOCK))

    for i in range(count):
        hits = (jnp.minimum(lasts, count - 1) == i).astype(jnp.float32)
        ending = jnp.sum(hits, axis=1, keepdims=True)
        put(i, ending)
        put(count + i, jnp.where(upward, jnp.full_like(ending, float(i == count - 1)), ending))
    for m in range(LEVELS):
        for i in range(count):
            put((2 + m) * count + i, (lasts[:, m : m + 1] == i).astype(jnp.float32))


def pre_kernel(resid, dictionary, partial_out, dict_out, resid_v, dict_v, sems):
    pieces, _, width = dict_v.shape
    copies = []
    for i in range(pieces):
        cols = pl.ds(i * width, width)
        copies.append(
            (
                pltpu.make_async_copy(resid.at[:, cols], resid_v.at[i], sems.at[0, i]),
                pltpu.make_async_copy(dictionary.at[:, cols], dict_v.at[i], sems.at[1, i]),
            )
        )
        for copy in copies[-1]:
            copy.start()
    total = None
    for i in range(pieces):
        for copy in copies[i]:
            copy.wait()
        term = lax.dot_general(
            dict_v[i], resid_v[i], (((1,), (1,)), ((), ())), preferred_element_type=jnp.float32
        )
        total = term if total is None else total + term
    partial_out[...] = total.T
    parts = dict_out.shape[1] // width
    for i in range(parts):
        dict_out[:, i * width : (i + 1) * width] = dict_v[lax.axis_index("tok") * parts + i]


def widen_kernel(array, bounds, out, table_out):
    out[...] = array[...].astype(jnp.float32)
    level_table(bounds, array.shape[0] // BLOCK, table_out)


def pieces_kernel(resid, bias, bias_out, *outs):
    width = outs[0].shape[1]
    tok = lax.axis_index("tok")

    def cols(t):
        return pl.ds(pl.multiple_of(t * width, width), width)

    bias_out[...] = bias[:, cols(tok)]
    for q, out in enumerate(outs):
        out[...] = resid[:, cols(tok ^ q)].astype(jnp.float32)


def block_mask(active, lats):
    count = lats // BLOCK
    ids = lax.axis_index("lat") * count + lax.broadcasted_iota(jnp.int32, (count, 1), 0)
    hits = total_of([(active[q : q + 1, :] == ids).astype(jnp.float32) for q in range(active.shape[0])])
    spread = lax.broadcasted_iota(jnp.int32, (count, lats), 1) // BLOCK
    spread = (spread == lax.broadcasted_iota(jnp.int32, (count, lats), 0)).astype(jnp.bfloat16)
    return lax.dot_general(
        hits.astype(jnp.bfloat16),
        spread,
        (((0,), (0,)), ((), ())),
        preferred_element_type=jnp.float32,
    )


def activate_kernel(mine, other, bias, active, pre_out, act_out, mask_out):
    pre = mine[...] + other[...] + bias[...]
    pre_out[...] = pre
    inner = GELU_C * (pre + GELU_A * (pre * pre * pre))
    gelu = 0.5 * pre * (1.0 + jnp.tanh(inner))
    mask = block_mask(active[...], pre.shape[1])
    mask_out[...] = mask
    act_out[...] = jnp.where(mask > 0.0, gelu, 0.0)


def half_of(wid, rows):
    return pl.ds(pl.multiple_of(wid * (rows // 2), rows // 2), rows // 2)


def stacked(parts, extra, out):
    rows, cols = parts.shape
    for i in range(cols // BLOCK):
        out[i * rows : (i + 1) * rows, :] = parts[:, i * BLOCK : (i + 1) * BLOCK]
    out[-LOSS_ROWS:, :] = extra


def unstacked(ref, count):
    rows = (ref.shape[0] - LOSS_ROWS) // count
    return jnp.concatenate([ref[i * rows : (i + 1) * rows, :] for i in range(count)], axis=1)


def g_pre_kernel(pre_ref, mask, loss, *refs):
    terms, out = refs[:-1], refs[-1]
    mine = half_of(lax.axis_index("wid"), pre_ref.shape[0])
    pre = pre_ref[mine, :]
    inner = GELU_C * (pre + GELU_A * (pre * pre * pre))
    slope = GELU_C * (1.0 + 3.0 * GELU_A * (pre * pre))
    bend = jnp.tanh(inner)
    deriv = 0.5 * (1.0 + bend) + 0.5 * pre * (1.0 - bend * bend) * slope
    hit = mask[mine, :] > 0.0
    stacked(jnp.where(hit, deriv * total_of([t[...] for t in terms]), 0.0), loss[...], out)


def running_parts(act, dict_ref):
    sums = []
    for i in range(dict_ref.shape[0] // BLOCK):
        span = slice(i * BLOCK, (i + 1) * BLOCK)
        part = jnp.dot(
            act[:, span], dict_ref[span, :].astype(jnp.bfloat16), preferred_element_type=jnp.float32
        )
        sums.append(sums[-1] + part if sums else part)
    return sums


def round_kernel(act, out):
    out[...] = act[...].astype(jnp.bfloat16)


def project_kernel(act, table, *refs):
    dicts, out = refs[:-1], refs[-1]
    for side, dictionary in enumerate(dicts):
        sums = running_parts(act[...], dictionary)
        count = len(sums)
        width = dictionary.shape[1]
        out[:, side * width : (side + 1) * width] = total_of(
            [table[count + i : count + i + 1, :1] * s for i, s in enumerate(sums)]
        )


def columns(ref, col, width):
    return ref[:, col * width : (col + 1) * width]


def message_kernel(places, cols, got, *refs):
    out = refs[-1]
    width = out.shape[1]
    index = place_in_chain()
    for place, piece, col in zip(places, refs[:-1], cols[1:]):

        @pl.when(index == place)
        def _():
            own = columns(piece, col, width)
            out[...] = own + columns(got, cols[0], width) if place else own


def choose_kernel(places, cols, *refs):
    arrived, out = refs[:-1], refs[-1]
    index = place_in_chain()

    @pl.when(index == 0)
    def _():
        out[...] = jnp.zeros_like(out)

    for place, ref, col in zip(places, arrived, cols):

        @pl.when(index == place if len(arrived) > 1 else index > 0)
        def _():
            out[...] = columns(ref, col, out.shape[1])


def square_sums(table, shifted):
    count = len(shifted)
    squares = []
    for v in shifted:
        lanes = jnp.sum(v * v, axis=0, keepdims=True)
        squares.append(total_of([lanes[:, i : i + BLOCK] for i in range(0, lanes.shape[1], BLOCK)]))
    rows = []
    for m in range(LEVELS):
        at = (2 + m) * count
        rows.append(total_of([table[at + i : at + i + 1, :] * s for i, s in enumerate(squares)]))
    return jnp.concatenate(rows + [jnp.zeros((LOSS_ROWS - LEVELS, BLOCK), jnp.float32)], axis=0)


def error_kernel(loss_count, act, dictionary, resid, bias, table, mine, other, *refs):
    before, refs = refs[:loss_count], refs[loss_count:]
    err_out, keep_out, give_out, loss_out = refs
    upward = lax.axis_index("wid") == 0
    earlier = jnp.where(upward, mine[...], other[...])
    later = jnp.where(upward, other[...], mine[...])
    base = bias[...] - resid[...] + earlier
    sums = running_parts(act[...], dictionary)
    shifted = [base + s for s in sums]
    loss_out[...] = total_of([square_sums(table, shifted)] + [b[...] for b in before])
    err = later
    for i in reversed(range(len(sums))):
        err = err + table[i : i + 1, :1] * shifted[i]
        rounded = err.astype(jnp.bfloat16)
        err_out[i] = rounded
        cols = slice(i * BLOCK, (i + 1) * BLOCK)
        gact = lax.dot_general(
            rounded,
            dictionary[cols, :],
            (((1,), (1,)), ((), ())),
            preferred_element_type=jnp.float32,
        )
        half = gact.shape[0] // 2
        keep_out[:, cols] = jnp.where(upward, gact[:half, :], gact[half:, :])
        give_out[:, cols] = jnp.where(upward, gact[half:, :], gact[:half, :])


def collect_kernel(keep, give, out):
    out[...] = keep[...] + give[...]


def add_kernel(*refs):
    refs[-1][...] = total_of([ref[...] for ref in refs[:-1]])


def decode_kernel(*refs):
    n = (len(refs) - 1) // 2
    errs, acts, out = refs[:n], refs[n : 2 * n], refs[-1]
    for i in range(errs[0].shape[0]):
        cols = slice(i * BLOCK, (i + 1) * BLOCK)
        err = jnp.concatenate([e[i] for e in errs], axis=0)
        act = jnp.concatenate([a[:, cols] for a in acts], axis=0)
        out[:, cols] = lax.dot_general(
            err, act, (((0,), (0,)), ((), ())), preferred_element_type=jnp.float32
        )


def encode_kernel(items, *refs):
    n, halves = items
    resids, grads, base, out = refs[:n], refs[n:-2], refs[-2], refs[-1]
    half = resids[0].shape[0] // 2
    count = out.shape[1] // BLOCK
    wid = lax.axis_index("wid")
    spans = [half_of(wid, 2 * half), half_of(1 - wid, 2 * half)]
    resid = jnp.concatenate(
        [resids[q][spans[side], :].astype(jnp.bfloat16) for q, side in halves], axis=0
    )
    grad = jnp.concatenate([unstacked(g, count).astype(jnp.bfloat16) for g in grads], axis=0)
    total = base[...] + lax.dot_general(
        resid, grad, (((0,), (0,)), ((), ())), preferred_element_type=jnp.float32
    )
    out[...] = total.astype(out.dtype)


def last_kernel(items, scale, n_early, *refs):
    *refs, out, loss_out = refs
    early, refs = refs[:n_early], refs[n_early:]
    encode_kernel(items, *refs, out)
    grads = list(early) + list(refs[items[0] : -1])
    lanes = total_of([g[-LOSS_ROWS:, :] for g in grads])
    for m in range(LEVELS):
        loss_out[m] = jnp.sum(lanes[m : m + 1, :]) * scale


def pick(index, choices):
    values = sorted(choices)
    result = choices[values[0]]
    for value in values[1:]:
        result = jnp.where(index == value, choices[value], result)
    return result


def body(resid, dictionary, enc_bias, dec_bias, active_blocks, level_bounds):
    rows, half = resid.shape
    lats = dictionary.shape[0]
    n_lat, n_wid, n_tok = lax.axis_size("lat"), lax.axis_size("wid"), lax.axis_size("tok")
    width = half // n_tok
    count = lats // BLOCK

    def across(array, q):
        return lax.ppermute(array, "tok", [(t, t ^ q) for t in range(n_tok)])

    def swap(array):
        return lax.ppermute(array, "wid", [(w, w ^ 1) for w in range(n_wid)])

    partial, dict_here = call(
        pre_kernel,
        [f32(rows, lats), bf16(lats, width)],
        (in_hbm(resid), in_hbm(dictionary)),
        specs=[HBM, HBM],
        scratch=[
            pltpu.VMEM((2 * n_tok, rows, width // 2), jnp.bfloat16),
            pltpu.VMEM((2 * n_tok, lats, width // 2), jnp.bfloat16),
            pltpu.SemaphoreType.DMA((2, 2 * n_tok)),
        ],
    )
    partial_other = swap(partial)
    dict_wide, table = call(
        widen_kernel,
        [f32(lats, width), f32((2 + LEVELS) * count, BLOCK)],
        (dict_here, level_bounds.reshape(1, LEVELS)),
        after=(partial_other,),
    )
    dict_other = swap(dict_wide)
    pre, act, mask = call(
        activate_kernel,
        [f32(rows, lats)] * 3,
        (partial, partial_other, enc_bias.reshape(1, lats), active_blocks.T),
        after=(dict_wide,),
    )
    order = [0, 1, 3, 2] if n_tok == 4 else list(range(n_tok))
    steps = n_tok + n_lat - 2
    places = list(range(1, n_lat))
    acts, errs, hands, gives, gacts, loss = {}, {}, [], [], [], ()
    sums, got, sent = ([], []), ([], []), []
    waits = {step: [] for step in range(steps)}

    gathered = {q: across(act, q) for q in order[1:-1]}

    def project(q, dicts):
        shape = [f32(rows, width * len(dicts))]
        return call(project_kernel, shape, (acts[q], table, *dicts))[0]

    for step in range(steps + 1):
        at = [p for p in range(n_lat - 1) if 0 <= step - p < n_tok]
        pairs = []
        for p in at:
            pairs.append((2 * p, 2 * (p + 1)))
            pairs.append((2 * (n_lat - 1 - p) + 1, 2 * (n_lat - 2 - p) + 1))
        if step == 0:
            acts[order[0]] = call(round_kernel, [bf16(rows, lats)], (act,))[0]
            for side, dict_ref in enumerate((dict_other, dict_here)):
                message = project(order[0], (dict_ref,))
                sums[side].append((message, 0))
                got[side].append((lax.ppermute(message, ("lat", "wid"), pairs), 0))
                sent = [message]
        elif step < steps:
            for side in range(2):
                items = [got[side][-1], *[sums[side][step - p] for p in at]]
                message = call(
                    functools.partial(message_kernel, at, [col for _, col in items]),
                    [f32(rows, width)],
                    [array for array, _ in items],
                    after=sent + (waits[step] if side == 0 else []) if step > 1 else (),
                )[0]
                got[side].append((lax.ppermute(message, ("lat", "wid"), pairs), 0))
                sent = [message]
        if step + 1 < n_tok:
            q = order[step + 1]
            acts[q] = call(round_kernel, [bf16(rows, lats)], (gathered[q],), after=sent)[0]
            if step == 1:
                late = call(add_kernel, [f32(rows, lats)], (act,), after=sent)[0]
                gathered[order[-1]] = across(late, order[-1])
                bias_here, *pieces = call(
                    pieces_kernel,
                    [f32(1, width)] + [f32(rows, width)] * n_tok,
                    (resid, dec_bias.reshape(1, half)),
                    after=(late,),
                )
                resids = [piece if r == 0 else across(piece, r) for r, piece in enumerate(pieces)]
                for place, r in enumerate(order[1:]):
                    waits[min(3 + place, steps - 1)].append(resids[r])
            for side, dict_ref in enumerate((dict_other, dict_here)):
                sums[side].append((project(q, (dict_ref,)), 0))
        ready = []
        c = step - (n_lat - 1)
        if c >= 0:
            chosen = []
            for side in range(2):
                items = [got[side][c + p - 1] for p in places]
                if n_lat > 4:
                    items = [a[:, col * width : (col + 1) * width] for a, col in items]
                    items = [(pick(place_in_chain(), dict(zip(places, items))), 0)]
                chosen.append(
                    call(
                        functools.partial(choose_kernel, places, [col for _, col in items]),
                        [f32(rows, width)],
                        [array for array, _ in items],
                        after=sent if step < steps else ready_before + chosen,
                    )[0]
                )
            hands.append((swap(chosen[0]), chosen[1]))
            ready += chosen
        stages = [c - 1] if step < steps else [c - 1, c]
        for c in stages:
            if c < 0:
                continue
            q = order[c]
            errs[q], keep, give, loss_here = call(
                functools.partial(error_kernel, len(loss)),
                [bf16(count, rows, width)] + [f32(rows // 2, lats)] * 2 + [f32(LOSS_ROWS, BLOCK)],
                (acts[q], dict_here, resids[q], bias_here, table, hands[c][1], hands[c][0], *loss),
                after=sent if step < steps else (),
            )
            loss = (loss_here,)
            gives.append((keep, swap(give)))
            ready.append(errs[q])
        stages = range(n_tok) if step == steps else []
        for c in stages:
            if c < 0:
                continue
            q = order[c]
            added = call(
                collect_kernel, [f32(rows // 2, lats)], gives[c], after=sent if step < steps else ()
            )[0]
            gacts.append(across(added, q) if q else added)
            ready.append(added)
        if step + 1 < steps:
            waits[step + 1] += ready
        ready_before = ready

    loss, gap = loss[0], 1
    while gap < n_lat:
        other = lax.ppermute(loss, "lat", [(p, p ^ gap) for p in range(n_lat)])
        loss = call(add_kernel, [f32(*loss.shape)], (loss, other))[0]
        gap *= 2

    decoded = call(
        decode_kernel,
        [f32(width, lats)],
        (*[errs[q] for q in order], *[acts[q] for q in order]),
    )[0]
    g_pre = call(
        g_pre_kernel,
        [f32(rows // 2 * count + LOSS_ROWS, BLOCK)],
        (pre, mask, loss, *gacts),
        after=(decoded,),
    )[0]
    mine = [across(g_pre, q) if q else g_pre for q in range(n_tok)]
    others = [swap(g) for g in mine]
    early = [(q, side) for side in range(2) for q in range(n_tok) if (q, side) != (1, 1)]
    halves = [mine, others]
    early_grads = [halves[side][q] for q, side in early]
    encoded = call(
        functools.partial(encode_kernel, (n_tok, early)),
        [f32(width, lats)],
        (*resids, *early_grads, decoded),
    )[0]
    grad, losses = call(
        functools.partial(
            last_kernel, (1, [(0, 1)]), 1.0 / (rows * n_tok * half * n_wid), len(early)
        ),
        [bf16(width, lats), f32(LEVELS)],
        (*early_grads, resids[1], others[1], encoded),
        out_specs=[VMEM, SMEM],
    )
    return (losses, grad)


def solution(mesh):
    return jax.shard_map(
        body,
        mesh=mesh,
        in_specs=(P("tok", "wid"), P("lat", "wid"), P("lat"), P("wid"), P("tok", None), P()),
        out_specs=(P(), P(("wid", "tok"), "lat")),
        check_vma=False,
    )
```
